512 devices in a mesh: dp: 4 (over x), code: 128 (over y, z, core).
Axes of the slice: x: 4, y: 4, z: 16, core: 2. Of those that a mesh axis runs over, the one named last changes fastest.
Arguments:
- latents: bfloat16 [262144, 128], P(('dp', 'code')), may hold values from -6 to 6
- code_ids: int32 [262144], P(('dp', 'code')), may hold values from 0 to 65535, as said below
- ema_sums: float32 [65536, 128], P('code'), may hold values from -6 to 6
- ema_counts: float32 [65536], P('code'), may hold values from 0.5 to 16
- dead_codes: int32 [16384], P(('dp', 'code')), may hold values from 0 to 65535, as said below
- restart_index: int32 [16384], P(('dp', 'code')), may hold values from 0 to 511
- next_latents: bfloat16 [131072, 128], P(('dp', 'code')), may hold values from -6 to 6
Outputs:
- codebook: float32 [65536, 128], P('code')
- fresh_counts: float32 [65536], P('code')
- next_distance: float32 [131072], P(('dp', 'code'))
The draws below stay inside these ranges and needn't reach their ends.
Inputs may be any that keep to these rules, and one draw needn't show every extreme that they name: `code_ids`: in each aligned block of 512 rows (the rows of one device) at most 12 ids lie in one range [o * 512, (o + 1) * 512), and some range holds exactly 12. `dead_codes`: all entries are distinct. In each aligned block of 32 entries (one device's) at most 1 codes lie in one range [o * 512, (o + 1) * 512), and some range holds exactly 1. `restart_index`: entry j names a row of the j // 32-th aligned block of 512 latents.
All inputs are finite; a program needn't handle non-finite values.
Results may differ from the reference program's by a relative error of at most 0.00035.
Values may be sent and summed in bfloat16 or wider, within the bound.
A program may use at most 64 MiB of HBM per device.

```python
import math
import jax
import jax.numpy as jnp
from jax import lax

E = 128
CODES = 65536
LAT_DEV = 512
K_DEV = 512
LATENTS = 262144
NEXT = 131072
CAP = 12
DEAD_DEV = 32
DEAD = 16384
N_DP = 4
N_CODE = 128


def draw_code_ids(key, part):
    key = jax.random.fold_in(key, 7)
    keys = jax.random.split(key, 9)
    devices = N_DP * N_CODE
    first = jax.random.randint(keys[0], (devices,), 0, N_CODE)
    second = jax.random.randint(keys[1], (devices,), 0, N_CODE)
    offset_hot = jax.random.randint(keys[2], (), 0, N_CODE)
    hottest = (jnp.minimum(first, second) + offset_hot) % N_CODE
    spread = jax.random.randint(keys[3], (devices, 1), 0, N_CODE - 1)
    slot_index = jnp.arange(LAT_DEV, dtype=jnp.int32)[None, :]
    others = (hottest[:, None] + 1 + (slot_index - CAP + spread) % (N_CODE - 1)) % N_CODE
    owner = jnp.where(slot_index < CAP, hottest[:, None], others)
    draw_one = jax.random.randint(keys[4], (devices, LAT_DEV), 0, K_DEV)
    draw_two = jax.random.randint(keys[5], (devices, LAT_DEV), 0, K_DEV)
    draw_three = jax.random.randint(keys[6], (devices, LAT_DEV), 0, K_DEV)
    offset_code = jax.random.randint(keys[7], (), 0, K_DEV)
    inner = (jnp.minimum(jnp.minimum(draw_one, draw_two), draw_three) + offset_code) % K_DEV
    labels = owner * K_DEV + inner
    orders = jax.vmap(lambda sub_key: jax.random.permutation(sub_key, LAT_DEV))(jax.random.split(keys[8], devices))
    labels = jnp.take_along_axis(labels, orders, 1)
    return labels.reshape(-1).astype(jnp.int32)


def draw_dead_codes(key, part):
    key = jax.random.fold_in(key, 11)
    keys = jax.random.split(key, 3)
    devices = N_DP * N_CODE
    device_index = jnp.arange(devices, dtype=jnp.int32)
    replica = device_index // N_CODE
    column = device_index % N_CODE
    entry = jnp.arange(DEAD_DEV, dtype=jnp.int32)
    shift_owner = jax.random.randint(keys[0], (), 0, N_CODE)
    owner = (entry[None, :] + column[:, None] + shift_owner) % N_CODE
    tables = jax.vmap(lambda sub_key: jax.random.permutation(sub_key, K_DEV))(jax.random.split(keys[1], N_CODE))
    ranking = entry[None, :] * N_DP + replica[:, None]
    labels = owner * K_DEV + tables[owner, ranking]
    orders = jax.vmap(lambda sub_key: jax.random.permutation(sub_key, DEAD_DEV))(jax.random.split(keys[2], devices))
    labels = jnp.take_along_axis(labels, orders, 1)
    return labels.reshape(-1).astype(jnp.int32)


def set_ends(drawn, key, low, top_value):
    longest = drawn.shape.index(max(drawn.shape))
    spots = []
    for shift in (0, 1):
        where = [jax.random.randint(jax.random.fold_in(key, axis), (), 0, length) for axis, length in enumerate(drawn.shape)]
        where[longest] = (where[longest] + shift) % drawn.shape[longest]
        spots.append(tuple(where))
    return drawn.at[spots[0]].set(low).at[spots[1]].set(top_value)


def level_of(rng, shape, pieces, smallest, top_value):
    def one(position, shards_of):
        heights = jax.random.uniform(jax.random.fold_in(jax.random.fold_in(rng, 6), position), (shards_of,), jnp.float32, smallest / len(pieces), top_value / len(pieces))
        return jnp.repeat(jnp.exp(heights), shape[position] // shards_of).reshape((-1,) + (1,) * (len(shape) - position - 1))

    factor_of = one(*pieces[0])
    for cut in pieces[1:]:
        factor_of = factor_of * one(*cut)
    return factor_of


def normal_values(key, shape, scale, most, pieces=(), kind=jnp.bfloat16):
    result = scale * jax.random.normal(key, shape, jnp.float32)
    if pieces:
        result = result * level_of(key, shape, pieces, -0.22, 0.18)
    return jnp.clip(result, -most, most).astype(kind)


def setup_inputs(seed: int = 0) -> dict:
    arg_keys = jax.random.split(jax.random.key(seed), 8)
    return {
        "latents": normal_values(arg_keys[0], (LATENTS, E), 1.0, 6.0, ((0, 512),)),
        "code_ids": draw_code_ids(jax.random.fold_in(arg_keys[7], 71), 0),
        "ema_sums": normal_values(arg_keys[2], (CODES, E), 1.0, 6.0, ((0, 128),), jnp.float32),
        "ema_counts": jnp.clip(jnp.exp(math.log(16.0) - 3.465736 * jax.random.uniform(arg_keys[3], (CODES,), jnp.float32) ** level_of(arg_keys[3], (CODES,), ((0, 128),), -0.2, 0.2)), 0.5, 16.0),
        "dead_codes": draw_dead_codes(jax.random.fold_in(arg_keys[7], 71), 0),
        "restart_index": set_ends(jax.random.randint(arg_keys[5], (DEAD,), 0, LAT_DEV), jax.random.fold_in(arg_keys[5], 1), 0, LAT_DEV - 1).astype(jnp.int32),
        "next_latents": normal_values(arg_keys[6], (NEXT, E), 1.0, 6.0, ((0, 512),)),
    }


decay_rate = 0.8


def reference(latents, code_ids, ema_sums, ema_counts, dead_codes, restart_index, next_latents):
    wide = latents.astype(jnp.float32)
    batch_sums = jax.ops.segment_sum(wide, code_ids, num_segments=CODES)
    batch_counts = jax.ops.segment_sum(jnp.ones((LATENTS,), jnp.float32), code_ids, num_segments=CODES)
    sources = (jnp.arange(DEAD, dtype=jnp.int32) // DEAD_DEV) * LAT_DEV + restart_index.astype(jnp.int32)
    restart_rows = jnp.zeros((CODES, E), jnp.float32).at[dead_codes].set(wide[sources])
    restart_flag = jnp.zeros((CODES,), jnp.float32).at[dead_codes].set(1.0)
    fresh_counts = decay_rate * ema_counts + (1.0 - decay_rate) * batch_counts
    fresh_sums = decay_rate * ema_sums + (1.0 - decay_rate) * batch_sums
    is_dead = restart_flag > 0.5
    fresh_counts = jnp.where(is_dead, jnp.ones_like(fresh_counts), fresh_counts)
    fresh_sums = jnp.where(is_dead[:, None], restart_rows, fresh_sums)
    codebook = fresh_sums / fresh_counts[:, None]
    shaped = lax.optimization_barrier(codebook.astype(jnp.bfloat16)).astype(jnp.float32)
    code_norms = jnp.sum(shaped * shaped, 1)
    queries = next_latents.astype(jnp.float32)
    block = min(512, NEXT)

    def nearest(query_block):
        scores = jnp.dot(query_block, shaped.T, precision=lax.Precision.HIGHEST)
        return jnp.min(code_norms[None, :] - 2.0 * scores, 1)

    best = lax.map(nearest, queries.reshape(NEXT // block, block, E)).reshape(NEXT)
    next_distance = (best + jnp.sum(queries * queries, 1)) / E
    return codebook, fresh_counts, next_distance
```

```python
import functools

import jax
import jax.numpy as jnp
from jax import lax
from jax.experimental import pallas as pl
from jax.experimental.pallas import tpu as pltpu
from jax.sharding import PartitionSpec as P

MESH = pl.DeviceIdType.MESH
DECAY = 0.8
TILE = 16
DEAD_SLOT = 12
CORES = 2
BIG = 3.0e38
NT = (((1,), (1,)), ((), ()))


def onehot(mask):
    return jnp.where(mask, 1.0, 0.0).astype(jnp.bfloat16)


def column(row):
    return jnp.broadcast_to(row, (128, 128)).T


def body(
    nx, ny, nz, lat, ids, dead, ridx, ema_s, ema_c, nxt, book, cnt_out, dist,
    pack, zbuf, gbuf, qbuf, ext, rs_send, rs_recv, code, norm, acc, low_send, low_recv, cnts,
    z_s, z_r, g_s, g_r, q_s, q_r, f_s, f_r, x_s, x_r, b_s, b_r, c_s, c_r, right_s, right_r, left_s, left_r, m_s, m_r,
):
    rows = lat.shape[0]
    k_dev = book.shape[0]
    sub = k_dev // nx
    nyc = ny * CORES
    planes = nx * nyc
    group = nz // 4
    block = nyc * TILE
    shift_k = k_dev.bit_length() - 1
    shift_z = nz.bit_length() - 1

    x = lax.axis_index("dp")
    me = lax.axis_index("code")
    c = lax.rem(me, CORES)
    z = lax.rem(lax.div(me, CORES), nz)
    y = lax.div(me, CORES * nz)
    me_yc = y * CORES + c
    me_p = x * nyc + me_yc

    def at(ax, ay, az, ac):
        return (ax, (ay * nz + az) * CORES + ac)

    def in_plane(p):
        yc = lax.rem(p, nyc)
        return at(lax.div(p, nyc), lax.div(yc, CORES), z, lax.rem(yc, CORES))

    def along_z(d):
        return at(x, y, lax.rem(z + d + nz, nz), c)

    barrier = pltpu.get_barrier_semaphore()

    @pl.loop(1, planes)
    def _(d):
        pl.semaphore_signal(barrier, inc=1, device_id=in_plane(lax.rem(me_p + d, planes)), device_id_type=MESH)

    @pl.loop(1, nz)
    def _(d):
        pl.semaphore_signal(barrier, inc=1, device_id=along_z(d), device_id_type=MESH)

    lanes = rows + 128
    own = ids[...]

    def place(labels):
        owner = labels >> shift_k
        oc, oz, oy = owner & 1, (owner >> 1) & (nz - 1), owner >> (1 + shift_z)
        return oz * nyc + oy * CORES + oc

    owner = place(own)
    match = lax.broadcasted_iota(jnp.int32, (nyc * nz, rows), 0) == owner
    before = lax.broadcasted_iota(jnp.int32, (rows, rows), 0) < lax.broadcasted_iota(jnp.int32, (rows, rows), 1)
    earlier = jnp.dot(onehot(match), onehot(before), preferred_element_type=jnp.float32)
    rank = jnp.sum(jnp.where(match, earlier, 0.0), axis=0, keepdims=True).astype(jnp.int32)

    ext[...] = jnp.full(ext.shape, -1, jnp.int32)
    ext[0:1, 0 : dead.shape[1]] = dead[...]
    ext[1:2, 0 : dead.shape[1]] = ridx[...]
    gone = ext[0:1, :]
    gone_owner = jnp.where(gone >= 0, place(gone), -1024)
    pick = column(ext[1:2, :].astype(jnp.float32)).astype(jnp.int32)
    lane = lax.broadcasted_iota(jnp.int32, (128, 128), 1)
    picks = jnp.concatenate([onehot(pick == lane + 128 * i) for i in range(rows // 128)], axis=1)
    restarts = jnp.dot(picks, lat[...], preferred_element_type=jnp.float32).astype(jnp.bfloat16)
    data = jnp.concatenate([lat[...], restarts], axis=0)

    all_owner = jnp.concatenate([owner, gone_owner], axis=1)
    slot = jnp.concatenate([rank, jnp.full((1, 128), DEAD_SLOT, jnp.int32)], axis=1)
    tag = jnp.concatenate([(own & (k_dev - 1)) + 1, (gone & (k_dev - 1)) + (k_dev + 1)], axis=1)
    low = (tag & 31).astype(jnp.float32)
    high = (tag - (tag & 31)).astype(jnp.float32)
    key = all_owner * TILE + slot
    tag_key = all_owner * TILE + (DEAD_SLOT + 1)
    spot = onehot((lax.broadcasted_iota(jnp.int32, (128, lanes), 0) & (TILE - 1)) == slot)
    line = lax.broadcasted_iota(jnp.int32, (block, lanes), 0)
    lane_tile = lax.broadcasted_iota(jnp.int32, (1, 128), 1) >> 4

    def offset(k):
        return jnp.where(lax.rem(k, 2) == 1, lax.div(k + 1, 2), nz - lax.div(k, 2))

    def packed(k):
        base = lax.rem(z + offset(k), nz) * block
        put = onehot(line == key - base)
        moved = jnp.dot(put, data, preferred_element_type=jnp.float32)
        marks = jnp.where(line == tag_key - base, high, 0.0) + jnp.where(line == tag_key + 1 - base, low, 0.0)
        tags = lax.dot_general(marks.astype(jnp.bfloat16), spot, NT, preferred_element_type=jnp.float32)
        here = lax.rem(me_yc * nz + k, 8)
        tags = jnp.where(lane_tile == here, tags, 0.0)
        return (moved + tags).astype(jnp.bfloat16).reshape(nyc, TILE, 128)

    def z_copy(k):
        return pltpu.make_async_remote_copy(
            src_ref=pack.at[k], dst_ref=zbuf.at[k], send_sem=z_s.at[k], recv_sem=z_r.at[k],
            device_id=along_z(offset(k)), device_id_type=MESH,
        )

    pl.semaphore_wait(barrier, planes - 1 + nz - 1)

    @pl.loop(1, nz)
    def _(k):
        pack[k] = packed(k)
        z_copy(k).start()

    zbuf[0] = packed(jnp.int32(0))

    def xy_slot(i):
        return i * CORES + c

    def q_copy(i, slot_index):
        return pltpu.make_async_remote_copy(
            src_ref=nxt, dst_ref=qbuf.at[slot_index], send_sem=q_s.at[i], recv_sem=q_r.at[i],
            device_id=in_plane(xy_slot(i)), device_id_type=MESH,
        )

    spots = nx * ny
    me_xy = x * ny + y

    def q_send(i):
        return pltpu.make_async_remote_copy(
            src_ref=nxt, dst_ref=qbuf.at[me_p], send_sem=q_s.at[i], recv_sem=q_r.at[me_xy],
            device_id=in_plane(xy_slot(i)), device_id_type=MESH,
        )

    @pl.loop(1, spots)
    def _(d):
        q_send(lax.rem(me_xy + d, spots)).start()

    qbuf[me_p] = nxt[...]
    acc[...] = jnp.full(acc.shape, BIG, jnp.float32)
    wide = nxt[...].astype(jnp.float32)
    query_norm = jnp.sum((wide * wide).T, axis=0, keepdims=True)

    def g_copy(g, j):
        return pltpu.make_async_remote_copy(
            src_ref=zbuf.at[pl.ds(g * group, group), j],
            dst_ref=gbuf.at[me_yc, pl.ds(g * group, group)],
            send_sem=g_s.at[g, j], recv_sem=g_r.at[g, me_yc],
            device_id=at(x, lax.div(j, CORES), z, lax.rem(j, CORES)), device_id_type=MESH,
        )

    def g_got(g, j):
        return pltpu.make_async_remote_copy(
            src_ref=zbuf.at[pl.ds(g * group, group), j],
            dst_ref=gbuf.at[j, pl.ds(g * group, group)],
            send_sem=g_s.at[g, j], recv_sem=g_r.at[g, j],
            device_id=at(x, lax.div(j, CORES), z, lax.rem(j, CORES)), device_id_type=MESH,
        )

    @pl.loop(0, 4)
    def _(g):
        @pl.loop(g * group, (g + 1) * group)
        def _(k):
            @pl.when(k > 0)
            def _():
                z_copy(k).wait_recv()

        @pl.loop(1, nyc)
        def _(d):
            g_copy(g, lax.rem(me_yc + d, nyc)).start()

        gbuf[me_yc, pl.ds(g * group, group)] = zbuf[pl.ds(g * group, group), me_yc]

    def f_copy(i):
        return pltpu.make_async_remote_copy(
            src_ref=qbuf.at[xy_slot(i)], dst_ref=qbuf.at[xy_slot(i)], send_sem=f_s.at[i], recv_sem=f_r.at[i],
            device_id=at(x, y, z, 1 - c), device_id_type=MESH,
        )

    def f_got(i):
        other = i * CORES + 1 - c
        return pltpu.make_async_remote_copy(
            src_ref=qbuf.at[other], dst_ref=qbuf.at[other], send_sem=f_s.at[i], recv_sem=f_r.at[i],
            device_id=at(x, y, z, 1 - c), device_id_type=MESH,
        )

    f_copy(me_xy).start()

    @pl.loop(1, spots)
    def _(d):
        i = lax.rem(me_xy + d, spots)
        q_copy(i, xy_slot(i)).wait_recv()
        f_copy(i).start()

    @pl.loop(0, 4)
    def _(g):
        @pl.loop(1, nyc)
        def _(d):
            g_got(g, lax.rem(me_yc + d, nyc)).wait_recv()

    total = nyc * nz * TILE
    got = gbuf[...].reshape(total, 128)
    in_tile = lax.broadcasted_iota(jnp.int32, (8, 128), 1) & (TILE - 1)
    read = onehot(in_tile > DEAD_SLOT)
    tags = jnp.concatenate(
        [
            jnp.dot(read, got[i * 128 : (i + 1) * 128], preferred_element_type=jnp.float32)[0:1].astype(jnp.int32)
            for i in range(total // 128)
        ],
        axis=1,
    )
    ones = jnp.ones((total, 128), jnp.bfloat16)
    name = lax.broadcasted_iota(jnp.int32, (sub, total), 0)

    def x_copy(to, frm):
        return pltpu.make_async_remote_copy(
            src_ref=rs_send.at[to], dst_ref=rs_recv.at[frm], send_sem=x_s.at[to], recv_sem=x_r.at[frm],
            device_id=at(to, y, z, c), device_id_type=MESH,
        )

    def tally(to):
        mine = tags - (to * sub + 1)
        hits = jnp.concatenate([onehot(name == mine), onehot(name == mine - k_dev)], axis=0)
        sums = jnp.dot(hits, got, preferred_element_type=jnp.float32)
        count = jnp.dot(hits, ones, preferred_element_type=jnp.float32)
        is_dead = count[sub:] > 0.5
        return jnp.where(is_dead, sums[sub:], sums[:sub]), jnp.where(is_dead, -1.0, count[:sub])

    for d in range(1, nx + 1):
        to = lax.rem(x + d, nx)
        sums, count = tally(to)
        ref = rs_send if d < nx else rs_recv
        ref[to, 0:sub, :] = sums
        ref[to, sub : sub + 8, :] = count.T[0:8]
        if d < nx:
            x_copy(to, x).start()
    for d in range(1, nx):
        x_copy(lax.rem(x + d, nx), lax.rem(x + d, nx)).wait_recv()

    count = jnp.zeros((1, 128), jnp.float32)
    dead_row = jnp.zeros((1, 128), jnp.float32)
    sums = jnp.zeros((sub, 128), jnp.float32)
    restart = jnp.zeros((sub, 128), jnp.float32)
    for i in range(nx):
        part = rs_recv[i, sub : sub + 1, :]
        count += jnp.maximum(part, 0.0)
        dead_row = jnp.maximum(dead_row, -part)
        piece = rs_recv[i, 0:sub, :]
        sums += piece
        restart += jnp.where(column(part) < 0.0, piece, 0.0)
    fresh_row = DECAY * ema_c[pl.ds(x, 1), :] + (1.0 - DECAY) * count
    fresh_row = jnp.where(dead_row > 0.5, 1.0, fresh_row)
    mine = pl.ds(pl.multiple_of(x * sub, sub), sub)
    fresh = DECAY * ema_s[mine, :] + (1.0 - DECAY) * sums
    fresh = jnp.where(column(dead_row) > 0.5, restart, fresh)
    rows_out = fresh / column(fresh_row)
    code[0] = (-2.0 * rows_out.astype(jnp.bfloat16).astype(jnp.float32)).astype(jnp.bfloat16)

    def right(t):
        return pltpu.make_async_remote_copy(
            src_ref=code.at[jnp.maximum(2 * t - 1, 0)], dst_ref=code.at[2 * t + 1],
            send_sem=right_s.at[t], recv_sem=right_r.at[t], device_id=along_z(1), device_id_type=MESH,
        )

    def left(t):
        return pltpu.make_async_remote_copy(
            src_ref=code.at[2 * t], dst_ref=code.at[2 * t + 2],
            send_sem=left_s.at[t], recv_sem=left_r.at[t], device_id=along_z(-1), device_id_type=MESH,
        )

    right(jnp.int32(0)).start()
    left(jnp.int32(0)).start()

    book[mine, :] = rows_out
    cnts[x] = jnp.broadcast_to(fresh_row, (8, 128))

    def b_copy(to, frm):
        span = pl.ds(pl.multiple_of(frm * sub, sub), sub)
        return pltpu.make_async_remote_copy(
            src_ref=book.at[span], dst_ref=book.at[span], send_sem=b_s.at[to], recv_sem=b_r.at[frm],
            device_id=at(to, y, z, c), device_id_type=MESH,
        )

    def c_copy(to, frm):
        return pltpu.make_async_remote_copy(
            src_ref=cnts.at[frm], dst_ref=cnts.at[frm], send_sem=c_s.at[to], recv_sem=c_r.at[frm],
            device_id=at(to, y, z, c), device_id_type=MESH,
        )

    for d in range(1, nx):
        to = lax.rem(x + d, nx)
        b_copy(to, x).start()
        c_copy(to, x).start()

    @pl.loop(0, spots)
    def _(i):
        f_got(i).wait_recv()

    steps = nz // 2
    unroll = min(8, planes)

    @pl.loop(0, steps)
    def _(t):
        right(t).wait_recv()

        @pl.when(t < steps - 1)
        def _():
            right(t + 1).start()
            left(t).wait_recv()

        @pl.when(t < steps - 2)
        def _():
            left(t + 1).start()

        table = code[pl.ds(2 * t, 2)].reshape(2 * sub, 128)
        wide_table = table.astype(jnp.float32)
        norm[...] = jnp.broadcast_to(0.25 * jnp.sum(wide_table * wide_table, axis=1, keepdims=True), (2 * sub, 128))

        @pl.loop(0, planes // unroll)
        def _(o):
            for i in range(unroll):
                p = o * unroll + i
                score = lax.dot_general(
                    code[pl.ds(2 * t, 2)].reshape(2 * sub, 128), qbuf[p], NT, preferred_element_type=jnp.float32
                )
                queries = score.shape[1]
                lows = [
                    jnp.min((norm[...] + score[:, h * 128 : (h + 1) * 128]).reshape(2 * sub // 8, 8, 128), axis=0)
                    for h in range(queries // 128)
                ]
                acc[p] = jnp.minimum(acc[p], jnp.concatenate(lows, axis=1))

    def m_copy(to, frm):
        return pltpu.make_async_remote_copy(
            src_ref=low_send.at[to], dst_ref=low_recv.at[frm], send_sem=m_s.at[to], recv_sem=m_r.at[frm],
            device_id=in_plane(to), device_id_type=MESH,
        )

    halves = nxt.shape[0] // 128

    def lowest(p):
        small = jnp.min(acc[p], axis=0, keepdims=True)
        parts = [jnp.broadcast_to(small[:, h * 128 : (h + 1) * 128], (8 // halves, 128)) for h in range(halves)]
        return jnp.concatenate(parts, axis=0)

    @pl.loop(1, planes)
    def _(d):
        to = lax.rem(me_p + d, planes)
        low_send[to] = lowest(to)
        m_copy(to, me_p).start()

    low_recv[me_p] = lowest(me_p)

    @pl.loop(1, planes)
    def _(d):
        frm = lax.rem(me_p + d, planes)
        m_copy(frm, frm).wait_recv()

    best = jnp.min(low_recv[...], axis=0)
    for h in range(halves):
        first = h * (8 // halves)
        dist[h : h + 1, :] = (best[first : first + 1] + query_norm[:, h * 128 : (h + 1) * 128]) / 128

    for d in range(1, nx):
        frm = lax.rem(x + d, nx)
        b_copy(frm, frm).wait_recv()
        c_copy(frm, frm).wait_recv()
    for i in range(nx):
        cnt_out[i : i + 1, :] = cnts[i, 0:1, :]

    @pl.loop(1, nz)
    def _(k):
        z_copy(k).wait_send()

    @pl.loop(1, spots)
    def _(d):
        q_send(lax.rem(me_xy + d, spots)).wait_send()

    @pl.loop(0, spots)
    def _(i):
        f_copy(i).wait_send()

    @pl.loop(0, 4)
    def _(g):
        @pl.loop(1, nyc)
        def _(d):
            g_copy(g, lax.rem(me_yc + d, nyc)).wait_send()

    for d in range(1, nx):
        to = lax.rem(x + d, nx)
        x_copy(to, x).wait_send()
        b_copy(to, x).wait_send()
        c_copy(to, x).wait_send()

    @pl.loop(0, steps)
    def _(t):
        right(t).wait_send()

        @pl.when(t < steps - 1)
        def _():
            left(t).wait_send()

    @pl.loop(1, planes)
    def _(d):
        m_copy(lax.rem(me_p + d, planes), me_p).wait_send()


def per_device(nx, ny, nz, latents, code_ids, ema_sums, ema_counts, dead_codes, restart_index, next_latents):
    k_dev = ema_sums.shape[0]
    sub = k_dev // nx
    nyc = ny * CORES
    planes = nx * nyc
    queries = next_latents.shape[0]
    vmem = pl.BlockSpec(memory_space=pltpu.VMEM)
    dma = pltpu.SemaphoreType.DMA
    bf16, f32 = jnp.bfloat16, jnp.float32
    book, counts, dist = pl.pallas_call(
        functools.partial(body, nx, ny, nz),
        out_shape=(
            jax.ShapeDtypeStruct((k_dev, 128), f32),
            jax.ShapeDtypeStruct((nx, sub), f32),
            jax.ShapeDtypeStruct((queries // 128, 128), f32),
        ),
        in_specs=[vmem] * 7,
        out_specs=(vmem,) * 3,
        scratch_shapes=[
            pltpu.VMEM((nz, nyc, TILE, 128), bf16),
            pltpu.VMEM((nz, nyc, TILE, 128), bf16),
            pltpu.VMEM((nyc, nz, TILE, 128), bf16),
            pltpu.VMEM((planes, queries, 128), bf16),
            pltpu.VMEM((8, 128), jnp.int32),
            pltpu.VMEM((nx, sub + 8, 128), f32),
            pltpu.VMEM((nx, sub + 8, 128), f32),
            pltpu.VMEM((nz, sub, 128), bf16),
            pltpu.VMEM((2 * sub, 128), f32),
            pltpu.VMEM((planes, 8, queries), f32),
            pltpu.VMEM((planes, 8, 128), f32),
            pltpu.VMEM((planes, 8, 128), f32),
            pltpu.VMEM((nx, 8, 128), f32),
            dma((nz,)), dma((nz,)),
            dma((4, nyc)), dma((4, nyc)),
            dma((nx * ny,)), dma((nx * ny,)),
            dma((nx * ny,)), dma((nx * ny,)),
            dma((nx,)), dma((nx,)),
            dma((nx,)), dma((nx,)),
            dma((nx,)), dma((nx,)),
            dma((nz // 2,)), dma((nz // 2,)),
            dma((nz // 2,)), dma((nz // 2,)),
            dma((planes,)), dma((planes,)),
        ],
        compiler_params=pltpu.CompilerParams(
            collective_id=0, has_side_effects=True, vmem_limit_bytes=40 * 1024 * 1024
        ),
    )(
        latents, code_ids.reshape(1, -1), dead_codes.reshape(1, -1), restart_index.reshape(1, -1),
        ema_sums, ema_counts.reshape(nx, sub), next_latents,
    )
    return book, counts.reshape(-1), dist.reshape(-1)


def solution(mesh, ny=4):
    nx = mesh.shape["dp"]
    nz = mesh.shape["code"] // (CORES * ny)
    in_specs = (
        P(("dp", "code"), None),
        P(("dp", "code")),
        P("code", None),
        P("code"),
        P(("dp", "code")),
        P(("dp", "code")),
        P(("dp", "code"), None),
    )
    reorder = functools.partial(per_device, nx, ny, nz)
    return jax.shard_map(
        lambda a, b, s, n, d, r, q: reorder(a, b, s, n, d, r, q),
        mesh=mesh,
        in_specs=in_specs,
        out_specs=(P("code", None), P("code"), P(("dp", "code"))),
        check_vma=False,
    )
```

```python
import functools

import jax
import jax.numpy as jnp
from jax import lax
from jax.experimental import pallas as pl
from jax.experimental.pallas import tpu as pltpu
from jax.sharding import PartitionSpec as P

MESH = pl.DeviceIdType.MESH
DECAY = 0.8
TILE = 16
DEAD_SLOT = 12
CORES = 2
BIG = 3.0e38


def onehot(mask):
    return jnp.where(mask, 1.0, 0.0).astype(jnp.bfloat16)


def column(row):
    return jnp.broadcast_to(row, (128, 128)).T


def body(
    nx, ny, nz, lat_in, ids_in, dead_in, ridx_in, ema_s_in, ema_c_in, nxt_in, book, cnt_out, dist,
    lat, ids, dead, ridx, ema_s, ema_c, nxt, turned,
    pack, zbuf, gbuf, qbuf, ext, rs_send, rs_recv, code, norm, acc, low_send, low_recv, cnts, in_s,
    z_s, z_r, g_s, g_r, q_s, q_r, f_s, f_r, x_s, x_r, b_s, b_r, c_s, c_r, right_s, right_r, left_s, left_r, m_s, m_r,
):
    rows = lat.shape[0]
    k_dev = book.shape[0]
    sub = k_dev // nx
    queries = nxt.shape[0]
    nyc = ny * CORES
    planes = nx * nyc
    group = nz // 4
    block = nyc * TILE
    shift_k = k_dev.bit_length() - 1
    shift_z = nz.bit_length() - 1

    x = lax.axis_index("dp")
    me = lax.axis_index("code")
    c = lax.rem(me, CORES)
    z = lax.rem(lax.div(me, CORES), nz)
    y = lax.div(me, CORES * nz)
    me_yc = y * CORES + c
    me_p = x * nyc + me_yc

    def at(ax, ay, az, ac):
        return (ax, (ay * nz + az) * CORES + ac)

    def in_plane(p):
        yc = lax.rem(p, nyc)
        return at(lax.div(p, nyc), lax.div(yc, CORES), z, lax.rem(yc, CORES))

    def along_z(d):
        return at(x, y, lax.rem(z + d + nz, nz), c)

    mine = pl.ds(pl.multiple_of(x * sub, sub), sub)
    sources = (lat_in, ids_in, dead_in, ridx_in, nxt_in, ema_c_in, ema_s_in.at[mine])
    loads = [
        pltpu.make_async_copy(src, dst, in_s.at[i])
        for i, (src, dst) in enumerate(zip(sources, (lat, ids, dead, ridx, nxt, ema_c, ema_s)))
    ]
    for load in loads:
        load.start()

    barrier = pltpu.get_barrier_semaphore()

    @pl.loop(1, planes)
    def _(d):
        pl.semaphore_signal(barrier, inc=1, device_id=in_plane(lax.rem(me_p + d, planes)), device_id_type=MESH)

    @pl.loop(1, nz)
    def _(d):
        pl.semaphore_signal(barrier, inc=1, device_id=along_z(d), device_id_type=MESH)

    for load in loads[:4]:
        load.wait()
    lanes = rows + 128
    own = ids[...]

    def place(labels):
        owner = labels >> shift_k
        oc, oz, oy = owner & 1, (owner >> 1) & (nz - 1), owner >> (1 + shift_z)
        return oz * nyc + oy * CORES + oc

    owner = place(own)
    match = lax.broadcasted_iota(jnp.int32, (nyc * nz, rows), 0) == owner
    before = lax.broadcasted_iota(jnp.int32, (rows, rows), 0) < lax.broadcasted_iota(jnp.int32, (rows, rows), 1)
    earlier = jnp.dot(onehot(match), onehot(before), preferred_element_type=jnp.float32)
    rank = jnp.sum(jnp.where(match, earlier, 0.0), axis=0, keepdims=True).astype(jnp.int32)

    ext[...] = jnp.full(ext.shape, -1, jnp.int32)
    ext[0:1, 0 : dead.shape[1]] = dead[...]
    ext[1:2, 0 : dead.shape[1]] = ridx[...]
    gone = ext[0:1, :]
    gone_owner = jnp.where(gone >= 0, place(gone), -1024)
    pick = column(ext[1:2, :].astype(jnp.float32)).astype(jnp.int32)
    lane = lax.broadcasted_iota(jnp.int32, (128, 128), 1)
    picks = jnp.concatenate([onehot(pick == lane + 128 * i) for i in range(rows // 128)], axis=1)
    restarts = jnp.dot(picks, lat[...], preferred_element_type=jnp.float32).astype(jnp.bfloat16)

    all_owner = jnp.concatenate([owner, gone_owner], axis=1)
    slot = jnp.concatenate([rank, jnp.full((1, 128), DEAD_SLOT, jnp.int32)], axis=1)
    tag = jnp.concatenate([own & (k_dev - 1), (gone & (k_dev - 1)) + k_dev], axis=1)
    tag = jnp.left_shift(128 + (tag & 127), tag >> 7).astype(jnp.float32)
    key = all_owner * TILE + slot
    tag_key = all_owner * TILE + (DEAD_SLOT + 1)
    spot = jnp.where((lax.broadcasted_iota(jnp.int32, (128, lanes), 0) & (TILE - 1)) == slot, 1.0, 0.0)
    spot = jnp.concatenate([spot[:, i * 128 : (i + 1) * 128].T for i in range(lanes // 128)], axis=0)
    data = jnp.concatenate([jnp.concatenate([lat[...], restarts], axis=0), spot.astype(jnp.bfloat16)], axis=1)
    line = lax.broadcasted_iota(jnp.int32, (block, lanes), 0)
    lane_tile = lax.broadcasted_iota(jnp.int32, (1, 128), 1) >> 4

    def offset(k):
        return jnp.where(lax.rem(k, 2) == 1, lax.div(k + 1, 2), nz - lax.div(k, 2))

    def packed(k):
        base = lax.rem(z + offset(k), nz) * block
        put = jnp.where(line == key - base, 1.0, jnp.where(line == tag_key - base, tag, 0.0))
        moved = jnp.dot(put.astype(jnp.bfloat16), data, preferred_element_type=jnp.float32)
        here = lax.rem(me_yc * nz + k, 8)
        tags = jnp.where(lane_tile == here, moved[:, 128:], 0.0)
        is_tag = (lax.broadcasted_iota(jnp.int32, (block, 128), 0) & (TILE - 1)) > DEAD_SLOT
        return jnp.where(is_tag, tags, moved[:, :128]).astype(jnp.bfloat16).reshape(nyc, TILE, 128)

    def z_copy(k):
        return pltpu.make_async_remote_copy(
            src_ref=pack.at[k], dst_ref=zbuf.at[k], send_sem=z_s.at[k], recv_sem=z_r.at[k],
            device_id=along_z(offset(k)), device_id_type=MESH,
        )

    pl.semaphore_wait(barrier, planes - 1 + nz - 1)

    @pl.loop(0, (nz - 1) // 3)
    def _(o):
        for i in range(3):
            k = 1 + o * 3 + i
            pack[k] = packed(k)
            z_copy(k).start()

    zbuf[0] = packed(jnp.int32(0))

    loads[4].wait()
    wide = nxt[...].astype(jnp.float32)
    query_norm = jnp.sum((wide * wide).T, axis=0, keepdims=True)
    turned[...] = wide.T.astype(jnp.bfloat16)

    def xy_slot(i):
        return i * CORES + c

    def q_copy(i, slot_index):
        return pltpu.make_async_remote_copy(
            src_ref=turned, dst_ref=qbuf.at[slot_index], send_sem=q_s.at[i], recv_sem=q_r.at[i],
            device_id=in_plane(xy_slot(i)), device_id_type=MESH,
        )

    spots = nx * ny
    me_xy = x * ny + y

    def q_send(i):
        return pltpu.make_async_remote_copy(
            src_ref=turned, dst_ref=qbuf.at[me_p], send_sem=q_s.at[i], recv_sem=q_r.at[me_xy],
            device_id=in_plane(xy_slot(i)), device_id_type=MESH,
        )

    @pl.loop(1, spots)
    def _(d):
        q_send(lax.rem(me_xy + d, spots)).start()

    qbuf[me_p] = turned[...]
    acc[...] = jnp.full(acc.shape, BIG, jnp.float32)

    def g_copy(g, j):
        return pltpu.make_async_remote_copy(
            src_ref=zbuf.at[pl.ds(g * group, group), j],
            dst_ref=gbuf.at[me_yc, pl.ds(g * group, group)],
            send_sem=g_s.at[g, j], recv_sem=g_r.at[g, me_yc],
            device_id=at(x, lax.div(j, CORES), z, lax.rem(j, CORES)), device_id_type=MESH,
        )

    def g_got(g, j):
        return pltpu.make_async_remote_copy(
            src_ref=zbuf.at[pl.ds(g * group, group), j],
            dst_ref=gbuf.at[j, pl.ds(g * group, group)],
            send_sem=g_s.at[g, j], recv_sem=g_r.at[g, j],
            device_id=at(x, lax.div(j, CORES), z, lax.rem(j, CORES)), device_id_type=MESH,
        )

    @pl.loop(0, 4)
    def _(g):
        @pl.loop(g * group, (g + 1) * group)
        def _(k):
            @pl.when(k > 0)
            def _():
                z_copy(k).wait_recv()

        @pl.loop(1, nyc)
        def _(d):
            g_copy(g, lax.rem(me_yc + d, nyc)).start()

        gbuf[me_yc, pl.ds(g * group, group)] = zbuf[pl.ds(g * group, group), me_yc]

    def f_copy(i):
        return pltpu.make_async_remote_copy(
            src_ref=qbuf.at[xy_slot(i)], dst_ref=qbuf.at[xy_slot(i)], send_sem=f_s.at[i], recv_sem=f_r.at[i],
            device_id=at(x, y, z, 1 - c), device_id_type=MESH,
        )

    def f_got(i):
        other = i * CORES + 1 - c
        return pltpu.make_async_remote_copy(
            src_ref=qbuf.at[other], dst_ref=qbuf.at[other], send_sem=f_s.at[i], recv_sem=f_r.at[i],
            device_id=at(x, y, z, 1 - c), device_id_type=MESH,
        )

    f_copy(me_xy).start()

    @pl.loop(1, spots)
    def _(d):
        i = lax.rem(me_xy + d, spots)
        q_copy(i, xy_slot(i)).wait_recv()
        f_copy(i).start()

    @pl.loop(0, 4)
    def _(g):
        @pl.loop(1, nyc)
        def _(d):
            g_got(g, lax.rem(me_yc + d, nyc)).wait_recv()

    total = nyc * nz * TILE
    got = gbuf[...].reshape(total, 128)
    in_tile = lax.broadcasted_iota(jnp.int32, (8, 128), 1) & (TILE - 1)
    read = onehot(in_tile > DEAD_SLOT)
    tags = jnp.concatenate(
        [
            jnp.dot(read, got[i * 128 : (i + 1) * 128], preferred_element_type=jnp.float32)[0:1]
            for i in range(total // 128)
        ],
        axis=1,
    )
    ones = jnp.ones((total, 128), jnp.bfloat16)
    name = (lax.broadcasted_iota(jnp.int32, (sub, total), 0) + 128).astype(jnp.float32)

    def x_copy(to, frm):
        return pltpu.make_async_remote_copy(
            src_ref=rs_send.at[to], dst_ref=rs_recv.at[frm], send_sem=x_s.at[to], recv_sem=x_r.at[frm],
            device_id=at(to, y, z, c), device_id_type=MESH,
        )

    def tally(to):
        scale = jnp.float32(1.0)
        for i in range(1, nx):
            scale = jnp.where(to == i, 0.5**i, scale)
        here = tags * scale
        hits = jnp.concatenate([onehot(name == here), onehot(name == here * 0.5**nx)], axis=0)
        sums = jnp.dot(hits, got, preferred_element_type=jnp.float32)
        count = jnp.dot(hits, ones, preferred_element_type=jnp.float32)
        is_dead = count[sub:] > 0.5
        return jnp.where(is_dead, sums[sub:], sums[:sub]), jnp.where(is_dead, -1.0, count[:sub])

    for d in range(1, nx + 1):
        to = lax.rem(x + d, nx)
        sums, count = tally(to)
        ref = rs_send if d < nx else rs_recv
        ref[to, 0:sub, :] = sums
        ref[to, sub : sub + 8, :] = count.T[0:8]
        if d < nx:
            x_copy(to, x).start()
    for d in range(1, nx):
        x_copy(lax.rem(x + d, nx), lax.rem(x + d, nx)).wait_recv()

    count = jnp.zeros((1, 128), jnp.float32)
    dead_row = jnp.zeros((1, 128), jnp.float32)
    sums = jnp.zeros((sub, 128), jnp.float32)
    restart = jnp.zeros((sub, 128), jnp.float32)
    for i in range(nx):
        part = rs_recv[i, sub : sub + 1, :]
        count += jnp.maximum(part, 0.0)
        dead_row = jnp.maximum(dead_row, -part)
        piece = rs_recv[i, 0:sub, :]
        sums += piece
        restart += jnp.where(column(part) < 0.0, piece, 0.0)
    for load in loads[5:]:
        load.wait()
    fresh_row = DECAY * ema_c[pl.ds(x, 1), :] + (1.0 - DECAY) * count
    fresh_row = jnp.where(dead_row > 0.5, 1.0, fresh_row)
    fresh = DECAY * ema_s[...] + (1.0 - DECAY) * sums
    fresh = jnp.where(column(dead_row) > 0.5, restart, fresh)
    rows_out = fresh / column(fresh_row)
    code[0] = (-2.0 * rows_out.astype(jnp.bfloat16).astype(jnp.float32)).astype(jnp.bfloat16)

    def right(t):
        return pltpu.make_async_remote_copy(
            src_ref=code.at[jnp.maximum(2 * t - 1, 0)], dst_ref=code.at[2 * t + 1],
            send_sem=right_s.at[t], recv_sem=right_r.at[t], device_id=along_z(1), device_id_type=MESH,
        )

    def left(t):
        return pltpu.make_async_remote_copy(
            src_ref=code.at[2 * t], dst_ref=code.at[2 * t + 2],
            send_sem=left_s.at[t], recv_sem=left_r.at[t], device_id=along_z(-1), device_id_type=MESH,
        )

    right(jnp.int32(0)).start()
    left(jnp.int32(0)).start()

    book[mine, :] = rows_out
    cnts[x] = jnp.broadcast_to(fresh_row, (8, 128))

    def b_copy(to, frm):
        span = pl.ds(pl.multiple_of(frm * sub, sub), sub)
        return pltpu.make_async_remote_copy(
            src_ref=book.at[span], dst_ref=book.at[span], send_sem=b_s.at[to], recv_sem=b_r.at[frm],
            device_id=at(to, y, z, c), device_id_type=MESH,
        )

    def c_copy(to, frm):
        return pltpu.make_async_remote_copy(
            src_ref=cnts.at[frm], dst_ref=cnts.at[frm], send_sem=c_s.at[to], recv_sem=c_r.at[frm],
            device_id=at(to, y, z, c), device_id_type=MESH,
        )

    for d in range(1, nx):
        to = lax.rem(x + d, nx)
        b_copy(to, x).start()
        c_copy(to, x).start()

    @pl.loop(0, spots)
    def _(i):
        f_got(i).wait_recv()

    def m_copy(to, frm):
        return pltpu.make_async_remote_copy(
            src_ref=low_send.at[to], dst_ref=low_recv.at[frm], send_sem=m_s.at[to], recv_sem=m_r.at[frm],
            device_id=in_plane(to), device_id_type=MESH,
        )

    halves = queries // 128

    def lowest(p):
        small = jnp.min(acc[p], axis=0, keepdims=True)
        parts = [jnp.broadcast_to(small[:, h * 128 : (h + 1) * 128], (8 // halves, 128)) for h in range(halves)]
        return jnp.concatenate(parts, axis=0)

    steps = nz // 2
    unroll = min(16, planes // 2)

    @pl.loop(0, steps)
    def _(t):
        right(t).wait_recv()

        @pl.when(t < steps - 1)
        def _():
            right(t + 1).start()
            left(t).wait_recv()

        @pl.when(t < steps - 2)
        def _():
            left(t + 1).start()

        wide_table = code[pl.ds(2 * t, 2)].reshape(2 * sub, 128).astype(jnp.float32)
        norm[...] = jnp.broadcast_to(0.25 * jnp.sum(wide_table * wide_table, axis=1, keepdims=True), (2 * sub, 128))

        @pl.loop(0, planes // unroll)
        def _(o):
            for i in range(unroll):
                p = lax.rem(me_p + 1 + o * unroll + i, planes)
                score = jnp.dot(
                    code[pl.ds(2 * t, 2)].reshape(2 * sub, 128), qbuf[p], preferred_element_type=jnp.float32
                )
                lows = [
                    jnp.min((norm[...] + score[:, h * 128 : (h + 1) * 128]).reshape(2 * sub // 8, 8, 128), axis=0)
                    for h in range(halves)
                ]
                acc[p] = jnp.minimum(acc[p], jnp.concatenate(lows, axis=1))

            @pl.when(t == steps - 1)
            def _():
                @pl.loop(o * unroll, jnp.minimum((o + 1) * unroll, planes - 1))
                def _(i):
                    to = lax.rem(me_p + 1 + i, planes)
                    low_send[to] = lowest(to)
                    m_copy(to, me_p).start()

    low_recv[me_p] = lowest(me_p)

    @pl.loop(1, planes)
    def _(d):
        frm = lax.rem(me_p + d, planes)
        m_copy(frm, frm).wait_recv()

    best = jnp.min(low_recv[...], axis=0)
    for h in range(halves):
        first = h * (8 // halves)
        dist[h : h + 1, :] = (best[first : first + 1] + query_norm[:, h * 128 : (h + 1) * 128]) / 128

    for d in range(1, nx):
        frm = lax.rem(x + d, nx)
        b_copy(frm, frm).wait_recv()
        c_copy(frm, frm).wait_recv()
    for i in range(nx):
        cnt_out[i : i + 1, :] = cnts[i, 0:1, :]

    @pl.loop(1, nz)
    def _(k):
        z_copy(k).wait_send()

    @pl.loop(1, spots)
    def _(d):
        q_send(lax.rem(me_xy + d, spots)).wait_send()

    @pl.loop(0, spots)
    def _(i):
        f_copy(i).wait_send()

    @pl.loop(0, 4)
    def _(g):
        @pl.loop(1, nyc)
        def _(d):
            g_copy(g, lax.rem(me_yc + d, nyc)).wait_send()

    for d in range(1, nx):
        to = lax.rem(x + d, nx)
        x_copy(to, x).wait_send()
        b_copy(to, x).wait_send()
        c_copy(to, x).wait_send()

    @pl.loop(0, steps)
    def _(t):
        right(t).wait_send()

        @pl.when(t < steps - 1)
        def _():
            left(t).wait_send()

    @pl.loop(1, planes)
    def _(d):
        m_copy(lax.rem(me_p + d, planes), me_p).wait_send()


def per_device(nx, ny, nz, latents, code_ids, ema_sums, ema_counts, dead_codes, restart_index, next_latents):
    k_dev = ema_sums.shape[0]
    sub = k_dev // nx
    nyc = ny * CORES
    planes = nx * nyc
    queries = next_latents.shape[0]
    hbm = pl.BlockSpec(memory_space=pl.ANY)
    vmem = pl.BlockSpec(memory_space=pltpu.VMEM)
    dma = pltpu.SemaphoreType.DMA
    bf16, f32 = jnp.bfloat16, jnp.float32
    book, counts, dist = pl.pallas_call(
        functools.partial(body, nx, ny, nz),
        out_shape=(
            jax.ShapeDtypeStruct((k_dev, 128), f32),
            jax.ShapeDtypeStruct((nx, sub), f32),
            jax.ShapeDtypeStruct((queries // 128, 128), f32),
        ),
        in_specs=[hbm] * 7,
        out_specs=(vmem,) * 3,
        scratch_shapes=[
            pltpu.VMEM(latents.shape, bf16),
            pltpu.VMEM((1, code_ids.shape[0]), jnp.int32),
            pltpu.VMEM((1, dead_codes.shape[0]), jnp.int32),
            pltpu.VMEM((1, dead_codes.shape[0]), jnp.int32),
            pltpu.VMEM((sub, 128), f32),
            pltpu.VMEM((nx, sub), f32),
            pltpu.VMEM((queries, 128), bf16),
            pltpu.VMEM((128, queries), bf16),
            pltpu.VMEM((nz, nyc, TILE, 128), bf16),
            pltpu.VMEM((nz, nyc, TILE, 128), bf16),
            pltpu.VMEM((nyc, nz, TILE, 128), bf16),
            pltpu.VMEM((planes, 128, queries), bf16),
            pltpu.VMEM((8, 128), jnp.int32),
            pltpu.VMEM((nx, sub + 8, 128), f32),
            pltpu.VMEM((nx, sub + 8, 128), f32),
            pltpu.VMEM((nz, sub, 128), bf16),
            pltpu.VMEM((2 * sub, 128), f32),
            pltpu.VMEM((planes, 8, queries), f32),
            pltpu.VMEM((planes, 8, 128), f32),
            pltpu.VMEM((planes, 8, 128), f32),
            pltpu.VMEM((nx, 8, 128), f32),
            dma((7,)),
            dma((nz,)), dma((nz,)),
            dma((4, nyc)), dma((4, nyc)),
            dma((nx * ny,)), dma((nx * ny,)),
            dma((nx * ny,)), dma((nx * ny,)),
            dma((nx,)), dma((nx,)),
            dma((nx,)), dma((nx,)),
            dma((nx,)), dma((nx,)),
            dma((nz // 2,)), dma((nz // 2,)),
            dma((nz // 2,)), dma((nz // 2,)),
            dma((planes,)), dma((planes,)),
        ],
        compiler_params=pltpu.CompilerParams(
            collective_id=0, has_side_effects=True, vmem_limit_bytes=56 * 1024 * 1024
        ),
    )(
        latents, code_ids.reshape(1, -1), dead_codes.reshape(1, -1), restart_index.reshape(1, -1),
        ema_sums, ema_counts.reshape(nx, sub), next_latents,
    )
    return book, counts.reshape(-1), dist.reshape(-1)


def solution(mesh, ny=4):
    nx = mesh.shape["dp"]
    nz = mesh.shape["code"] // (CORES * ny)
    in_specs = (
        P(("dp", "code"), None),
        P(("dp", "code")),
        P("code", None),
        P("code"),
        P(("dp", "code")),
        P(("dp", "code")),
        P(("dp", "code"), None),
    )
    reorder = functools.partial(per_device, nx, ny, nz)
    return jax.shard_map(
        lambda a, b, s, n, d, r, q: reorder(a, b, s, n, d, r, q),
        mesh=mesh,
        in_specs=in_specs,
        out_specs=(P("code", None), P("code"), P(("dp", "code"))),
        check_vma=False,
    )
```

```python
import functools

import jax
import jax.numpy as jnp
from jax import lax
from jax.experimental import pallas as pl
from jax.experimental.pallas import tpu as pltpu
from jax.sharding import PartitionSpec as P

MESH = pl.DeviceIdType.MESH
DECAY = 0.8
TILE = 16
USED = 14
DEAD_SLOT = 12
CORES = 2
BIG = 3.0e38


def onehot(mask):
    return jnp.where(mask, 1.0, 0.0).astype(jnp.bfloat16)


def column(row):
    return jnp.broadcast_to(row, (128, 128)).T


def body(
    nx, ny, nz, lat_in, ids_in, dead_in, ridx_in, ema_s_in, ema_c_in, nxt_in, book, cnt_out, dist,
    lat, ids, dead, ridx, ema_s, ema_c, nxt, turned,
    pack, zbuf, relay, gsrc, gbuf, qbuf, ext, rs_send, rs_recv, code, norm, acc, low_send, low_recv, cnts, in_s,
    z_s, z_r, relay_s, relay_r, g_s, g_r, q_s, q_r, f_s, f_r, x_s, x_r, b_s, b_r, c_s, c_r, right_s, right_r, left_s, left_r, m_s, m_r,
):
    rows = lat.shape[0]
    k_dev = book.shape[0]
    sub = k_dev // nx
    queries = nxt.shape[0]
    nyc = ny * CORES
    planes = nx * nyc
    group = nz // 4
    block = nyc * USED
    shift_k = k_dev.bit_length() - 1
    shift_z = nz.bit_length() - 1

    x = lax.axis_index("dp")
    me = lax.axis_index("code")
    c = lax.rem(me, CORES)
    z = lax.rem(lax.div(me, CORES), nz)
    y = lax.div(me, CORES * nz)
    me_yc = y * CORES + c
    me_p = x * nyc + me_yc

    def at(ax, ay, az, ac):
        return (ax, (ay * nz + az) * CORES + ac)

    def in_plane(p):
        yc = lax.rem(p, nyc)
        return at(lax.div(p, nyc), lax.div(yc, CORES), z, lax.rem(yc, CORES))

    def along_z(d):
        return at(x, y, lax.rem(z + d + nz, nz), c)

    mine = pl.ds(pl.multiple_of(x * sub, sub), sub)
    sources = (lat_in, ids_in, dead_in, ridx_in, nxt_in, ema_c_in, ema_s_in.at[mine])
    loads = [
        pltpu.make_async_copy(src, dst, in_s.at[i])
        for i, (src, dst) in enumerate(zip(sources, (lat, ids, dead, ridx, nxt, ema_c, ema_s)))
    ]
    for load in loads:
        load.start()

    barrier = pltpu.get_barrier_semaphore()

    @pl.loop(1, planes)
    def _(d):
        pl.semaphore_signal(barrier, inc=1, device_id=in_plane(lax.rem(me_p + d, planes)), device_id_type=MESH)

    @pl.loop(1, nz)
    def _(d):
        pl.semaphore_signal(barrier, inc=1, device_id=along_z(d), device_id_type=MESH)

    for load in loads[:4]:
        load.wait()
    lanes = rows + 128
    own = ids[...]

    def place(labels):
        owner = labels >> shift_k
        oc, oz, oy = owner & 1, (owner >> 1) & (nz - 1), owner >> (1 + shift_z)
        return oz * nyc + oy * CORES + oc

    owner = place(own)
    match = lax.broadcasted_iota(jnp.int32, (nyc * nz, rows), 0) == owner
    before = lax.broadcasted_iota(jnp.int32, (rows, rows), 0) < lax.broadcasted_iota(jnp.int32, (rows, rows), 1)
    earlier = jnp.dot(onehot(match), onehot(before), preferred_element_type=jnp.float32)
    rank = jnp.sum(jnp.where(match, earlier, 0.0), axis=0, keepdims=True).astype(jnp.int32)

    ext[...] = jnp.full(ext.shape, -1, jnp.int32)
    ext[0:1, 0 : dead.shape[1]] = dead[...]
    ext[1:2, 0 : dead.shape[1]] = ridx[...]
    gone = ext[0:1, :]
    gone_owner = jnp.where(gone >= 0, place(gone), -1024)
    pick = column(ext[1:2, :].astype(jnp.float32)).astype(jnp.int32)
    lane = lax.broadcasted_iota(jnp.int32, (128, 128), 1)
    picks = jnp.concatenate([onehot(pick == lane + 128 * i) for i in range(rows // 128)], axis=1)
    restarts = jnp.dot(picks, lat[...], preferred_element_type=jnp.float32).astype(jnp.bfloat16)

    all_owner = jnp.concatenate([owner, gone_owner], axis=1)
    slot = jnp.concatenate([rank, jnp.full((1, 128), DEAD_SLOT, jnp.int32)], axis=1)
    tag = jnp.concatenate([own & (k_dev - 1), (gone & (k_dev - 1)) + k_dev], axis=1)
    tag = jnp.left_shift(128 + (tag & 127), tag >> 7).astype(jnp.float32)
    local = all_owner & (nyc - 1)
    goal = all_owner >> (nyc.bit_length() - 1)
    key = local * (USED - 1) + slot
    tag_key = local + nyc * (USED - 1)
    spot = jnp.where((lax.broadcasted_iota(jnp.int32, (128, lanes), 0) & (TILE - 1)) == slot, 1.0, 0.0)
    spot = jnp.concatenate([spot[:, i * 128 : (i + 1) * 128].T for i in range(lanes // 128)], axis=0)
    data = jnp.concatenate([jnp.concatenate([lat[...], restarts], axis=0), spot.astype(jnp.bfloat16)], axis=1)
    line = lax.broadcasted_iota(jnp.int32, (block, lanes), 0)
    lane_tile = lax.broadcasted_iota(jnp.int32, (1, 128), 1) >> 4

    half = nz // 2
    way = 1 - 2 * c

    def offset(k):
        return jnp.where(lax.rem(k, 2) == 1, half - lax.div(k + 1, 2), nz - half + lax.div(k, 2))

    def packed(k):
        to = goal == lax.rem(z + offset(k), nz)
        put = jnp.where(line == jnp.where(to, key, -1), 1.0, jnp.where(line == jnp.where(to, tag_key, -1), tag, 0.0))
        moved = jnp.dot(put.astype(jnp.bfloat16), data, preferred_element_type=jnp.float32)
        here = lax.rem(me_yc * nz + k, 8)
        tags = jnp.where(lane_tile == here, moved[:, 128:], 0.0)
        is_tag = lax.broadcasted_iota(jnp.int32, (block, 128), 0) >= nyc * (USED - 1)
        return jnp.where(is_tag, tags, moved[:, :128]).astype(jnp.bfloat16)

    def z_copy(k):
        return pltpu.make_async_remote_copy(
            src_ref=pack.at[k], dst_ref=zbuf.at[k], send_sem=z_s.at[k], recv_sem=z_r.at[k],
            device_id=along_z(offset(k)), device_id_type=MESH,
        )

    def relay_in():
        return pltpu.make_async_remote_copy(
            src_ref=pack.at[0], dst_ref=relay, send_sem=z_s.at[0], recv_sem=relay_r,
            device_id=along_z(way), device_id_type=MESH,
        )

    def relay_out():
        return pltpu.make_async_remote_copy(
            src_ref=relay, dst_ref=zbuf.at[0], send_sem=relay_s, recv_sem=z_r.at[0],
            device_id=along_z(way * (half - 1)), device_id_type=MESH,
        )

    pack[0] = packed(jnp.int32(0))
    pl.semaphore_wait(barrier, planes - 1 + nz - 1)
    relay_in().start()

    @pl.loop(0, half - 1)
    def _(o):
        for i in range(2):
            k = 1 + o * 2 + i
            pack[k] = packed(k)
            z_copy(k).start()

        @pl.when(o == (half - 1) // 2)
        def _():
            relay_in().wait_recv()
            relay_out().start()

    zbuf[nz - 1] = packed(jnp.int32(nz - 1))

    loads[4].wait()
    wide = nxt[...].astype(jnp.float32)
    query_norm = jnp.sum((wide * wide).T, axis=0, keepdims=True)
    turned[...] = wide.T.astype(jnp.bfloat16)

    def xy_slot(i):
        return i * CORES + c

    def q_copy(i, slot_index):
        return pltpu.make_async_remote_copy(
            src_ref=turned, dst_ref=qbuf.at[slot_index], send_sem=q_s.at[i], recv_sem=q_r.at[i],
            device_id=in_plane(xy_slot(i)), device_id_type=MESH,
        )

    spots = nx * ny
    me_xy = x * ny + y

    def q_send(i):
        return pltpu.make_async_remote_copy(
            src_ref=turned, dst_ref=qbuf.at[me_p], send_sem=q_s.at[i], recv_sem=q_r.at[me_xy],
            device_id=in_plane(xy_slot(i)), device_id_type=MESH,
        )

    @pl.loop(1, spots)
    def _(d):
        q_send(lax.rem(me_xy + d, spots)).start()

    qbuf[me_p] = turned[...]
    acc[...] = jnp.full(acc.shape, BIG, jnp.float32)

    def g_copy(g, j):
        return pltpu.make_async_remote_copy(
            src_ref=gsrc.at[pl.ds(g * group, group), j],
            dst_ref=gbuf.at[me_yc, pl.ds(g * group, group)],
            send_sem=g_s.at[g, j], recv_sem=g_r.at[g, me_yc],
            device_id=at(x, lax.div(j, CORES), z, lax.rem(j, CORES)), device_id_type=MESH,
        )

    def g_got(g, j):
        return pltpu.make_async_remote_copy(
            src_ref=gsrc.at[pl.ds(g * group, group), j],
            dst_ref=gbuf.at[j, pl.ds(g * group, group)],
            send_sem=g_s.at[g, j], recv_sem=g_r.at[g, j],
            device_id=at(x, lax.div(j, CORES), z, lax.rem(j, CORES)), device_id_type=MESH,
        )

    row = lax.broadcasted_iota(jnp.int32, (nyc * TILE, block), 0)
    tile, spare = row >> 4, (row & (TILE - 1)) - DEAD_SLOT
    origin = jnp.where(spare <= 0, tile * (USED - 1) + DEAD_SLOT + spare, jnp.where(spare == 1, tile + nyc * (USED - 1), -1))
    spread = onehot(lax.broadcasted_iota(jnp.int32, (nyc * TILE, block), 1) == origin)

    @pl.loop(0, 4)
    def _(g):
        @pl.loop(g * group, jnp.minimum((g + 1) * group, nz - 1))
        def _(k):
            z_copy(k).wait_recv()

        for i in range(group):
            k = g * group + i
            tiles = jnp.dot(spread, zbuf[k], preferred_element_type=jnp.float32)
            gsrc[k] = tiles.astype(jnp.bfloat16).reshape(nyc, TILE, 128)

        @pl.loop(1, nyc)
        def _(d):
            g_copy(g, lax.rem(me_yc + d, nyc)).start()

        gbuf[me_yc, pl.ds(g * group, group)] = gsrc[pl.ds(g * group, group), me_yc]

    def f_copy(i):
        return pltpu.make_async_remote_copy(
            src_ref=qbuf.at[xy_slot(i)], dst_ref=qbuf.at[xy_slot(i)], send_sem=f_s.at[i], recv_sem=f_r.at[i],
            device_id=at(x, y, z, 1 - c), device_id_type=MESH,
        )

    def f_got(i):
        other = i * CORES + 1 - c
        return pltpu.make_async_remote_copy(
            src_ref=qbuf.at[other], dst_ref=qbuf.at[other], send_sem=f_s.at[i], recv_sem=f_r.at[i],
            device_id=at(x, y, z, 1 - c), device_id_type=MESH,
        )

    f_copy(me_xy).start()

    @pl.loop(1, spots)
    def _(d):
        i = lax.rem(me_xy + d, spots)
        q_copy(i, xy_slot(i)).wait_recv()
        f_copy(i).start()

    @pl.loop(0, 4)
    def _(g):
        @pl.loop(1, nyc)
        def _(d):
            g_got(g, lax.rem(me_yc + d, nyc)).wait_recv()

    total = nyc * nz * TILE
    got = gbuf[...].reshape(total, 128)
    in_tile = lax.broadcasted_iota(jnp.int32, (8, 128), 1) & (TILE - 1)
    read = onehot(in_tile > DEAD_SLOT)
    tags = jnp.concatenate(
        [
            jnp.dot(read, got[i * 128 : (i + 1) * 128], preferred_element_type=jnp.float32)[0:1]
            for i in range(total // 128)
        ],
        axis=1,
    )
    ones = jnp.ones((total, 128), jnp.bfloat16)
    name = (lax.broadcasted_iota(jnp.int32, (sub, total), 0) + 128).astype(jnp.float32)

    def x_copy(to, frm):
        return pltpu.make_async_remote_copy(
            src_ref=rs_send.at[to], dst_ref=rs_recv.at[frm], send_sem=x_s.at[to], recv_sem=x_r.at[frm],
            device_id=at(to, y, z, c), device_id_type=MESH,
        )

    def tally(to):
        scale = jnp.float32(1.0)
        for i in range(1, nx):
            scale = jnp.where(to == i, 0.5**i, scale)
        here = tags * scale
        hits = jnp.concatenate([onehot(name == here), onehot(name == here * 0.5**nx)], axis=0)
        sums = jnp.dot(hits, got, preferred_element_type=jnp.float32)
        count = jnp.dot(hits, ones, preferred_element_type=jnp.float32)
        is_dead = count[sub:] > 0.5
        return jnp.where(is_dead, sums[sub:], sums[:sub]), jnp.where(is_dead, -1.0, count[:sub])

    for d in range(1, nx + 1):
        to = lax.rem(x + d, nx)
        sums, count = tally(to)
        ref = rs_send if d < nx else rs_recv
        ref[to, 0:sub, :] = sums
        ref[to, sub : sub + 8, :] = count.T[0:8]
        if d < nx:
            x_copy(to, x).start()
    for d in range(1, nx):
        x_copy(lax.rem(x + d, nx), lax.rem(x + d, nx)).wait_recv()

    count = jnp.zeros((1, 128), jnp.float32)
    dead_row = jnp.zeros((1, 128), jnp.float32)
    sums = jnp.zeros((sub, 128), jnp.float32)
    restart = jnp.zeros((sub, 128), jnp.float32)
    for i in range(nx):
        part = rs_recv[i, sub : sub + 1, :]
        count += jnp.maximum(part, 0.0)
        dead_row = jnp.maximum(dead_row, -part)
        piece = rs_recv[i, 0:sub, :]
        sums += piece
        restart += jnp.where(column(part) < 0.0, piece, 0.0)
    for load in loads[5:]:
        load.wait()
    fresh_row = DECAY * ema_c[pl.ds(x, 1), :] + (1.0 - DECAY) * count
    fresh_row = jnp.where(dead_row > 0.5, 1.0, fresh_row)
    fresh = DECAY * ema_s[...] + (1.0 - DECAY) * sums
    fresh = jnp.where(column(dead_row) > 0.5, restart, fresh)
    rows_out = fresh / column(fresh_row)
    code[0] = (-2.0 * rows_out.astype(jnp.bfloat16).astype(jnp.float32)).astype(jnp.bfloat16)

    def right(t):
        return pltpu.make_async_remote_copy(
            src_ref=code.at[jnp.maximum(2 * t - 1, 0)], dst_ref=code.at[2 * t + 1],
            send_sem=right_s.at[t], recv_sem=right_r.at[t], device_id=along_z(1), device_id_type=MESH,
        )

    def left(t):
        return pltpu.make_async_remote_copy(
            src_ref=code.at[2 * t], dst_ref=code.at[2 * t + 2],
            send_sem=left_s.at[t], recv_sem=left_r.at[t], device_id=along_z(-1), device_id_type=MESH,
        )

    right(jnp.int32(0)).start()
    left(jnp.int32(0)).start()

    book[mine, :] = rows_out
    cnts[x] = jnp.broadcast_to(fresh_row, (8, 128))

    def b_copy(to, frm):
        span = pl.ds(pl.multiple_of(frm * sub, sub), sub)
        return pltpu.make_async_remote_copy(
            src_ref=book.at[span], dst_ref=book.at[span], send_sem=b_s.at[to], recv_sem=b_r.at[frm],
            device_id=at(to, y, z, c), device_id_type=MESH,
        )

    def c_copy(to, frm):
        return pltpu.make_async_remote_copy(
            src_ref=cnts.at[frm], dst_ref=cnts.at[frm], send_sem=c_s.at[to], recv_sem=c_r.at[frm],
            device_id=at(to, y, z, c), device_id_type=MESH,
        )

    for d in range(1, nx):
        to = lax.rem(x + d, nx)
        b_copy(to, x).start()
        c_copy(to, x).start()

    @pl.loop(0, spots)
    def _(i):
        f_got(i).wait_recv()

    def m_copy(to, frm):
        return pltpu.make_async_remote_copy(
            src_ref=low_send.at[to], dst_ref=low_recv.at[frm], send_sem=m_s.at[to], recv_sem=m_r.at[frm],
            device_id=in_plane(to), device_id_type=MESH,
        )

    halves = queries // 128

    def lowest(p):
        small = jnp.min(acc[p], axis=0, keepdims=True)
        parts = [jnp.broadcast_to(small[:, h * 128 : (h + 1) * 128], (8 // halves, 128)) for h in range(halves)]
        return jnp.concatenate(parts, axis=0)

    steps = nz // 2
    unroll = min(16, planes // 2)

    @pl.loop(0, steps)
    def _(t):
        right(t).wait_recv()

        @pl.when(t < steps - 1)
        def _():
            right(t + 1).start()
            left(t).wait_recv()

        @pl.when(t < steps - 2)
        def _():
            left(t + 1).start()

        wide_table = code[pl.ds(2 * t, 2)].reshape(2 * sub, 128).astype(jnp.float32)
        norm[...] = jnp.broadcast_to(0.25 * jnp.sum(wide_table * wide_table, axis=1, keepdims=True), (2 * sub, 128))

        @pl.loop(0, planes // unroll)
        def _(o):
            for i in range(unroll):
                p = lax.rem(me_p + 1 + o * unroll + i, planes)
                score = jnp.dot(
                    code[pl.ds(2 * t, 2)].reshape(2 * sub, 128), qbuf[p], preferred_element_type=jnp.float32
                )
                lows = [
                    jnp.min((norm[...] + score[:, h * 128 : (h + 1) * 128]).reshape(2 * sub // 8, 8, 128), axis=0)
                    for h in range(halves)
                ]
                acc[p] = jnp.minimum(acc[p], jnp.concatenate(lows, axis=1))

            @pl.when(t == steps - 1)
            def _():
                @pl.loop(o * unroll, jnp.minimum((o + 1) * unroll, planes - 1))
                def _(i):
                    to = lax.rem(me_p + 1 + i, planes)
                    low_send[to] = lowest(to)
                    m_copy(to, me_p).start()

    low_recv[me_p] = lowest(me_p)

    @pl.loop(1, planes)
    def _(d):
        frm = lax.rem(me_p + d, planes)
        m_copy(frm, frm).wait_recv()

    best = jnp.min(low_recv[...], axis=0)
    for h in range(halves):
        first = h * (8 // halves)
        dist[h : h + 1, :] = (best[first : first + 1] + query_norm[:, h * 128 : (h + 1) * 128]) / 128

    for d in range(1, nx):
        frm = lax.rem(x + d, nx)
        b_copy(frm, frm).wait_recv()
        c_copy(frm, frm).wait_recv()
    for i in range(nx):
        cnt_out[i : i + 1, :] = cnts[i, 0:1, :]

    relay_in().wait_send()
    relay_out().wait_send()

    @pl.loop(1, nz - 1)
    def _(k):
        z_copy(k).wait_send()

    @pl.loop(1, spots)
    def _(d):
        q_send(lax.rem(me_xy + d, spots)).wait_send()

    @pl.loop(0, spots)
    def _(i):
        f_copy(i).wait_send()

    @pl.loop(0, 4)
    def _(g):
        @pl.loop(1, nyc)
        def _(d):
            g_copy(g, lax.rem(me_yc + d, nyc)).wait_send()

    for d in range(1, nx):
        to = lax.rem(x + d, nx)
        x_copy(to, x).wait_send()
        b_copy(to, x).wait_send()
        c_copy(to, x).wait_send()

    @pl.loop(0, steps)
    def _(t):
        right(t).wait_send()

        @pl.when(t < steps - 1)
        def _():
            left(t).wait_send()

    @pl.loop(1, planes)
    def _(d):
        m_copy(lax.rem(me_p + d, planes), me_p).wait_send()


def hand_over(book, counts, dist, book_out, counts_out, dist_out, sem):
    pairs = ((book, book_out), (counts, counts_out), (dist, dist_out))
    copies = [pltpu.make_async_copy(src, dst, sem.at[i]) for i, (src, dst) in enumerate(pairs)]
    for copy in copies:
        copy.start()
    for copy in copies:
        copy.wait()


def per_device(nx, ny, nz, latents, code_ids, ema_sums, ema_counts, dead_codes, restart_index, next_latents):
    k_dev = ema_sums.shape[0]
    sub = k_dev // nx
    nyc = ny * CORES
    planes = nx * nyc
    queries = next_latents.shape[0]
    hbm = pl.BlockSpec(memory_space=pl.ANY)
    vmem = pl.BlockSpec(memory_space=pltpu.VMEM)
    dma = pltpu.SemaphoreType.DMA
    bf16, f32 = jnp.bfloat16, jnp.float32
    book, counts, dist = pl.pallas_call(
        functools.partial(body, nx, ny, nz),
        out_shape=(
            jax.ShapeDtypeStruct((k_dev, 128), f32),
            jax.ShapeDtypeStruct((nx, sub), f32),
            jax.ShapeDtypeStruct((queries // 128, 128), f32),
        ),
        in_specs=[hbm] * 7,
        out_specs=(vmem,) * 3,
        scratch_shapes=[
            pltpu.VMEM(latents.shape, bf16),
            pltpu.VMEM((1, code_ids.shape[0]), jnp.int32),
            pltpu.VMEM((1, dead_codes.shape[0]), jnp.int32),
            pltpu.VMEM((1, dead_codes.shape[0]), jnp.int32),
            pltpu.VMEM((sub, 128), f32),
            pltpu.VMEM((nx, sub), f32),
            pltpu.VMEM((queries, 128), bf16),
            pltpu.VMEM((128, queries), bf16),
            pltpu.VMEM((nz, nyc * USED, 128), bf16),
            pltpu.VMEM((nz, nyc * USED, 128), bf16),
            pltpu.VMEM((nyc * USED, 128), bf16),
            pltpu.VMEM((nz, nyc, TILE, 128), bf16),
            pltpu.VMEM((nyc, nz, TILE, 128), bf16),
            pltpu.VMEM((planes, 128, queries), bf16),
            pltpu.VMEM((8, 128), jnp.int32),
            pltpu.VMEM((nx, sub + 8, 128), f32),
            pltpu.VMEM((nx, sub + 8, 128), f32),
            pltpu.VMEM((nz, sub, 128), bf16),
            pltpu.VMEM((2 * sub, 128), f32),
            pltpu.VMEM((planes, 8, queries), f32),
            pltpu.VMEM((planes, 8, 128), f32),
            pltpu.VMEM((planes, 8, 128), f32),
            pltpu.VMEM((nx, 8, 128), f32),
            dma((7,)),
            dma((nz,)), dma((nz,)),
            dma, dma,
            dma((4, nyc)), dma((4, nyc)),
            dma((nx * ny,)), dma((nx * ny,)),
            dma((nx * ny,)), dma((nx * ny,)),
            dma((nx,)), dma((nx,)),
            dma((nx,)), dma((nx,)),
            dma((nx,)), dma((nx,)),
            dma((nz // 2,)), dma((nz // 2,)),
            dma((nz // 2,)), dma((nz // 2,)),
            dma((planes,)), dma((planes,)),
        ],
        compiler_params=pltpu.CompilerParams(
            collective_id=0, has_side_effects=True, vmem_limit_bytes=56 * 1024 * 1024
        ),
    )(
        latents, code_ids.reshape(1, -1), dead_codes.reshape(1, -1), restart_index.reshape(1, -1),
        ema_sums, ema_counts.reshape(nx, sub), next_latents,
    )
    return pl.pallas_call(
        hand_over,
        out_shape=(
            jax.ShapeDtypeStruct((k_dev, 128), f32),
            jax.ShapeDtypeStruct((k_dev,), f32),
            jax.ShapeDtypeStruct((queries,), f32),
        ),
        in_specs=[hbm] * 3,
        out_specs=(hbm,) * 3,
        scratch_shapes=[dma((3,))],
        compiler_params=pltpu.CompilerParams(vmem_limit_bytes=56 * 1024 * 1024),
    )(book, counts.reshape(-1), dist.reshape(-1))


def solution(mesh, ny=4):
    nx = mesh.shape["dp"]
    nz = mesh.shape["code"] // (CORES * ny)
    in_specs = (
        P(("dp", "code"), None),
        P(("dp", "code")),
        P("code", None),
        P("code"),
        P(("dp", "code")),
        P(("dp", "code")),
        P(("dp", "code"), None),
    )
    reorder = functools.partial(per_device, nx, ny, nz)
    return jax.shard_map(
        lambda a, b, s, n, d, r, q: reorder(a, b, s, n, d, r, q),
        mesh=mesh,
        in_specs=in_specs,
        out_specs=(P("code", None), P("code"), P(("dp", "code"))),
        check_vma=False,
    )
```

```python
import functools

import jax
import jax.numpy as jnp
from jax import lax
from jax.experimental import pallas as pl
from jax.experimental.pallas import tpu as pltpu
from jax.sharding import PartitionSpec as P

MESH = pl.DeviceIdType.MESH
DECAY = 0.8
TILE = 16
USED = 14
DEAD_SLOT = 12
CORES = 2
BIG = 3.0e38


def onehot(mask):
    return jnp.where(mask, 1.0, 0.0).astype(jnp.bfloat16)


def column(row):
    return jnp.broadcast_to(row, (128, 128)).T


def body(
    nx, ny, nz, lat_in, ids_in, dead_in, ridx_in, ema_s_in, ema_c_in, nxt_in, book, cnt_out, dist,
    lat, ids, dead, ridx, ema_s, ema_c, nxt, turned,
    pack, zbuf, relay, gsrc, gbuf, qbuf, ext, rs_send, rs_recv, code, norm, acc, low_send, low_recv, cnts, in_s,
    z_s, z_r, relay_s, relay_r, g_s, g_r, qy_s, qy_r, qx_s, qx_r, f_s, f_r, x_s, x_r, b_s, b_r, c_s, c_r,
    right_s, right_r, left_s, left_r, m_s, m_r,
):
    rows = lat.shape[0]
    k_dev = book.shape[0]
    sub = k_dev // nx
    queries = nxt.shape[0]
    nyc = ny * CORES
    planes = nx * nyc
    group = nz // 4
    block = nyc * USED
    shift_k = k_dev.bit_length() - 1
    shift_z = nz.bit_length() - 1

    x = lax.axis_index("dp")
    me = lax.axis_index("code")
    c = lax.rem(me, CORES)
    z = lax.rem(lax.div(me, CORES), nz)
    y = lax.div(me, CORES * nz)
    me_yc = y * CORES + c
    me_p = x * nyc + me_yc

    def at(ax, ay, az, ac):
        return (ax, (ay * nz + az) * CORES + ac)

    def in_plane(p):
        yc = lax.rem(p, nyc)
        return at(lax.div(p, nyc), lax.div(yc, CORES), z, lax.rem(yc, CORES))

    def sent(ref, sem):
        pltpu.make_async_copy(ref, ref, sem).wait()

    def along_z(d):
        return at(x, y, lax.rem(z + d + nz, nz), c)

    mine = pl.ds(pl.multiple_of(x * sub, sub), sub)
    sources = (lat_in, ids_in, dead_in, ridx_in, nxt_in, ema_c_in, ema_s_in.at[mine])
    loads = [
        pltpu.make_async_copy(src, dst, in_s.at[i])
        for i, (src, dst) in enumerate(zip(sources, (lat, ids, dead, ridx, nxt, ema_c, ema_s)))
    ]
    for load in loads:
        load.start()

    barrier = pltpu.get_barrier_semaphore()

    @pl.loop(1, planes)
    def _(d):
        pl.semaphore_signal(barrier, inc=1, device_id=in_plane(lax.rem(me_p + d, planes)), device_id_type=MESH)

    @pl.loop(1, nz)
    def _(d):
        pl.semaphore_signal(barrier, inc=1, device_id=along_z(d), device_id_type=MESH)

    for load in loads[:4]:
        load.wait()
    lanes = rows + 128
    own = ids[...]

    def place(labels):
        owner = labels >> shift_k
        oc, oz, oy = owner & 1, (owner >> 1) & (nz - 1), owner >> (1 + shift_z)
        return oz * nyc + oy * CORES + oc

    owner = place(own)
    match = lax.broadcasted_iota(jnp.int32, (nyc * nz, rows), 0) == owner
    before = lax.broadcasted_iota(jnp.int32, (rows, rows), 0) < lax.broadcasted_iota(jnp.int32, (rows, rows), 1)
    earlier = jnp.dot(onehot(match), onehot(before), preferred_element_type=jnp.float32)
    rank = jnp.sum(jnp.where(match, earlier, 0.0), axis=0, keepdims=True).astype(jnp.int32)

    ext[...] = jnp.full(ext.shape, -1, jnp.int32)
    ext[0:1, 0 : dead.shape[1]] = dead[...]
    ext[1:2, 0 : dead.shape[1]] = ridx[...]
    gone = ext[0:1, :]
    gone_owner = jnp.where(gone >= 0, place(gone), -1024)
    pick = column(ext[1:2, :].astype(jnp.float32)).astype(jnp.int32)
    lane = lax.broadcasted_iota(jnp.int32, (128, 128), 1)
    picks = jnp.concatenate([onehot(pick == lane + 128 * i) for i in range(rows // 128)], axis=1)
    restarts = jnp.dot(picks, lat[...], preferred_element_type=jnp.float32).astype(jnp.bfloat16)

    all_owner = jnp.concatenate([owner, gone_owner], axis=1)
    slot = jnp.concatenate([rank, jnp.full((1, 128), DEAD_SLOT, jnp.int32)], axis=1)
    tag = jnp.concatenate([own & (k_dev - 1), (gone & (k_dev - 1)) + k_dev], axis=1)
    tag = jnp.left_shift(128 + (tag & 127), tag >> 7).astype(jnp.float32)
    local = all_owner & (nyc - 1)
    goal = all_owner >> (nyc.bit_length() - 1)
    key = local * (USED - 1) + slot
    tag_key = local + nyc * (USED - 1)
    spot = jnp.where((lax.broadcasted_iota(jnp.int32, (128, lanes), 0) & (TILE - 1)) == slot, 1.0, 0.0)
    spot = jnp.concatenate([spot[:, i * 128 : (i + 1) * 128].T for i in range(lanes // 128)], axis=0)
    data = jnp.concatenate([jnp.concatenate([lat[...], restarts], axis=0), spot.astype(jnp.bfloat16)], axis=1)
    line = lax.broadcasted_iota(jnp.int32, (block, lanes), 0)
    lane_tile = lax.broadcasted_iota(jnp.int32, (1, 128), 1) >> 4

    half = nz // 2
    way = 1 - 2 * c

    def offset(k):
        return jnp.where(lax.rem(k, 2) == 1, half - lax.div(k + 1, 2), nz - half + lax.div(k, 2))

    def packed(k):
        to = goal == lax.rem(z + offset(k), nz)
        put = jnp.where(line == jnp.where(to, key, -1), 1.0, jnp.where(line == jnp.where(to, tag_key, -1), tag, 0.0))
        moved = jnp.dot(put.astype(jnp.bfloat16), data, preferred_element_type=jnp.float32)
        here = lax.rem(me_yc * nz + k, 8)
        tags = jnp.where(lane_tile == here, moved[:, 128:], 0.0)
        is_tag = lax.broadcasted_iota(jnp.int32, (block, 128), 0) >= nyc * (USED - 1)
        return jnp.where(is_tag, tags, moved[:, :128]).astype(jnp.bfloat16)

    def z_copy(k):
        return pltpu.make_async_remote_copy(
            src_ref=pack.at[k], dst_ref=zbuf.at[k], send_sem=z_s, recv_sem=z_r.at[lax.div(k, group)],
            device_id=along_z(offset(k)), device_id_type=MESH,
        )

    def relay_in():
        return pltpu.make_async_remote_copy(
            src_ref=pack.at[0], dst_ref=relay, send_sem=z_s, recv_sem=relay_r,
            device_id=along_z(way), device_id_type=MESH,
        )

    def relay_out():
        return pltpu.make_async_remote_copy(
            src_ref=relay, dst_ref=zbuf.at[0], send_sem=relay_s, recv_sem=z_r.at[0],
            device_id=along_z(way * (half - 1)), device_id_type=MESH,
        )

    pack[0] = packed(jnp.int32(0))
    pl.semaphore_wait(barrier, planes - 1 + nz - 1)
    relay_in().start()

    @pl.loop(0, half - 1)
    def _(o):
        for i in range(2):
            k = 1 + o * 2 + i
            pack[k] = packed(k)
            z_copy(k).start()

        @pl.when(o == (half - 1) // 2)
        def _():
            relay_in().wait_recv()
            relay_out().start()

    zbuf[nz - 1] = packed(jnp.int32(nz - 1))

    loads[4].wait()
    wide = nxt[...].astype(jnp.float32)
    query_norm = jnp.sum((wide * wide).T, axis=0, keepdims=True)
    turned[...] = wide.T.astype(jnp.bfloat16)

    def qy_copy(to):
        return pltpu.make_async_remote_copy(
            src_ref=turned, dst_ref=qbuf.at[x, y, c], send_sem=qy_s, recv_sem=qy_r,
            device_id=at(x, to, z, c), device_id_type=MESH,
        )

    def qx_copy(to):
        return pltpu.make_async_remote_copy(
            src_ref=qbuf.at[x, :, c], dst_ref=qbuf.at[x, :, c], send_sem=qx_s, recv_sem=qx_r,
            device_id=at(to, y, z, c), device_id_type=MESH,
        )

    def f_copy():
        return pltpu.make_async_remote_copy(
            src_ref=qbuf.at[:, :, c], dst_ref=qbuf.at[:, :, c], send_sem=f_s, recv_sem=f_r,
            device_id=at(x, y, z, 1 - c), device_id_type=MESH,
        )

    for d in range(1, ny):
        qy_copy(lax.rem(y + d, ny)).start()
    qbuf[x, y, c] = turned[...]
    acc[...] = jnp.full(acc.shape, BIG, jnp.float32)

    def g_copy(g, j):
        return pltpu.make_async_remote_copy(
            src_ref=gsrc.at[pl.ds(g * group, group), j],
            dst_ref=gbuf.at[me_yc, pl.ds(g * group, group)],
            send_sem=g_s, recv_sem=g_r,
            device_id=at(x, lax.div(j, CORES), z, lax.rem(j, CORES)), device_id_type=MESH,
        )

    row = lax.broadcasted_iota(jnp.int32, (nyc * TILE, block), 0)
    tile, spare = row >> 4, (row & (TILE - 1)) - DEAD_SLOT
    origin = jnp.where(spare <= 0, tile * (USED - 1) + DEAD_SLOT + spare, jnp.where(spare == 1, tile + nyc * (USED - 1), -1))
    spread = onehot(lax.broadcasted_iota(jnp.int32, (nyc * TILE, block), 1) == origin)

    for g in range(4):
        here = pl.ds(g * group, min(group, nz - 1 - g * group))
        sent(zbuf.at[here], z_r.at[g])
        for k in range(g * group, (g + 1) * group):
            tiles = jnp.dot(spread, zbuf[k], preferred_element_type=jnp.float32)
            gsrc[k] = tiles.astype(jnp.bfloat16).reshape(nyc, TILE, 128)

        @pl.loop(1, nyc)
        def _(d):
            g_copy(g, lax.rem(me_yc + d, nyc)).start()

        gbuf[me_yc, pl.ds(g * group, group)] = gsrc[pl.ds(g * group, group), me_yc]
        if g == 1:
            sent(qbuf.at[0, 0 : ny - 1, 0], qy_r)
            for d in range(1, nx):
                qx_copy(lax.rem(x + d, nx)).start()

    sent(gbuf.at[0 : nyc - 1], g_r)

    total = nyc * nz * TILE
    got = gbuf[...].reshape(total, 128)
    got = jnp.concatenate([got, jnp.ones((total, 128), jnp.bfloat16)], axis=1)
    in_tile = lax.broadcasted_iota(jnp.int32, (8, 128), 1) & (TILE - 1)
    read = onehot(in_tile > DEAD_SLOT)
    tags = jnp.concatenate(
        [
            jnp.dot(read, got[i * 128 : (i + 1) * 128, :128], preferred_element_type=jnp.float32)[0:1]
            for i in range(total // 128)
        ],
        axis=1,
    )
    name = (lax.broadcasted_iota(jnp.int32, (sub, total), 0) + 128).astype(jnp.float32)

    def x_copy(to, frm):
        return pltpu.make_async_remote_copy(
            src_ref=rs_send.at[to], dst_ref=rs_recv.at[frm], send_sem=x_s, recv_sem=x_r,
            device_id=at(to, y, z, c), device_id_type=MESH,
        )

    def tally(to):
        scale = jnp.float32(1.0)
        for i in range(1, nx):
            scale = jnp.where(to == i, 0.5**i, scale)
        here = tags * scale
        hits = jnp.concatenate([onehot(name == here), onehot(name == here * 0.5**nx)], axis=0)
        both = jnp.dot(hits, got, preferred_element_type=jnp.float32)
        sums, count = both[:, :128], both[:, 128:]
        is_dead = count[sub:] > 0.5
        return jnp.where(is_dead, sums[sub:], sums[:sub]), jnp.where(is_dead, -1.0, count[:sub])

    for d in range(1, nx + 1):
        to = lax.rem(x + d, nx)
        sums, count = tally(to)
        ref = rs_send if d < nx else rs_recv
        ref[to, 0:sub, :] = sums
        ref[to, sub : sub + 8, :] = count.T[0:8]
        if d < nx:
            x_copy(to, x).start()

    sent(qbuf.at[0 : nx - 1, :, 0], qx_r)
    f_copy().start()
    sent(rs_recv.at[0 : nx - 1], x_r)

    count = jnp.zeros((1, 128), jnp.float32)
    dead_row = jnp.zeros((1, 128), jnp.float32)
    sums = jnp.zeros((sub, 128), jnp.float32)
    restart = jnp.zeros((sub, 128), jnp.float32)
    for i in range(nx):
        part = rs_recv[i, sub : sub + 1, :]
        count += jnp.maximum(part, 0.0)
        dead_row = jnp.maximum(dead_row, -part)
        piece = rs_recv[i, 0:sub, :]
        sums += piece
        restart += jnp.where(column(part) < 0.0, piece, 0.0)
    for load in loads[5:]:
        load.wait()
    fresh_row = DECAY * ema_c[pl.ds(x, 1), :] + (1.0 - DECAY) * count
    fresh_row = jnp.where(dead_row > 0.5, 1.0, fresh_row)
    fresh = DECAY * ema_s[...] + (1.0 - DECAY) * sums
    fresh = jnp.where(column(dead_row) > 0.5, restart, fresh)
    rows_out = fresh / column(fresh_row)
    code[0] = (-2.0 * rows_out.astype(jnp.bfloat16).astype(jnp.float32)).astype(jnp.bfloat16)

    def right(t):
        return pltpu.make_async_remote_copy(
            src_ref=code.at[jnp.maximum(2 * t - 1, 0)], dst_ref=code.at[2 * t + 1],
            send_sem=right_s, recv_sem=right_r.at[t], device_id=along_z(1), device_id_type=MESH,
        )

    def left(t):
        return pltpu.make_async_remote_copy(
            src_ref=code.at[2 * t], dst_ref=code.at[2 * t + 2],
            send_sem=left_s, recv_sem=left_r.at[t], device_id=along_z(-1), device_id_type=MESH,
        )

    right(jnp.int32(0)).start()
    left(jnp.int32(0)).start()

    book[mine, :] = rows_out
    cnts[x] = jnp.broadcast_to(fresh_row, (8, 128))

    def b_copy(to, frm):
        span = pl.ds(pl.multiple_of(frm * sub, sub), sub)
        return pltpu.make_async_remote_copy(
            src_ref=book.at[span], dst_ref=book.at[span], send_sem=b_s, recv_sem=b_r,
            device_id=at(to, y, z, c), device_id_type=MESH,
        )

    def c_copy(to, frm):
        return pltpu.make_async_remote_copy(
            src_ref=cnts.at[frm], dst_ref=cnts.at[frm], send_sem=c_s, recv_sem=c_r,
            device_id=at(to, y, z, c), device_id_type=MESH,
        )

    for d in range(1, nx):
        to = lax.rem(x + d, nx)
        b_copy(to, x).start()
        c_copy(to, x).start()

    sent(qbuf.at[:, :, 0], f_r)

    def m_copy(to, frm):
        return pltpu.make_async_remote_copy(
            src_ref=low_send.at[to], dst_ref=low_recv.at[frm], send_sem=m_s, recv_sem=m_r,
            device_id=in_plane(to), device_id_type=MESH,
        )

    halves = queries // 128

    def lowest(p):
        small = jnp.min(acc[p], axis=0, keepdims=True)
        parts = [jnp.broadcast_to(small[:, h * 128 : (h + 1) * 128], (8 // halves, 128)) for h in range(halves)]
        return jnp.concatenate(parts, axis=0)

    steps = nz // 2
    unroll = min(16, planes // 2)

    @pl.loop(0, steps)
    def _(t):
        right(t).wait_recv()

        @pl.when(t < steps - 1)
        def _():
            right(t + 1).start()
            left(t).wait_recv()

        @pl.when(t < steps - 2)
        def _():
            left(t + 1).start()

        wide_table = code[pl.ds(2 * t, 2)].reshape(2 * sub, 128).astype(jnp.float32)
        norm[...] = jnp.broadcast_to(0.25 * jnp.sum(wide_table * wide_table, axis=1, keepdims=True), (2 * sub, 128))

        @pl.loop(0, planes // unroll)
        def _(o):
            for i in range(unroll):
                p = lax.rem(me_p + 1 + o * unroll + i, planes)
                score = jnp.dot(
                    code[pl.ds(2 * t, 2)].reshape(2 * sub, 128), qbuf[lax.div(p, nyc), lax.rem(lax.div(p, CORES), ny), lax.rem(p, CORES)], preferred_element_type=jnp.float32
                )
                lows = [
                    jnp.min((norm[...] + score[:, h * 128 : (h + 1) * 128]).reshape(2 * sub // 8, 8, 128), axis=0)
                    for h in range(halves)
                ]
                acc[p] = jnp.minimum(acc[p], jnp.concatenate(lows, axis=1))

            @pl.when(t == steps - 1)
            def _():
                @pl.loop(o * unroll, jnp.minimum((o + 1) * unroll, planes - 1))
                def _(i):
                    to = lax.rem(me_p + 1 + i, planes)
                    low_send[to] = lowest(to)
                    m_copy(to, me_p).start()

    low_recv[me_p] = lowest(me_p)

    sent(low_recv.at[0 : planes - 1], m_r)

    best = jnp.min(low_recv[...], axis=0)
    for h in range(halves):
        first = h * (8 // halves)
        dist[h : h + 1, :] = (best[first : first + 1] + query_norm[:, h * 128 : (h + 1) * 128]) / 128

    sent(book.at[0 : (nx - 1) * sub], b_r)
    sent(cnts.at[0 : nx - 1], c_r)
    for i in range(nx):
        cnt_out[i : i + 1, :] = cnts[i, 0:1, :]

    sent(pack.at[0 : nz - 1], z_s)
    sent(relay, relay_s)
    sent(qbuf.at[0, 0 : ny - 1, 0], qy_s)
    sent(qbuf.at[0 : nx - 1, :, 0], qx_s)
    sent(qbuf.at[:, :, 0], f_s)
    sent(gsrc.at[:, 0 : nyc - 1], g_s)
    sent(rs_send.at[0 : nx - 1], x_s)
    sent(book.at[0 : (nx - 1) * sub], b_s)
    sent(cnts.at[0 : nx - 1], c_s)
    sent(code.at[0:steps], right_s)
    sent(code.at[0 : steps - 1], left_s)
    sent(low_send.at[0 : planes - 1], m_s)


def per_device(nx, ny, nz, latents, code_ids, ema_sums, ema_counts, dead_codes, restart_index, next_latents):
    k_dev = ema_sums.shape[0]
    sub = k_dev // nx
    nyc = ny * CORES
    planes = nx * nyc
    queries = next_latents.shape[0]
    hbm = pl.BlockSpec(memory_space=pl.ANY)
    vmem = pl.BlockSpec(memory_space=pltpu.VMEM)
    dma = pltpu.SemaphoreType.DMA
    bf16, f32 = jnp.bfloat16, jnp.float32
    book, counts, dist = pl.pallas_call(
        functools.partial(body, nx, ny, nz),
        out_shape=(
            jax.ShapeDtypeStruct((k_dev, 128), f32),
            jax.ShapeDtypeStruct((nx, sub), f32),
            jax.ShapeDtypeStruct((queries // 128, 128), f32),
        ),
        in_specs=[hbm] * 7,
        out_specs=(vmem,) * 3,
        scratch_shapes=[
            pltpu.VMEM(latents.shape, bf16),
            pltpu.VMEM((1, code_ids.shape[0]), jnp.int32),
            pltpu.VMEM((1, dead_codes.shape[0]), jnp.int32),
            pltpu.VMEM((1, dead_codes.shape[0]), jnp.int32),
            pltpu.VMEM((sub, 128), f32),
            pltpu.VMEM((nx, sub), f32),
            pltpu.VMEM((queries, 128), bf16),
            pltpu.VMEM((128, queries), bf16),
            pltpu.VMEM((nz, nyc * USED, 128), bf16),
            pltpu.VMEM((nz, nyc * USED, 128), bf16),
            pltpu.VMEM((nyc * USED, 128), bf16),
            pltpu.VMEM((nz, nyc, TILE, 128), bf16),
            pltpu.VMEM((nyc, nz, TILE, 128), bf16),
            pltpu.VMEM((nx, ny, CORES, 128, queries), bf16),
            pltpu.VMEM((8, 128), jnp.int32),
            pltpu.VMEM((nx, sub + 8, 128), f32),
            pltpu.VMEM((nx, sub + 8, 128), f32),
            pltpu.VMEM((nz, sub, 128), bf16),
            pltpu.VMEM((2 * sub, 128), f32),
            pltpu.VMEM((planes, 8, queries), f32),
            pltpu.VMEM((planes, 8, 128), f32),
            pltpu.VMEM((planes, 8, 128), f32),
            pltpu.VMEM((nx, 8, 128), f32),
            dma((7,)),
            dma, dma((4,)), dma, dma,
            dma, dma,
            dma, dma, dma, dma, dma, dma,
            dma, dma, dma, dma, dma, dma,
            dma, dma((nz // 2,)), dma, dma((nz // 2,)),
            dma, dma,
        ],
        compiler_params=pltpu.CompilerParams(
            collective_id=0, has_side_effects=True, vmem_limit_bytes=56 * 1024 * 1024
        ),
    )(
        latents, code_ids.reshape(1, -1), dead_codes.reshape(1, -1), restart_index.reshape(1, -1),
        ema_sums, ema_counts.reshape(nx, sub), next_latents,
    )
    return book, counts.reshape(-1), dist.reshape(-1)


def solution(mesh, ny=4):
    nx = mesh.shape["dp"]
    nz = mesh.shape["code"] // (CORES * ny)
    in_specs = (
        P(("dp", "code"), None),
        P(("dp", "code")),
        P("code", None),
        P("code"),
        P(("dp", "code")),
        P(("dp", "code")),
        P(("dp", "code"), None),
    )
    reorder = functools.partial(per_device, nx, ny, nz)
    return jax.shard_map(
        lambda a, b, s, n, d, r, q: reorder(a, b, s, n, d, r, q),
        mesh=mesh,
        in_specs=in_specs,
        out_specs=(P("code", None), P("code"), P(("dp", "code"))),
        check_vma=False,
    )
```

```python
import functools

import jax
import jax.numpy as jnp
from jax import lax
from jax.experimental import pallas as pl
from jax.experimental.pallas import tpu as pltpu
from jax.sharding import PartitionSpec as P

MESH = pl.DeviceIdType.MESH
DECAY = 0.8
TILE = 16
USED = 14
DEAD_SLOT = 12
CORES = 2
BIG = 3.0e38


def onehot(mask):
    return jnp.where(mask, 1.0, 0.0).astype(jnp.bfloat16)


def column(row):
    return jnp.broadcast_to(row, (128, 128)).T


def body(
    nx, ny, nz, lat_in, ids_in, dead_in, ridx_in, ema_s_in, ema_c_in, nxt_in, book, cnt_out, dist,
    lat, ids, dead, ridx, ema_s, ema_c, nxt, turned,
    pack, zbuf, relay, gsrc, gbuf, qbuf, ext, parts, rs_send, rs_recv, code, norm, acc, low_send, low_recv, cnts, in_s,
    z_s, z_r, relay_s, relay_r, g_s, g_r, qy_s, qy_r, qx_s, qx_r, f_s, f_r, x_s, x_r, b_s, b_r, c_s, c_r,
    right_s, right_r, left_s, left_r, m_s, m_r,
):
    rows = lat.shape[0]
    k_dev = book.shape[0]
    sub = k_dev // nx
    queries = nxt.shape[0]
    nyc = ny * CORES
    planes = nx * nyc
    group = nz // 4
    block = nyc * USED
    shift_k = k_dev.bit_length() - 1
    shift_z = nz.bit_length() - 1

    x = lax.axis_index("dp")
    me = lax.axis_index("code")
    c = lax.rem(me, CORES)
    z = lax.rem(lax.div(me, CORES), nz)
    y = lax.div(me, CORES * nz)
    me_yc = y * CORES + c
    me_p = x * nyc + me_yc

    def at(ax, ay, az, ac):
        return (ax, (ay * nz + az) * CORES + ac)

    def in_plane(p):
        yc = lax.rem(p, nyc)
        return at(lax.div(p, nyc), lax.div(yc, CORES), z, lax.rem(yc, CORES))

    def sent(ref, sem):
        pltpu.make_async_copy(ref, ref, sem).wait()

    def along_z(d):
        return at(x, y, lax.rem(z + d + nz, nz), c)

    mine = pl.ds(pl.multiple_of(x * sub, sub), sub)
    sources = (lat_in, ids_in, dead_in, ridx_in, nxt_in, ema_c_in, ema_s_in.at[mine])
    loads = [
        pltpu.make_async_copy(src, dst, in_s.at[i])
        for i, (src, dst) in enumerate(zip(sources, (lat, ids, dead, ridx, nxt, ema_c, ema_s)))
    ]
    for load in loads:
        load.start()

    barrier = pltpu.get_barrier_semaphore()

    @pl.loop(1, planes)
    def _(d):
        pl.semaphore_signal(barrier, inc=1, device_id=in_plane(lax.rem(me_p + d, planes)), device_id_type=MESH)

    @pl.loop(1, nz)
    def _(d):
        pl.semaphore_signal(barrier, inc=1, device_id=along_z(d), device_id_type=MESH)

    for load in loads[:4]:
        load.wait()
    lanes = rows + 128
    own = ids[...]

    def place(labels):
        owner = labels >> shift_k
        oc, oz, oy = owner & 1, (owner >> 1) & (nz - 1), owner >> (1 + shift_z)
        return oz * nyc + oy * CORES + oc

    owner = place(own)
    match = lax.broadcasted_iota(jnp.int32, (nyc * nz, rows), 0) == owner
    before = lax.broadcasted_iota(jnp.int32, (rows, rows), 0) < lax.broadcasted_iota(jnp.int32, (rows, rows), 1)
    earlier = jnp.dot(onehot(match), onehot(before), preferred_element_type=jnp.float32)
    rank = jnp.sum(jnp.where(match, earlier, 0.0), axis=0, keepdims=True).astype(jnp.int32)

    ext[...] = jnp.full(ext.shape, -1, jnp.int32)
    ext[0:1, 0 : dead.shape[1]] = dead[...]
    ext[1:2, 0 : dead.shape[1]] = ridx[...]
    gone = ext[0:1, :]
    gone_owner = jnp.where(gone >= 0, place(gone), -1024)
    pick = column(ext[1:2, :].astype(jnp.float32)).astype(jnp.int32)
    lane = lax.broadcasted_iota(jnp.int32, (128, 128), 1)
    picks = jnp.concatenate([onehot(pick == lane + 128 * i) for i in range(rows // 128)], axis=1)
    restarts = jnp.dot(picks, lat[...], preferred_element_type=jnp.float32).astype(jnp.bfloat16)

    all_owner = jnp.concatenate([owner, gone_owner], axis=1)
    slot = jnp.concatenate([rank, jnp.full((1, 128), DEAD_SLOT, jnp.int32)], axis=1)
    tag = jnp.concatenate([own & (k_dev - 1), (gone & (k_dev - 1)) + k_dev], axis=1)
    tag = jnp.left_shift(128 + (tag & 127), tag >> 7).astype(jnp.float32)
    local = all_owner & (nyc - 1)
    goal = all_owner >> (nyc.bit_length() - 1)
    key = local * (USED - 1) + slot
    tag_key = local + nyc * (USED - 1)
    spot = jnp.where((lax.broadcasted_iota(jnp.int32, (128, lanes), 0) & (TILE - 1)) == slot, 1.0, 0.0)
    spot = jnp.concatenate([spot[:, i * 128 : (i + 1) * 128].T for i in range(lanes // 128)], axis=0)
    data = jnp.concatenate([jnp.concatenate([lat[...], restarts], axis=0), spot.astype(jnp.bfloat16)], axis=1)
    line = lax.broadcasted_iota(jnp.int32, (block, lanes), 0)
    lane_tile = lax.broadcasted_iota(jnp.int32, (1, 128), 1) >> 4

    half = nz // 2
    way = 1 - 2 * c

    def offset(k):
        return jnp.where(lax.rem(k, 2) == 1, half - lax.div(k + 1, 2), nz - half + lax.div(k, 2))

    def packed(k):
        to = goal == lax.rem(z + offset(k), nz)
        put = jnp.where(line == jnp.where(to, key, -1), 1.0, jnp.where(line == jnp.where(to, tag_key, -1), tag, 0.0))
        moved = jnp.dot(put.astype(jnp.bfloat16), data, preferred_element_type=jnp.float32)
        here = lax.rem(me_yc * group + lax.rem(k, group), 8)
        tags = jnp.where(lane_tile == here, moved[:, 128:], 0.0)
        is_tag = lax.broadcasted_iota(jnp.int32, (block, 128), 0) >= nyc * (USED - 1)
        return jnp.where(is_tag, tags, moved[:, :128]).astype(jnp.bfloat16)

    def z_copy(k):
        return pltpu.make_async_remote_copy(
            src_ref=pack.at[k], dst_ref=zbuf.at[k], send_sem=z_s, recv_sem=z_r.at[lax.div(k, group)],
            device_id=along_z(offset(k)), device_id_type=MESH,
        )

    def relay_in():
        return pltpu.make_async_remote_copy(
            src_ref=pack.at[0], dst_ref=relay, send_sem=z_s, recv_sem=relay_r,
            device_id=along_z(way), device_id_type=MESH,
        )

    def relay_out():
        return pltpu.make_async_remote_copy(
            src_ref=relay, dst_ref=zbuf.at[0], send_sem=relay_s, recv_sem=z_r.at[0],
            device_id=along_z(way * (half - 1)), device_id_type=MESH,
        )

    pack[0] = packed(jnp.int32(0))
    pl.semaphore_wait(barrier, planes - 1 + nz - 1)
    relay_in().start()

    @pl.loop(0, half - 1)
    def _(o):
        for i in range(2):
            k = 1 + o * 2 + i
            pack[k] = packed(k)
            z_copy(k).start()

        @pl.when(o == (half - 1) // 2)
        def _():
            relay_in().wait_recv()
            relay_out().start()

    zbuf[nz - 1] = packed(jnp.int32(nz - 1))

    loads[4].wait()
    wide = nxt[...].astype(jnp.float32)
    query_norm = jnp.sum((wide * wide).T, axis=0, keepdims=True)
    turned[...] = wide.T.astype(jnp.bfloat16)

    def qy_copy(to):
        return pltpu.make_async_remote_copy(
            src_ref=turned, dst_ref=qbuf.at[x, y, c], send_sem=qy_s, recv_sem=qy_r,
            device_id=at(x, to, z, c), device_id_type=MESH,
        )

    def qx_copy(to):
        return pltpu.make_async_remote_copy(
            src_ref=qbuf.at[x, :, c], dst_ref=qbuf.at[x, :, c], send_sem=qx_s, recv_sem=qx_r,
            device_id=at(to, y, z, c), device_id_type=MESH,
        )

    def f_copy():
        return pltpu.make_async_remote_copy(
            src_ref=qbuf.at[:, :, c], dst_ref=qbuf.at[:, :, c], send_sem=f_s, recv_sem=f_r,
            device_id=at(x, y, z, 1 - c), device_id_type=MESH,
        )

    for d in range(1, ny):
        qy_copy(lax.rem(y + d, ny)).start()
    qbuf[x, y, c] = turned[...]
    acc[...] = jnp.full(acc.shape, BIG, jnp.float32)

    def g_copy(g, j):
        return pltpu.make_async_remote_copy(
            src_ref=gsrc.at[pl.ds(g * group, group), j],
            dst_ref=gbuf.at[me_yc, pl.ds(g * group, group)],
            send_sem=g_s, recv_sem=g_r.at[g],
            device_id=at(x, lax.div(j, CORES), z, lax.rem(j, CORES)), device_id_type=MESH,
        )

    row = lax.broadcasted_iota(jnp.int32, (nyc * TILE, block), 0)
    tile, spare = row >> 4, (row & (TILE - 1)) - DEAD_SLOT
    origin = jnp.where(spare <= 0, tile * (USED - 1) + DEAD_SLOT + spare, jnp.where(spare == 1, tile + nyc * (USED - 1), -1))
    spread = onehot(lax.broadcasted_iota(jnp.int32, (nyc * TILE, block), 1) == origin)

    total = nyc * group * TILE
    in_tile = lax.broadcasted_iota(jnp.int32, (8, 128), 1) & (TILE - 1)
    read = onehot(in_tile > DEAD_SLOT)
    name = (lax.broadcasted_iota(jnp.int32, (sub, total), 0) + 128).astype(jnp.float32)

    def arrived(g):
        sent(gbuf.at[0 : nyc - 1, pl.ds(g * group, group)], g_r.at[g])
        got = gbuf[:, pl.ds(g * group, group)].reshape(total, 128)
        tags = [
            jnp.dot(read, got[i * 128 : (i + 1) * 128], preferred_element_type=jnp.float32)[0:1]
            for i in range(total // 128)
        ]
        return jnp.concatenate(tags, axis=1), jnp.concatenate([got, jnp.ones((total, 128), jnp.bfloat16)], axis=1)

    def tally(tags, got, scale):
        here = tags * scale
        hits = jnp.concatenate([onehot(name == here), onehot(name == here * 0.5**nx)], axis=0)
        return jnp.dot(hits, got, preferred_element_type=jnp.float32)

    for g in range(4):
        here = pl.ds(g * group, min(group, nz - 1 - g * group))
        sent(zbuf.at[here], z_r.at[g])
        for k in range(g * group, (g + 1) * group):
            tiles = jnp.dot(spread, zbuf[k], preferred_element_type=jnp.float32)
            gsrc[k] = tiles.astype(jnp.bfloat16).reshape(nyc, TILE, 128)

        @pl.loop(1, nyc)
        def _(d):
            g_copy(g, lax.rem(me_yc + d, nyc)).start()

        gbuf[me_yc, pl.ds(g * group, group)] = gsrc[pl.ds(g * group, group), me_yc]
        if g > 0:
            tags, got = arrived(g - 1)
            for i in range(nx):
                part = tally(tags, got, 0.5**i)
                parts[i] = part if g == 1 else parts[i] + part
        if g == 1:
            sent(qbuf.at[0, 0 : ny - 1, 0], qy_r)
            for d in range(1, nx):
                qx_copy(lax.rem(x + d, nx)).start()

    def x_copy(to, frm):
        return pltpu.make_async_remote_copy(
            src_ref=rs_send.at[to], dst_ref=rs_recv.at[frm], send_sem=x_s, recv_sem=x_r,
            device_id=at(to, y, z, c), device_id_type=MESH,
        )

    tags, got = arrived(3)
    for d in range(1, nx + 1):
        to = lax.rem(x + d, nx)
        scale = jnp.float32(1.0)
        for i in range(1, nx):
            scale = jnp.where(to == i, 0.5**i, scale)
        both = parts[to] + tally(tags, got, scale)
        sums, count = both[:, :128], both[:, 128:]
        is_dead = count[sub:] > 0.5
        ref = rs_send if d < nx else rs_recv
        ref[to, 0:sub, :] = jnp.where(is_dead, sums[sub:], sums[:sub])
        ref[to, sub : sub + 8, :] = jnp.where(is_dead, -1.0, count[:sub]).T[0:8]
        if d < nx:
            x_copy(to, x).start()

    sent(qbuf.at[0 : nx - 1, :, 0], qx_r)
    f_copy().start()
    sent(rs_recv.at[0 : nx - 1], x_r)

    count = jnp.zeros((1, 128), jnp.float32)
    dead_row = jnp.zeros((1, 128), jnp.float32)
    sums = jnp.zeros((sub, 128), jnp.float32)
    restart = jnp.zeros((sub, 128), jnp.float32)
    for i in range(nx):
        part = rs_recv[i, sub : sub + 1, :]
        count += jnp.maximum(part, 0.0)
        dead_row = jnp.maximum(dead_row, -part)
        piece = rs_recv[i, 0:sub, :]
        sums += piece
        restart += jnp.where(column(part) < 0.0, piece, 0.0)
    for load in loads[5:]:
        load.wait()
    fresh_row = DECAY * ema_c[pl.ds(x, 1), :] + (1.0 - DECAY) * count
    fresh_row = jnp.where(dead_row > 0.5, 1.0, fresh_row)
    fresh = DECAY * ema_s[...] + (1.0 - DECAY) * sums
    fresh = jnp.where(column(dead_row) > 0.5, restart, fresh)
    rows_out = fresh / column(fresh_row)
    code[0] = (-2.0 * rows_out.astype(jnp.bfloat16).astype(jnp.float32)).astype(jnp.bfloat16)

    rounds = nz // 4

    def right(r, j):
        return pltpu.make_async_remote_copy(
            src_ref=code.at[jnp.maximum(4 * r - 2, 0)], dst_ref=code.at[4 * r + j],
            send_sem=right_s, recv_sem=right_r.at[r], device_id=along_z(j), device_id_type=MESH,
        )

    def left(r, j):
        return pltpu.make_async_remote_copy(
            src_ref=code.at[4 * r], dst_ref=code.at[4 * r + 2 + j],
            send_sem=left_s, recv_sem=left_r.at[r], device_id=along_z(-j), device_id_type=MESH,
        )

    right(jnp.int32(0), 2).start()
    left(jnp.int32(0), 2).start()
    right(jnp.int32(0), 1).start()
    left(jnp.int32(0), 1).start()

    book[mine, :] = rows_out
    cnts[x] = jnp.broadcast_to(fresh_row, (8, 128))

    def b_copy(to, frm):
        span = pl.ds(pl.multiple_of(frm * sub, sub), sub)
        return pltpu.make_async_remote_copy(
            src_ref=book.at[span], dst_ref=book.at[span], send_sem=b_s, recv_sem=b_r,
            device_id=at(to, y, z, c), device_id_type=MESH,
        )

    def c_copy(to, frm):
        return pltpu.make_async_remote_copy(
            src_ref=cnts.at[frm], dst_ref=cnts.at[frm], send_sem=c_s, recv_sem=c_r,
            device_id=at(to, y, z, c), device_id_type=MESH,
        )

    for d in range(1, nx):
        to = lax.rem(x + d, nx)
        b_copy(to, x).start()
        c_copy(to, x).start()

    sent(qbuf.at[:, :, 0], f_r)

    def m_copy(to, frm):
        return pltpu.make_async_remote_copy(
            src_ref=low_send.at[to], dst_ref=low_recv.at[frm], send_sem=m_s, recv_sem=m_r,
            device_id=in_plane(to), device_id_type=MESH,
        )

    halves = queries // 128

    def lowest(p):
        small = jnp.min(acc[p], axis=0, keepdims=True)
        parts = [jnp.broadcast_to(small[:, h * 128 : (h + 1) * 128], (8 // halves, 128)) for h in range(halves)]
        return jnp.concatenate(parts, axis=0)

    unroll = min(8, planes // 2)
    deep = 4 * sub

    @pl.loop(0, rounds)
    def _(t):
        sent(code.at[0:2], right_r.at[t])

        @pl.when(t < rounds - 1)
        def _():
            right(t + 1, 2).start()
            sent(code.at[0:2], left_r.at[t])

        @pl.when(t < rounds - 2)
        def _():
            left(t + 1, 2).start()

        @pl.when(t < rounds - 1)
        def _():
            right(t + 1, 1).start()
            left(t + 1, 1).start()

        @pl.when(t == rounds - 1)
        def _():
            sent(code.at[0], left_r.at[t])

        wide_table = code[pl.ds(4 * t, 4)].reshape(deep, 128).astype(jnp.float32)
        norm[...] = jnp.broadcast_to(0.25 * jnp.sum(wide_table * wide_table, axis=1, keepdims=True), (deep, 128))

        @pl.loop(0, planes // unroll)
        def _(o):
            for i in range(unroll):
                p = lax.rem(me_p + 1 + o * unroll + i, planes)
                score = jnp.dot(
                    code[pl.ds(4 * t, 4)].reshape(deep, 128),
                    qbuf[lax.div(p, nyc), lax.rem(lax.div(p, CORES), ny), lax.rem(p, CORES)],
                    preferred_element_type=jnp.float32,
                )
                lows = [
                    jnp.min((norm[...] + score[:, h * 128 : (h + 1) * 128]).reshape(deep // 8, 8, 128), axis=0)
                    for h in range(halves)
                ]
                acc[p] = jnp.minimum(acc[p], jnp.concatenate(lows, axis=1))

            @pl.when(t == rounds - 1)
            def _():
                @pl.loop(o * unroll, jnp.minimum((o + 1) * unroll, planes - 1))
                def _(i):
                    to = lax.rem(me_p + 1 + i, planes)
                    low_send[to] = lowest(to)
                    m_copy(to, me_p).start()

    low_recv[me_p] = lowest(me_p)

    sent(low_recv.at[0 : planes - 1], m_r)

    best = jnp.min(low_recv[...], axis=0)
    for h in range(halves):
        first = h * (8 // halves)
        dist[h : h + 1, :] = (best[first : first + 1] + query_norm[:, h * 128 : (h + 1) * 128]) / 128

    sent(book.at[0 : (nx - 1) * sub], b_r)
    sent(cnts.at[0 : nx - 1], c_r)
    for i in range(nx):
        cnt_out[i : i + 1, :] = cnts[i, 0:1, :]

    sent(pack.at[0 : nz - 1], z_s)
    sent(relay, relay_s)
    sent(qbuf.at[0, 0 : ny - 1, 0], qy_s)
    sent(qbuf.at[0 : nx - 1, :, 0], qx_s)
    sent(qbuf.at[:, :, 0], f_s)
    sent(gsrc.at[:, 0 : nyc - 1], g_s)
    sent(rs_send.at[0 : nx - 1], x_s)
    sent(book.at[0 : (nx - 1) * sub], b_s)
    sent(cnts.at[0 : nx - 1], c_s)
    sent(code.at[0 : 2 * rounds], right_s)
    sent(code.at[0 : 2 * rounds - 1], left_s)
    sent(low_send.at[0 : planes - 1], m_s)


def per_device(nx, ny, nz, latents, code_ids, ema_sums, ema_counts, dead_codes, restart_index, next_latents):
    k_dev = ema_sums.shape[0]
    sub = k_dev // nx
    nyc = ny * CORES
    planes = nx * nyc
    queries = next_latents.shape[0]
    hbm = pl.BlockSpec(memory_space=pl.ANY)
    vmem = pl.BlockSpec(memory_space=pltpu.VMEM)
    dma = pltpu.SemaphoreType.DMA
    bf16, f32 = jnp.bfloat16, jnp.float32
    book, counts, dist = pl.pallas_call(
        functools.partial(body, nx, ny, nz),
        out_shape=(
            jax.ShapeDtypeStruct((k_dev, 128), f32),
            jax.ShapeDtypeStruct((nx, sub), f32),
            jax.ShapeDtypeStruct((queries // 128, 128), f32),
        ),
        in_specs=[hbm] * 7,
        out_specs=(vmem,) * 3,
        scratch_shapes=[
            pltpu.VMEM(latents.shape, bf16),
            pltpu.VMEM((1, code_ids.shape[0]), jnp.int32),
            pltpu.VMEM((1, dead_codes.shape[0]), jnp.int32),
            pltpu.VMEM((1, dead_codes.shape[0]), jnp.int32),
            pltpu.VMEM((sub, 128), f32),
            pltpu.VMEM((nx, sub), f32),
            pltpu.VMEM((queries, 128), bf16),
            pltpu.VMEM((128, queries), bf16),
            pltpu.VMEM((nz, nyc * USED, 128), bf16),
            pltpu.VMEM((nz, nyc * USED, 128), bf16),
            pltpu.VMEM((nyc * USED, 128), bf16),
            pltpu.VMEM((nz, nyc, TILE, 128), bf16),
            pltpu.VMEM((nyc, nz, TILE, 128), bf16),
            pltpu.VMEM((nx, ny, CORES, 128, queries), bf16),
            pltpu.VMEM((8, 128), jnp.int32),
            pltpu.VMEM((nx, 2 * sub, 256), f32),
            pltpu.VMEM((nx, sub + 8, 128), f32),
            pltpu.VMEM((nx, sub + 8, 128), f32),
            pltpu.VMEM((nz, sub, 128), bf16),
            pltpu.VMEM((4 * sub, 128), f32),
            pltpu.VMEM((planes, 8, queries), f32),
            pltpu.VMEM((planes, 8, 128), f32),
            pltpu.VMEM((planes, 8, 128), f32),
            pltpu.VMEM((nx, 8, 128), f32),
            dma((7,)),
            dma, dma((4,)), dma, dma,
            dma, dma((4,)),
            dma, dma, dma, dma, dma, dma,
            dma, dma, dma, dma, dma, dma,
            dma, dma((nz // 4,)), dma, dma((nz // 4,)),
            dma, dma,
        ],
        compiler_params=pltpu.CompilerParams(
            collective_id=0, has_side_effects=True, vmem_limit_bytes=56 * 1024 * 1024
        ),
    )(
        latents, code_ids.reshape(1, -1), dead_codes.reshape(1, -1), restart_index.reshape(1, -1),
        ema_sums, ema_counts.reshape(nx, sub), next_latents,
    )
    return book, counts.reshape(-1), dist.reshape(-1)


def solution(mesh, ny=4):
    nx = mesh.shape["dp"]
    nz = mesh.shape["code"] // (CORES * ny)
    in_specs = (
        P(("dp", "code"), None),
        P(("dp", "code")),
        P("code", None),
        P("code"),
        P(("dp", "code")),
        P(("dp", "code")),
        P(("dp", "code"), None),
    )
    reorder = functools.partial(per_device, nx, ny, nz)
    return jax.shard_map(
        lambda a, b, s, n, d, r, q: reorder(a, b, s, n, d, r, q),
        mesh=mesh,
        in_specs=in_specs,
        out_specs=(P("code", None), P("code"), P(("dp", "code"))),
        check_vma=False,
    )
```

```python
import functools

import jax
import jax.numpy as jnp
from jax import lax
from jax.experimental import pallas as pl
from jax.experimental.pallas import tpu as pltpu
from jax.sharding import PartitionSpec as P

MESH = pl.DeviceIdType.MESH
DECAY = 0.8
TILE = 16
USED = 14
DEAD_SLOT = 12
CORES = 2
BIG = 3.0e38


def onehot(mask):
    return jnp.where(mask, 1.0, 0.0).astype(jnp.bfloat16)


def column(row):
    return jnp.broadcast_to(row, (128, 128)).T


def places(nx, ny, nz):
    x = lax.axis_index("dp")
    me = lax.axis_index("code")
    c = lax.rem(me, CORES)
    z = lax.rem(lax.div(me, CORES), nz)
    y = lax.div(me, CORES * nz)
    nyc = ny * CORES

    def at(ax, ay, az, ac):
        return (ax, (ay * nz + az) * CORES + ac)

    def in_plane(p):
        yc = lax.rem(p, nyc)
        return at(lax.div(p, nyc), lax.div(yc, CORES), z, lax.rem(yc, CORES))

    def along_z(d):
        return at(x, y, lax.rem(z + d + nz, nz), c)

    return x, y, z, c, at, in_plane, along_z


def sent(ref, sem):
    pltpu.make_async_copy(ref, ref, sem).wait()


def meet(devices):
    barrier = pltpu.get_barrier_semaphore()
    count = 0
    for first, last, where in devices:

        @pl.loop(first, last)
        def _(d, where=where):
            pl.semaphore_signal(barrier, inc=1, device_id=where(d), device_id_type=MESH)

        count += last - first
    return lambda: pl.semaphore_wait(barrier, count)


def update(
    nx, ny, nz, lat_in, ids_in, dead_in, ridx_in, ema_s_in, ema_c_in, nxt_in, fresh_out, cnt_out, code_out, qnorm_out, qbuf,
    lat, ids, dead, ridx, ema_s, ema_c, nxt, turned,
    pack, zbuf, relay, gsrc, gbuf, ext, parts, rs_send, rs_recv, in_s,
    z_s, z_r, relay_s, relay_r, g_s, g_r, qy_s, qy_r, qx_s, qx_r, f_s, f_r, x_s, x_r,
):
    rows = lat.shape[0]
    k_dev = ema_s_in.shape[0]
    sub = k_dev // nx
    queries = nxt.shape[0]
    nyc = ny * CORES
    planes = nx * nyc
    group = nz // 4
    block = nyc * USED
    shift_k = k_dev.bit_length() - 1
    shift_z = nz.bit_length() - 1

    x, y, z, c, at, in_plane, along_z = places(nx, ny, nz)
    me_yc = y * CORES + c
    me_p = x * nyc + me_yc

    mine = pl.ds(pl.multiple_of(x * sub, sub), sub)
    sources = (lat_in, ids_in, dead_in, ridx_in, nxt_in, ema_c_in, ema_s_in.at[mine])
    loads = [
        pltpu.make_async_copy(src, dst, in_s.at[i])
        for i, (src, dst) in enumerate(zip(sources, (lat, ids, dead, ridx, nxt, ema_c, ema_s)))
    ]
    for load in loads:
        load.start()

    met = meet(
        [(1, planes, lambda d: in_plane(lax.rem(me_p + d, planes))), (1, nz, along_z)]
    )

    for load in loads[:4]:
        load.wait()
    lanes = rows + 128
    own = ids[...]

    def place(labels):
        owner = labels >> shift_k
        oc, oz, oy = owner & 1, (owner >> 1) & (nz - 1), owner >> (1 + shift_z)
        return oz * nyc + oy * CORES + oc

    owner = place(own)
    match = lax.broadcasted_iota(jnp.int32, (nyc * nz, rows), 0) == owner
    before = lax.broadcasted_iota(jnp.int32, (rows, rows), 0) < lax.broadcasted_iota(jnp.int32, (rows, rows), 1)
    earlier = jnp.dot(onehot(match), onehot(before), preferred_element_type=jnp.float32)
    rank = jnp.sum(jnp.where(match, earlier, 0.0), axis=0, keepdims=True).astype(jnp.int32)

    ext[...] = jnp.full(ext.shape, -1, jnp.int32)
    ext[0:1, 0 : dead.shape[1]] = dead[...]
    ext[1:2, 0 : dead.shape[1]] = ridx[...]
    gone = ext[0:1, :]
    gone_owner = jnp.where(gone >= 0, place(gone), -1024)
    pick = column(ext[1:2, :].astype(jnp.float32)).astype(jnp.int32)
    lane = lax.broadcasted_iota(jnp.int32, (128, 128), 1)
    picks = jnp.concatenate([onehot(pick == lane + 128 * i) for i in range(rows // 128)], axis=1)
    restarts = jnp.dot(picks, lat[...], preferred_element_type=jnp.float32).astype(jnp.bfloat16)

    all_owner = jnp.concatenate([owner, gone_owner], axis=1)
    slot = jnp.concatenate([rank, jnp.full((1, 128), DEAD_SLOT, jnp.int32)], axis=1)
    tag = jnp.concatenate([own & (k_dev - 1), (gone & (k_dev - 1)) + k_dev], axis=1)
    tag = jnp.left_shift(128 + (tag & 127), tag >> 7).astype(jnp.float32)
    local = all_owner & (nyc - 1)
    goal = all_owner >> (nyc.bit_length() - 1)
    key = local * (USED - 1) + slot
    tag_key = local + nyc * (USED - 1)
    spot = jnp.where((lax.broadcasted_iota(jnp.int32, (128, lanes), 0) & (TILE - 1)) == slot, 1.0, 0.0)
    spot = jnp.concatenate([spot[:, i * 128 : (i + 1) * 128].T for i in range(lanes // 128)], axis=0)
    data = jnp.concatenate([jnp.concatenate([lat[...], restarts], axis=0), spot.astype(jnp.bfloat16)], axis=1)
    line = lax.broadcasted_iota(jnp.int32, (block, lanes), 0)
    lane_tile = lax.broadcasted_iota(jnp.int32, (1, 128), 1) >> 4

    half = nz // 2
    way = 1 - 2 * c

    def offset(k):
        return jnp.where(lax.rem(k, 2) == 1, half - lax.div(k + 1, 2), nz - half + lax.div(k, 2))

    def packed(k):
        to = goal == lax.rem(z + offset(k), nz)
        put = jnp.where(line == jnp.where(to, key, -1), 1.0, jnp.where(line == jnp.where(to, tag_key, -1), tag, 0.0))
        moved = jnp.dot(put.astype(jnp.bfloat16), data, preferred_element_type=jnp.float32)
        here = lax.rem(me_yc * group + lax.rem(k, group), 8)
        tags = jnp.where(lane_tile == here, moved[:, 128:], 0.0)
        is_tag = lax.broadcasted_iota(jnp.int32, (block, 128), 0) >= nyc * (USED - 1)
        return jnp.where(is_tag, tags, moved[:, :128]).astype(jnp.bfloat16)

    def z_copy(k):
        return pltpu.make_async_remote_copy(
            src_ref=pack.at[k], dst_ref=zbuf.at[k], send_sem=z_s, recv_sem=z_r.at[lax.div(k, group)],
            device_id=along_z(offset(k)), device_id_type=MESH,
        )

    def relay_in():
        return pltpu.make_async_remote_copy(
            src_ref=pack.at[0], dst_ref=relay, send_sem=z_s, recv_sem=relay_r,
            device_id=along_z(way), device_id_type=MESH,
        )

    def relay_out():
        return pltpu.make_async_remote_copy(
            src_ref=relay, dst_ref=zbuf.at[0], send_sem=relay_s, recv_sem=z_r.at[0],
            device_id=along_z(way * (half - 1)), device_id_type=MESH,
        )

    pack[0] = packed(jnp.int32(0))
    met()
    relay_in().start()

    @pl.loop(0, half - 1)
    def _(o):
        for i in range(2):
            k = 1 + o * 2 + i
            pack[k] = packed(k)
            z_copy(k).start()

        @pl.when(o == (half - 1) // 2)
        def _():
            relay_in().wait_recv()
            relay_out().start()

    zbuf[nz - 1] = packed(jnp.int32(nz - 1))

    loads[4].wait()
    wide = nxt[...].astype(jnp.float32)
    query_norm = jnp.sum((wide * wide).T, axis=0, keepdims=True)
    turned[...] = wide.T.astype(jnp.bfloat16)

    def qy_copy(to):
        return pltpu.make_async_remote_copy(
            src_ref=turned, dst_ref=qbuf.at[x, y, c], send_sem=qy_s, recv_sem=qy_r,
            device_id=at(x, to, z, c), device_id_type=MESH,
        )

    def qx_copy(to):
        return pltpu.make_async_remote_copy(
            src_ref=qbuf.at[x, :, c], dst_ref=qbuf.at[x, :, c], send_sem=qx_s, recv_sem=qx_r,
            device_id=at(to, y, z, c), device_id_type=MESH,
        )

    def f_copy():
        return pltpu.make_async_remote_copy(
            src_ref=qbuf.at[:, :, c], dst_ref=qbuf.at[:, :, c], send_sem=f_s, recv_sem=f_r,
            device_id=at(x, y, z, 1 - c), device_id_type=MESH,
        )

    for d in range(1, ny):
        qy_copy(lax.rem(y + d, ny)).start()
    qbuf[x, y, c] = turned[...]
    qnorm_out[...] = jnp.broadcast_to(query_norm, qnorm_out.shape)

    def g_copy(g, j):
        return pltpu.make_async_remote_copy(
            src_ref=gsrc.at[pl.ds(g * group, group), j],
            dst_ref=gbuf.at[me_yc, pl.ds(g * group, group)],
            send_sem=g_s, recv_sem=g_r.at[g],
            device_id=at(x, lax.div(j, CORES), z, lax.rem(j, CORES)), device_id_type=MESH,
        )

    row = lax.broadcasted_iota(jnp.int32, (nyc * TILE, block), 0)
    tile, spare = row >> 4, (row & (TILE - 1)) - DEAD_SLOT
    origin = jnp.where(spare <= 0, tile * (USED - 1) + DEAD_SLOT + spare, jnp.where(spare == 1, tile + nyc * (USED - 1), -1))
    spread = onehot(lax.broadcasted_iota(jnp.int32, (nyc * TILE, block), 1) == origin)

    total = nyc * group * TILE
    in_tile = lax.broadcasted_iota(jnp.int32, (8, 128), 1) & (TILE - 1)
    read = onehot(in_tile > DEAD_SLOT)
    name = (lax.broadcasted_iota(jnp.int32, (sub, total), 0) + 128).astype(jnp.float32)

    def arrived(g):
        sent(gbuf.at[0 : nyc - 1, pl.ds(g * group, group)], g_r.at[g])
        got = gbuf[:, pl.ds(g * group, group)].reshape(total, 128)
        tags = [
            jnp.dot(read, got[i * 128 : (i + 1) * 128], preferred_element_type=jnp.float32)[0:1]
            for i in range(total // 128)
        ]
        return jnp.concatenate(tags, axis=1), jnp.concatenate([got, jnp.ones((total, 128), jnp.bfloat16)], axis=1)

    def tally(tags, got, scale):
        here = tags * scale
        hits = jnp.concatenate([onehot(name == here), onehot(name == here * 0.5**nx)], axis=0)
        return jnp.dot(hits, got, preferred_element_type=jnp.float32)

    for g in range(4):
        here = pl.ds(g * group, min(group, nz - 1 - g * group))
        sent(zbuf.at[here], z_r.at[g])
        for k in range(g * group, (g + 1) * group):
            tiles = jnp.dot(spread, zbuf[k], preferred_element_type=jnp.float32)
            gsrc[k] = tiles.astype(jnp.bfloat16).reshape(nyc, TILE, 128)

        @pl.loop(1, nyc)
        def _(d):
            g_copy(g, lax.rem(me_yc + d, nyc)).start()

        gbuf[me_yc, pl.ds(g * group, group)] = gsrc[pl.ds(g * group, group), me_yc]
        if g > 0:
            tags, got = arrived(g - 1)
            for i in range(nx):
                part = tally(tags, got, 0.5**i)
                parts[i] = part if g == 1 else parts[i] + part
        if g == 1:
            sent(qbuf.at[0, 0 : ny - 1, 0], qy_r)
            for d in range(1, nx):
                qx_copy(lax.rem(x + d, nx)).start()

    def x_copy(to, frm):
        return pltpu.make_async_remote_copy(
            src_ref=rs_send.at[to], dst_ref=rs_recv.at[frm], send_sem=x_s, recv_sem=x_r,
            device_id=at(to, y, z, c), device_id_type=MESH,
        )

    tags, got = arrived(3)
    for d in range(1, nx + 1):
        to = lax.rem(x + d, nx)
        scale = jnp.float32(1.0)
        for i in range(1, nx):
            scale = jnp.where(to == i, 0.5**i, scale)
        both = parts[to] + tally(tags, got, scale)
        sums, count = both[:, :128], both[:, 128:]
        is_dead = count[sub:] > 0.5
        ref = rs_send if d < nx else rs_recv
        ref[to, 0:sub, :] = jnp.where(is_dead, sums[sub:], sums[:sub])
        ref[to, sub : sub + 8, :] = jnp.where(is_dead, -1.0, count[:sub]).T[0:8]
        if d < nx:
            x_copy(to, x).start()

    sent(qbuf.at[0 : nx - 1, :, 0], qx_r)
    f_copy().start()
    sent(rs_recv.at[0 : nx - 1], x_r)

    count = jnp.zeros((1, 128), jnp.float32)
    dead_row = jnp.zeros((1, 128), jnp.float32)
    sums = jnp.zeros((sub, 128), jnp.float32)
    restart = jnp.zeros((sub, 128), jnp.float32)
    for i in range(nx):
        part = rs_recv[i, sub : sub + 1, :]
        count += jnp.maximum(part, 0.0)
        dead_row = jnp.maximum(dead_row, -part)
        piece = rs_recv[i, 0:sub, :]
        sums += piece
        restart += jnp.where(column(part) < 0.0, piece, 0.0)
    for load in loads[5:]:
        load.wait()
    fresh_row = DECAY * ema_c[pl.ds(x, 1), :] + (1.0 - DECAY) * count
    fresh_row = jnp.where(dead_row > 0.5, 1.0, fresh_row)
    fresh = DECAY * ema_s[...] + (1.0 - DECAY) * sums
    fresh = jnp.where(column(dead_row) > 0.5, restart, fresh)
    rows_out = fresh / column(fresh_row)
    fresh_out[...] = rows_out
    cnt_out[...] = jnp.broadcast_to(fresh_row, (8, 128))
    code_out[...] = (-2.0 * rows_out.astype(jnp.bfloat16).astype(jnp.float32)).astype(jnp.bfloat16)

    sent(qbuf.at[:, :, 0], f_r)

    sent(pack.at[0 : nz - 1], z_s)
    sent(relay, relay_s)
    sent(qbuf.at[0, 0 : ny - 1, 0], qy_s)
    sent(qbuf.at[0 : nx - 1, :, 0], qx_s)
    sent(qbuf.at[:, :, 0], f_s)
    sent(gsrc.at[:, 0 : nyc - 1], g_s)
    sent(rs_send.at[0 : nx - 1], x_s)


def nearest(
    nx, ny, nz, rows_in, cnt_in, own, qnorm, qbuf, book, cnt_out, dist,
    code, norm, acc, low_send, low_recv, cnts,
    b_s, b_r, c_s, c_r, right_s, right_r, left_s, left_r, m_s, m_r,
):
    sub = own.shape[0]
    nyc = ny * CORES
    planes = nx * nyc
    queries = qbuf.shape[-1]
    x, y, z, c, at, in_plane, along_z = places(nx, ny, nz)
    me_p = x * nyc + y * CORES + c
    mine = pl.ds(pl.multiple_of(x * sub, sub), sub)
    met = meet(
        [
            (1, planes, lambda d: in_plane(lax.rem(me_p + d, planes))),
            (1, 3, along_z),
            (1, 3, lambda d: along_z(-d)),
        ]
    )
    code[0] = own[...]
    acc[...] = jnp.full(acc.shape, BIG, jnp.float32)
    book[mine, :] = rows_in[...]
    cnts[x] = cnt_in[...]
    met()

    rounds = nz // 4

    def right(r, j):
        return pltpu.make_async_remote_copy(
            src_ref=code.at[jnp.maximum(4 * r - 2, 0)], dst_ref=code.at[4 * r + j],
            send_sem=right_s, recv_sem=right_r.at[r], device_id=along_z(j), device_id_type=MESH,
        )

    def left(r, j):
        return pltpu.make_async_remote_copy(
            src_ref=code.at[4 * r], dst_ref=code.at[4 * r + 2 + j],
            send_sem=left_s, recv_sem=left_r.at[r], device_id=along_z(-j), device_id_type=MESH,
        )

    right(jnp.int32(0), 2).start()
    left(jnp.int32(0), 2).start()
    right(jnp.int32(0), 1).start()
    left(jnp.int32(0), 1).start()

    def b_copy(to, frm):
        span = pl.ds(pl.multiple_of(frm * sub, sub), sub)
        return pltpu.make_async_remote_copy(
            src_ref=book.at[span], dst_ref=book.at[span], send_sem=b_s, recv_sem=b_r,
            device_id=at(to, y, z, c), device_id_type=MESH,
        )

    def c_copy(to, frm):
        return pltpu.make_async_remote_copy(
            src_ref=cnts.at[frm], dst_ref=cnts.at[frm], send_sem=c_s, recv_sem=c_r,
            device_id=at(to, y, z, c), device_id_type=MESH,
        )

    for d in range(1, nx):
        to = lax.rem(x + d, nx)
        b_copy(to, x).start()
        c_copy(to, x).start()

    def m_copy(to, frm):
        return pltpu.make_async_remote_copy(
            src_ref=low_send.at[to], dst_ref=low_recv.at[frm], send_sem=m_s, recv_sem=m_r,
            device_id=in_plane(to), device_id_type=MESH,
        )

    halves = queries // 128

    def lowest(p):
        small = jnp.min(acc[p], axis=0, keepdims=True)
        parts = [jnp.broadcast_to(small[:, h * 128 : (h + 1) * 128], (8 // halves, 128)) for h in range(halves)]
        return jnp.concatenate(parts, axis=0)

    unroll = min(8, planes // 2)
    deep = 4 * sub

    @pl.loop(0, rounds)
    def _(t):
        sent(code.at[0:2], right_r.at[t])

        @pl.when(t < rounds - 1)
        def _():
            right(t + 1, 2).start()
            sent(code.at[0:2], left_r.at[t])

        @pl.when(t < rounds - 2)
        def _():
            left(t + 1, 2).start()

        @pl.when(t < rounds - 1)
        def _():
            right(t + 1, 1).start()
            left(t + 1, 1).start()

        @pl.when(t == rounds - 1)
        def _():
            sent(code.at[0], left_r.at[t])

        wide_table = code[pl.ds(4 * t, 4)].reshape(deep, 128).astype(jnp.float32)
        norm[...] = jnp.broadcast_to(0.25 * jnp.sum(wide_table * wide_table, axis=1, keepdims=True), (deep, 128))

        @pl.loop(0, planes // unroll)
        def _(o):
            for i in range(unroll):
                p = lax.rem(me_p + 1 + o * unroll + i, planes)
                score = jnp.dot(
                    code[pl.ds(4 * t, 4)].reshape(deep, 128),
                    qbuf[lax.div(p, nyc), lax.rem(lax.div(p, CORES), ny), lax.rem(p, CORES)],
                    preferred_element_type=jnp.float32,
                )
                lows = [
                    jnp.min((norm[...] + score[:, h * 128 : (h + 1) * 128]).reshape(deep // 8, 8, 128), axis=0)
                    for h in range(halves)
                ]
                acc[p] = jnp.minimum(acc[p], jnp.concatenate(lows, axis=1))

            @pl.when(t == rounds - 1)
            def _():
                @pl.loop(o * unroll, jnp.minimum((o + 1) * unroll, planes - 1))
                def _(i):
                    to = lax.rem(me_p + 1 + i, planes)
                    low_send[to] = lowest(to)
                    m_copy(to, me_p).start()

    low_recv[me_p] = lowest(me_p)

    sent(low_recv.at[0 : planes - 1], m_r)

    best = jnp.min(low_recv[...], axis=0)
    for h in range(halves):
        first = h * (8 // halves)
        dist[h : h + 1, :] = (best[first : first + 1] + qnorm[0:1, h * 128 : (h + 1) * 128]) / 128

    sent(book.at[0 : (nx - 1) * sub], b_r)
    sent(cnts.at[0 : nx - 1], c_r)
    for i in range(nx):
        cnt_out[i : i + 1, :] = cnts[i, 0:1, :]

    sent(book.at[0 : (nx - 1) * sub], b_s)
    sent(cnts.at[0 : nx - 1], c_s)
    sent(code.at[0 : 2 * rounds], right_s)
    sent(code.at[0 : 2 * rounds - 1], left_s)
    sent(low_send.at[0 : planes - 1], m_s)


def per_device(nx, ny, nz, latents, code_ids, ema_sums, ema_counts, dead_codes, restart_index, next_latents):
    k_dev = ema_sums.shape[0]
    sub = k_dev // nx
    nyc = ny * CORES
    planes = nx * nyc
    queries = next_latents.shape[0]
    hbm = pl.BlockSpec(memory_space=pl.ANY)
    vmem = pl.BlockSpec(memory_space=pltpu.VMEM)
    dma = pltpu.SemaphoreType.DMA
    bf16, f32 = jnp.bfloat16, jnp.float32
    wide = pltpu.CompilerParams(collective_id=0, has_side_effects=True, vmem_limit_bytes=40 * 1024 * 1024)
    rows_out, counts, own, qnorm, qbuf = pl.pallas_call(
        functools.partial(update, nx, ny, nz),
        out_shape=(
            jax.ShapeDtypeStruct((sub, 128), f32),
            jax.ShapeDtypeStruct((8, sub), f32),
            jax.ShapeDtypeStruct((sub, 128), bf16),
            jax.ShapeDtypeStruct((8, queries), f32),
            jax.ShapeDtypeStruct((nx, ny, CORES, 128, queries), bf16),
        ),
        in_specs=[hbm] * 7,
        out_specs=(vmem,) * 5,
        scratch_shapes=[
            pltpu.VMEM(latents.shape, bf16),
            pltpu.VMEM((1, code_ids.shape[0]), jnp.int32),
            pltpu.VMEM((1, dead_codes.shape[0]), jnp.int32),
            pltpu.VMEM((1, dead_codes.shape[0]), jnp.int32),
            pltpu.VMEM((sub, 128), f32),
            pltpu.VMEM((nx, sub), f32),
            pltpu.VMEM((queries, 128), bf16),
            pltpu.VMEM((128, queries), bf16),
            pltpu.VMEM((nz, nyc * USED, 128), bf16),
            pltpu.VMEM((nz, nyc * USED, 128), bf16),
            pltpu.VMEM((nyc * USED, 128), bf16),
            pltpu.VMEM((nz, nyc, TILE, 128), bf16),
            pltpu.VMEM((nyc, nz, TILE, 128), bf16),
            pltpu.VMEM((8, 128), jnp.int32),
            pltpu.VMEM((nx, 2 * sub, 256), f32),
            pltpu.VMEM((nx, sub + 8, 128), f32),
            pltpu.VMEM((nx, sub + 8, 128), f32),
            dma((7,)),
            dma, dma((4,)), dma, dma,
            dma, dma((4,)),
            dma, dma, dma, dma, dma, dma,
            dma, dma,
        ],
        compiler_params=wide,
    )(
        latents, code_ids.reshape(1, -1), dead_codes.reshape(1, -1), restart_index.reshape(1, -1),
        ema_sums, ema_counts.reshape(nx, sub), next_latents,
    )
    book, counts, dist = pl.pallas_call(
        functools.partial(nearest, nx, ny, nz),
        out_shape=(
            jax.ShapeDtypeStruct((k_dev, 128), f32),
            jax.ShapeDtypeStruct((nx, sub), f32),
            jax.ShapeDtypeStruct((queries // 128, 128), f32),
        ),
        in_specs=[vmem] * 5,
        out_specs=(vmem,) * 3,
        scratch_shapes=[
            pltpu.VMEM((nz, sub, 128), bf16),
            pltpu.VMEM((4 * sub, 128), f32),
            pltpu.VMEM((planes, 8, queries), f32),
            pltpu.VMEM((planes, 8, 128), f32),
            pltpu.VMEM((planes, 8, 128), f32),
            pltpu.VMEM((nx, 8, 128), f32),
            dma, dma, dma, dma,
            dma, dma((nz // 4,)), dma, dma((nz // 4,)),
            dma, dma,
        ],
        compiler_params=pltpu.CompilerParams(
            collective_id=1, has_side_effects=True, vmem_limit_bytes=40 * 1024 * 1024
        ),
    )(rows_out, counts, own, qnorm, qbuf)
    return book, counts.reshape(-1), dist.reshape(-1)


def solution(mesh, ny=4):
    nx = mesh.shape["dp"]
    nz = mesh.shape["code"] // (CORES * ny)
    in_specs = (
        P(("dp", "code"), None),
        P(("dp", "code")),
        P("code", None),
        P("code"),
        P(("dp", "code")),
        P(("dp", "code")),
        P(("dp", "code"), None),
    )
    reorder = functools.partial(per_device, nx, ny, nz)
    return jax.shard_map(
        lambda a, b, s, n, d, r, q: reorder(a, b, s, n, d, r, q),
        mesh=mesh,
        in_specs=in_specs,
        out_specs=(P("code", None), P("code"), P(("dp", "code"))),
        check_vma=False,
    )
```

```python
import functools

import jax
import jax.numpy as jnp
from jax import lax
from jax.experimental import pallas as pl
from jax.experimental.pallas import tpu as pltpu
from jax.sharding import PartitionSpec as P

MESH = pl.DeviceIdType.MESH
DECAY = 0.8
TILE = 16
USED = 14
DEAD_SLOT = 12
CORES = 2
BIG = 3.0e38


def onehot(mask):
    return jnp.where(mask, 1.0, 0.0).astype(jnp.bfloat16)


def column(row):
    return jnp.broadcast_to(row, (128, 128)).T


def body(
    nx, ny, nz, lat_in, ids_in, dead_in, ridx_in, ema_s_in, ema_c_in, nxt_in, book, cnt_out, dist,
    lat, ids, dead, ridx, ema_s, ema_c, nxt, turned,
    pack, zbuf, relay, gsrc, gbuf, qbuf, ext, parts, rs_send, rs_recv, code, norm, acc, low_send, low_recv, cnts, in_s,
    z_s, z_r, relay_s, relay_r, g_s, g_r, q1_s, q1_r, q2_s, q2_r, q3_s, q3_r, f_s, f_r, x_s, x_r, b_s, b_r, c_s, c_r,
    right_s, right_r, left_s, left_r, m_s, m_r,
):
    rows = lat.shape[0]
    k_dev = book.shape[0]
    sub = k_dev // nx
    queries = nxt.shape[0]
    nyc = ny * CORES
    planes = nx * nyc
    group = nz // 4
    block = nyc * USED
    shift_k = k_dev.bit_length() - 1
    shift_z = nz.bit_length() - 1

    x = lax.axis_index("dp")
    me = lax.axis_index("code")
    c = lax.rem(me, CORES)
    z = lax.rem(lax.div(me, CORES), nz)
    y = lax.div(me, CORES * nz)
    me_yc = y * CORES + c
    me_p = x * nyc + me_yc

    def at(ax, ay, az, ac):
        return (ax, (ay * nz + az) * CORES + ac)

    def in_plane(p):
        yc = lax.rem(p, nyc)
        return at(lax.div(p, nyc), lax.div(yc, CORES), z, lax.rem(yc, CORES))

    def sent(ref, sem):
        pltpu.make_async_copy(ref, ref, sem).wait()

    def along_z(d):
        return at(x, y, lax.rem(z + d + nz, nz), c)

    mine = pl.ds(pl.multiple_of(x * sub, sub), sub)
    sources = (lat_in, ids_in, dead_in, ridx_in, nxt_in, ema_c_in, ema_s_in.at[mine])
    loads = [
        pltpu.make_async_copy(src, dst, in_s.at[i])
        for i, (src, dst) in enumerate(zip(sources, (lat, ids, dead, ridx, nxt, ema_c, ema_s)))
    ]
    for load in loads:
        load.start()

    barrier = pltpu.get_barrier_semaphore()

    @pl.loop(1, planes)
    def _(d):
        pl.semaphore_signal(barrier, inc=1, device_id=in_plane(lax.rem(me_p + d, planes)), device_id_type=MESH)

    @pl.loop(1, nz)
    def _(d):
        pl.semaphore_signal(barrier, inc=1, device_id=along_z(d), device_id_type=MESH)

    for load in loads[:4]:
        load.wait()
    lanes = rows + 128
    own = ids[...]

    def place(labels):
        owner = labels >> shift_k
        oc, oz, oy = owner & 1, (owner >> 1) & (nz - 1), owner >> (1 + shift_z)
        return oz * nyc + oy * CORES + oc

    owner = place(own)
    match = lax.broadcasted_iota(jnp.int32, (nyc * nz, rows), 0) == owner
    before = lax.broadcasted_iota(jnp.int32, (rows, rows), 0) < lax.broadcasted_iota(jnp.int32, (rows, rows), 1)
    earlier = jnp.dot(onehot(match), onehot(before), preferred_element_type=jnp.float32)
    rank = jnp.sum(jnp.where(match, earlier, 0.0), axis=0, keepdims=True).astype(jnp.int32)

    ext[...] = jnp.full(ext.shape, -1, jnp.int32)
    ext[0:1, 0 : dead.shape[1]] = dead[...]
    ext[1:2, 0 : dead.shape[1]] = ridx[...]
    gone = ext[0:1, :]
    gone_owner = jnp.where(gone >= 0, place(gone), -1024)
    pick = column(ext[1:2, :].astype(jnp.float32)).astype(jnp.int32)
    lane = lax.broadcasted_iota(jnp.int32, (128, 128), 1)
    picks = jnp.concatenate([onehot(pick == lane + 128 * i) for i in range(rows // 128)], axis=1)
    restarts = jnp.dot(picks, lat[...], preferred_element_type=jnp.float32).astype(jnp.bfloat16)

    all_owner = jnp.concatenate([owner, gone_owner], axis=1)
    slot = jnp.concatenate([rank, jnp.full((1, 128), DEAD_SLOT, jnp.int32)], axis=1)
    tag = jnp.concatenate([own & (k_dev - 1), (gone & (k_dev - 1)) + k_dev], axis=1)
    tag = jnp.left_shift(128 + (tag & 127), tag >> 7).astype(jnp.float32)
    local = all_owner & (nyc - 1)
    goal = all_owner >> (nyc.bit_length() - 1)
    key = local * (USED - 1) + slot
    tag_key = local + nyc * (USED - 1)
    spot = jnp.where((lax.broadcasted_iota(jnp.int32, (128, lanes), 0) & (TILE - 1)) == slot, 1.0, 0.0)
    spot = jnp.concatenate([spot[:, i * 128 : (i + 1) * 128].T for i in range(lanes // 128)], axis=0)
    data = jnp.concatenate([jnp.concatenate([lat[...], restarts], axis=0), spot.astype(jnp.bfloat16)], axis=1)
    line = lax.broadcasted_iota(jnp.int32, (block, lanes), 0)
    lane_tile = lax.broadcasted_iota(jnp.int32, (1, 128), 1) >> 4

    half = nz // 2
    way = 1 - 2 * c

    def offset(k):
        return jnp.where(lax.rem(k, 2) == 1, half - lax.div(k + 1, 2), nz - half + lax.div(k, 2))

    def packed(k):
        to = goal == lax.rem(z + offset(k), nz)
        put = jnp.where(line == jnp.where(to, key, -1), 1.0, jnp.where(line == jnp.where(to, tag_key, -1), tag, 0.0))
        moved = jnp.dot(put.astype(jnp.bfloat16), data, preferred_element_type=jnp.float32)
        here = lax.rem(me_yc * group + lax.rem(k, group), 8)
        tags = jnp.where(lane_tile == here, moved[:, 128:], 0.0)
        is_tag = lax.broadcasted_iota(jnp.int32, (block, 128), 0) >= nyc * (USED - 1)
        return jnp.where(is_tag, tags, moved[:, :128]).astype(jnp.bfloat16)

    def z_copy(k):
        return pltpu.make_async_remote_copy(
            src_ref=pack.at[k], dst_ref=zbuf.at[k], send_sem=z_s, recv_sem=z_r.at[lax.div(k, group)],
            device_id=along_z(offset(k)), device_id_type=MESH,
        )

    def relay_in():
        return pltpu.make_async_remote_copy(
            src_ref=pack.at[0], dst_ref=relay, send_sem=z_s, recv_sem=relay_r,
            device_id=along_z(way), device_id_type=MESH,
        )

    def relay_out():
        return pltpu.make_async_remote_copy(
            src_ref=relay, dst_ref=zbuf.at[0], send_sem=relay_s, recv_sem=z_r.at[0],
            device_id=along_z(way * (half - 1)), device_id_type=MESH,
        )

    def neighbour(axis, d):
        if axis == "x":
            return at(lax.rem(x + d + nx, nx), y, z, c)
        return at(x, lax.rem(y + d + ny, ny), z, c)

    def send(src, dst, sems, device):
        return pltpu.make_async_remote_copy(
            src_ref=src, dst_ref=dst, send_sem=sems[0], recv_sem=sems[1], device_id=device, device_id_type=MESH
        )

    one, two, three = (q1_s, q1_r), (q2_s, q2_r), (q3_s, q3_r)
    cores = ((0, "y", "x"), (1, "x", "y"))

    def queries_one():
        for core, axis, _ in cores:

            @pl.when(c == core)
            def _(core=core, axis=axis):
                for d in range(1, ny):
                    send(turned, qbuf.at[x, y, core], one, neighbour(axis, d)).start()

    def queries_two():
        sent(qbuf.at[0, 0 : ny - 1, 0], q1_r)
        for core, _, axis in cores:

            @pl.when(c == core)
            def _(core=core, axis=axis):
                line_of = qbuf.at[x, :, core] if axis == "x" else qbuf.at[:, y, core]
                send(line_of, line_of, two, neighbour(axis, 1)).start()
                send(line_of, line_of, two, neighbour(axis, -1)).start()

    def queries_three():
        sent(qbuf.at[0:2, :, 0], q2_r)
        for core, _, axis in cores:

            @pl.when(c == core)
            def _(core=core, axis=axis):
                lower, upper = pl.ds(0, ny // 2), pl.ds(ny // 2, ny // 2)
                if axis == "x":
                    before, after = lax.rem(x + nx - 1, nx), lax.rem(x + 1, nx)
                    on, back = qbuf.at[before, lower, core], qbuf.at[after, upper, core]
                else:
                    before, after = lax.rem(y + ny - 1, ny), lax.rem(y + 1, ny)
                    on, back = qbuf.at[lower, before, core], qbuf.at[upper, after, core]
                send(on, on, three, neighbour(axis, 1)).start()
                send(back, back, three, neighbour(axis, -1)).start()

    def queries_across():
        mine_too = qbuf.at[:, :, c]
        return send(mine_too, mine_too, (f_s, f_r), at(x, y, z, 1 - c))

    loads[4].wait()
    wide = nxt[...].astype(jnp.float32)
    query_norm = jnp.sum((wide * wide).T, axis=0, keepdims=True)
    turned[...] = wide.T.astype(jnp.bfloat16)
    qbuf[x, y, c] = turned[...]
    pack[0] = packed(jnp.int32(0))
    pl.semaphore_wait(barrier, planes - 1 + nz - 1)
    relay_in().start()
    queries_one()

    @pl.loop(0, half - 1)
    def _(o):
        for i in range(2):
            k = 1 + o * 2 + i
            pack[k] = packed(k)
            z_copy(k).start()

        @pl.when(o == (half - 1) // 2)
        def _():
            relay_in().wait_recv()
            relay_out().start()

    zbuf[nz - 1] = packed(jnp.int32(nz - 1))
    queries_two()

    acc[...] = jnp.full(acc.shape, BIG, jnp.float32)

    def g_copy(g, j):
        return pltpu.make_async_remote_copy(
            src_ref=gsrc.at[pl.ds(g * group, group), j],
            dst_ref=gbuf.at[me_yc, pl.ds(g * group, group)],
            send_sem=g_s, recv_sem=g_r.at[g],
            device_id=at(x, lax.div(j, CORES), z, lax.rem(j, CORES)), device_id_type=MESH,
        )

    row = lax.broadcasted_iota(jnp.int32, (nyc * TILE, block), 0)
    tile, spare = row >> 4, (row & (TILE - 1)) - DEAD_SLOT
    origin = jnp.where(spare <= 0, tile * (USED - 1) + DEAD_SLOT + spare, jnp.where(spare == 1, tile + nyc * (USED - 1), -1))
    spread = onehot(lax.broadcasted_iota(jnp.int32, (nyc * TILE, block), 1) == origin)

    total = nyc * group * TILE
    in_tile = lax.broadcasted_iota(jnp.int32, (8, 128), 1) & (TILE - 1)
    read = onehot(in_tile > DEAD_SLOT)
    name = (lax.broadcasted_iota(jnp.int32, (sub, total), 0) + 128).astype(jnp.float32)

    def arrived(g):
        sent(gbuf.at[0 : nyc - 1, pl.ds(g * group, group)], g_r.at[g])
        got = gbuf[:, pl.ds(g * group, group)].reshape(total, 128)
        tags = [
            jnp.dot(read, got[i * 128 : (i + 1) * 128], preferred_element_type=jnp.float32)[0:1]
            for i in range(total // 128)
        ]
        return jnp.concatenate(tags, axis=1), jnp.concatenate([got, jnp.ones((total, 128), jnp.bfloat16)], axis=1)

    def tally(tags, got, scale):
        here = tags * scale
        hits = jnp.concatenate([onehot(name == here), onehot(name == here * 0.5**nx)], axis=0)
        return jnp.dot(hits, got, preferred_element_type=jnp.float32)

    for g in range(4):
        here = pl.ds(g * group, min(group, nz - 1 - g * group))
        sent(zbuf.at[here], z_r.at[g])
        for k in range(g * group, (g + 1) * group):
            tiles = jnp.dot(spread, zbuf[k], preferred_element_type=jnp.float32)
            gsrc[k] = tiles.astype(jnp.bfloat16).reshape(nyc, TILE, 128)

        @pl.loop(1, nyc)
        def _(d):
            g_copy(g, lax.rem(me_yc + d, nyc)).start()

        gbuf[me_yc, pl.ds(g * group, group)] = gsrc[pl.ds(g * group, group), me_yc]
        if g > 0:
            tags, got = arrived(g - 1)
            for i in range(nx):
                part = tally(tags, got, 0.5**i)
                parts[i] = part if g == 1 else parts[i] + part
        if g == 0:
            queries_three()
        if g == 1:
            sent(qbuf.at[0, :, 0], q3_r)
            queries_across().start()

    def x_copy(to, frm):
        return pltpu.make_async_remote_copy(
            src_ref=rs_send.at[to], dst_ref=rs_recv.at[frm], send_sem=x_s, recv_sem=x_r,
            device_id=at(to, y, z, c), device_id_type=MESH,
        )

    tags, got = arrived(3)
    for d in range(1, nx + 1):
        to = lax.rem(x + d, nx)
        scale = jnp.float32(1.0)
        for i in range(1, nx):
            scale = jnp.where(to == i, 0.5**i, scale)
        both = parts[to] + tally(tags, got, scale)
        sums, count = both[:, :128], both[:, 128:]
        is_dead = count[sub:] > 0.5
        ref = rs_send if d < nx else rs_recv
        ref[to, 0:sub, :] = jnp.where(is_dead, sums[sub:], sums[:sub])
        ref[to, sub : sub + 8, :] = jnp.where(is_dead, -1.0, count[:sub]).T[0:8]
        if d < nx:
            x_copy(to, x).start()

    sent(rs_recv.at[0 : nx - 1], x_r)

    count = jnp.zeros((1, 128), jnp.float32)
    dead_row = jnp.zeros((1, 128), jnp.float32)
    sums = jnp.zeros((sub, 128), jnp.float32)
    restart = jnp.zeros((sub, 128), jnp.float32)
    for i in range(nx):
        part = rs_recv[i, sub : sub + 1, :]
        count += jnp.maximum(part, 0.0)
        dead_row = jnp.maximum(dead_row, -part)
        piece = rs_recv[i, 0:sub, :]
        sums += piece
        restart += jnp.where(column(part) < 0.0, piece, 0.0)
    for load in loads[5:]:
        load.wait()
    fresh_row = DECAY * ema_c[pl.ds(x, 1), :] + (1.0 - DECAY) * count
    fresh_row = jnp.where(dead_row > 0.5, 1.0, fresh_row)
    fresh = DECAY * ema_s[...] + (1.0 - DECAY) * sums
    fresh = jnp.where(column(dead_row) > 0.5, restart, fresh)
    rows_out = fresh / column(fresh_row)
    code[0] = (-2.0 * rows_out.astype(jnp.bfloat16).astype(jnp.float32)).astype(jnp.bfloat16)

    rounds = nz // 4

    def right(r, j):
        return pltpu.make_async_remote_copy(
            src_ref=code.at[jnp.maximum(4 * r - 2, 0)], dst_ref=code.at[4 * r + j],
            send_sem=right_s, recv_sem=right_r.at[r], device_id=along_z(j), device_id_type=MESH,
        )

    def left(r, j):
        return pltpu.make_async_remote_copy(
            src_ref=code.at[4 * r], dst_ref=code.at[4 * r + 2 + j],
            send_sem=left_s, recv_sem=left_r.at[r], device_id=along_z(-j), device_id_type=MESH,
        )

    right(jnp.int32(0), 2).start()
    if rounds > 1:
        left(jnp.int32(0), 2).start()
    right(jnp.int32(0), 1).start()
    left(jnp.int32(0), 1).start()

    book[mine, :] = rows_out
    cnts[x] = jnp.broadcast_to(fresh_row, (8, 128))

    def b_copy(to, frm):
        span = pl.ds(pl.multiple_of(frm * sub, sub), sub)
        return pltpu.make_async_remote_copy(
            src_ref=book.at[span], dst_ref=book.at[span], send_sem=b_s, recv_sem=b_r,
            device_id=at(to, y, z, c), device_id_type=MESH,
        )

    def c_copy(to, frm):
        return pltpu.make_async_remote_copy(
            src_ref=cnts.at[frm], dst_ref=cnts.at[frm], send_sem=c_s, recv_sem=c_r,
            device_id=at(to, y, z, c), device_id_type=MESH,
        )

    for d in range(1, nx):
        to = lax.rem(x + d, nx)
        b_copy(to, x).start()
        c_copy(to, x).start()

    sent(qbuf.at[:, :, 0], f_r)

    def m_copy(to, frm):
        return pltpu.make_async_remote_copy(
            src_ref=low_send.at[to], dst_ref=low_recv.at[frm], send_sem=m_s, recv_sem=m_r,
            device_id=in_plane(to), device_id_type=MESH,
        )

    halves = queries // 128

    def lowest(p):
        small = jnp.min(acc[p], axis=0, keepdims=True)
        parts_of = [jnp.broadcast_to(small[:, h * 128 : (h + 1) * 128], (8 // halves, 128)) for h in range(halves)]
        return jnp.concatenate(parts_of, axis=0)

    unroll = min(8, planes // 2)
    spread_out = planes // unroll

    def norms(first, count):
        table = code[pl.ds(first, count)].reshape(count * sub, 128).astype(jnp.float32)
        both = 0.25 * jnp.sum(table * table, axis=1, keepdims=True)
        norm[0 : count * sub] = jnp.broadcast_to(both, (count * sub, 128))

    def compare(first, count, o):
        deep = count * sub
        for i in range(unroll):
            p = lax.rem(me_p + 1 + o * unroll + i, planes)
            score = jnp.dot(
                code[pl.ds(first, count)].reshape(deep, 128),
                qbuf[lax.div(p, nyc), lax.rem(lax.div(p, CORES), ny), lax.rem(p, CORES)],
                preferred_element_type=jnp.float32,
            )
            lows = [
                jnp.min((norm[0:deep] + score[:, h * 128 : (h + 1) * 128]).reshape(deep // 8, 8, 128), axis=0)
                for h in range(halves)
            ]
            acc[p] = jnp.minimum(acc[p], jnp.concatenate(lows, axis=1))

    norms(0, 1)

    @pl.loop(0, spread_out)
    def _(o):
        compare(0, 1, o)

    @pl.loop(0, rounds - 1)
    def _(t):
        sent(code.at[0:2], right_r.at[t])
        right(t + 1, 2).start()
        sent(code.at[0:2], left_r.at[t])

        @pl.when(t < rounds - 2)
        def _():
            left(t + 1, 2).start()

        right(t + 1, 1).start()
        left(t + 1, 1).start()
        norms(4 * t + 1, 4)

        @pl.loop(0, spread_out)
        def _(o):
            compare(4 * t + 1, 4, o)

    last = 4 * (rounds - 1) + 1
    sent(code.at[0:2], right_r.at[rounds - 1])
    sent(code.at[0], left_r.at[rounds - 1])
    norms(last, 3)

    @pl.loop(0, spread_out)
    def _(o):
        compare(last, 3, o)

        @pl.loop(o * unroll, jnp.minimum((o + 1) * unroll, planes - 1))
        def _(i):
            to = lax.rem(me_p + 1 + i, planes)
            low_send[to] = lowest(to)
            m_copy(to, me_p).start()

    low_recv[me_p] = lowest(me_p)

    sent(low_recv.at[0 : planes - 1], m_r)

    best = jnp.min(low_recv[...], axis=0)
    for h in range(halves):
        first = h * (8 // halves)
        dist[h : h + 1, :] = (best[first : first + 1] + query_norm[:, h * 128 : (h + 1) * 128]) / 128

    sent(book.at[0 : (nx - 1) * sub], b_r)
    sent(cnts.at[0 : nx - 1], c_r)
    for i in range(nx):
        cnt_out[i : i + 1, :] = cnts[i, 0:1, :]

    sent(pack.at[0 : nz - 1], z_s)
    sent(relay, relay_s)
    sent(qbuf.at[0, 0 : ny - 1, 0], q1_s)
    sent(qbuf.at[0:2, :, 0], q2_s)
    sent(qbuf.at[0, :, 0], q3_s)
    sent(qbuf.at[:, :, 0], f_s)
    sent(gsrc.at[:, 0 : nyc - 1], g_s)
    sent(rs_send.at[0 : nx - 1], x_s)
    sent(book.at[0 : (nx - 1) * sub], b_s)
    sent(cnts.at[0 : nx - 1], c_s)
    sent(code.at[0 : 2 * rounds], right_s)
    sent(code.at[0 : 2 * rounds - 1], left_s)
    sent(low_send.at[0 : planes - 1], m_s)


def per_device(nx, ny, nz, latents, code_ids, ema_sums, ema_counts, dead_codes, restart_index, next_latents):
    k_dev = ema_sums.shape[0]
    sub = k_dev // nx
    nyc = ny * CORES
    planes = nx * nyc
    queries = next_latents.shape[0]
    hbm = pl.BlockSpec(memory_space=pl.ANY)
    vmem = pl.BlockSpec(memory_space=pltpu.VMEM)
    dma = pltpu.SemaphoreType.DMA
    bf16, f32 = jnp.bfloat16, jnp.float32
    book, counts, dist = pl.pallas_call(
        functools.partial(body, nx, ny, nz),
        out_shape=(
            jax.ShapeDtypeStruct((k_dev, 128), f32),
            jax.ShapeDtypeStruct((nx, sub), f32),
            jax.ShapeDtypeStruct((queries // 128, 128), f32),
        ),
        in_specs=[hbm] * 7,
        out_specs=(vmem,) * 3,
        scratch_shapes=[
            pltpu.VMEM(latents.shape, bf16),
            pltpu.VMEM((1, code_ids.shape[0]), jnp.int32),
            pltpu.VMEM((1, dead_codes.shape[0]), jnp.int32),
            pltpu.VMEM((1, dead_codes.shape[0]), jnp.int32),
            pltpu.VMEM((sub, 128), f32),
            pltpu.VMEM((nx, sub), f32),
            pltpu.VMEM((queries, 128), bf16),
            pltpu.VMEM((128, queries), bf16),
            pltpu.VMEM((nz, nyc * USED, 128), bf16),
            pltpu.VMEM((nz, nyc * USED, 128), bf16),
            pltpu.VMEM((nyc * USED, 128), bf16),
            pltpu.VMEM((nz, nyc, TILE, 128), bf16),
            pltpu.VMEM((nyc, nz, TILE, 128), bf16),
            pltpu.VMEM((nx, ny, CORES, 128, queries), bf16),
            pltpu.VMEM((8, 128), jnp.int32),
            pltpu.VMEM((nx, 2 * sub, 256), f32),
            pltpu.VMEM((nx, sub + 8, 128), f32),
            pltpu.VMEM((nx, sub + 8, 128), f32),
            pltpu.VMEM((nz, sub, 128), bf16),
            pltpu.VMEM((4 * sub, 128), f32),
            pltpu.VMEM((planes, 8, queries), f32),
            pltpu.VMEM((planes, 8, 128), f32),
            pltpu.VMEM((planes, 8, 128), f32),
            pltpu.VMEM((nx, 8, 128), f32),
            dma((7,)),
            dma, dma((4,)), dma, dma,
            dma, dma((4,)),
            dma, dma, dma, dma, dma, dma, dma, dma,
            dma, dma, dma, dma, dma, dma,
            dma, dma((nz // 4,)), dma, dma((nz // 4,)),
            dma, dma,
        ],
        compiler_params=pltpu.CompilerParams(
            collective_id=0, has_side_effects=True, vmem_limit_bytes=56 * 1024 * 1024
        ),
    )(
        latents, code_ids.reshape(1, -1), dead_codes.reshape(1, -1), restart_index.reshape(1, -1),
        ema_sums, ema_counts.reshape(nx, sub), next_latents,
    )
    return book, counts.reshape(-1), dist.reshape(-1)


def solution(mesh, ny=4):
    nx = mesh.shape["dp"]
    nz = mesh.shape["code"] // (CORES * ny)
    in_specs = (
        P(("dp", "code"), None),
        P(("dp", "code")),
        P("code", None),
        P("code"),
        P(("dp", "code")),
        P(("dp", "code")),
        P(("dp", "code"), None),
    )
    reorder = functools.partial(per_device, nx, ny, nz)
    return jax.shard_map(
        lambda a, b, s, n, d, r, q: reorder(a, b, s, n, d, r, q),
        mesh=mesh,
        in_specs=in_specs,
        out_specs=(P("code", None), P("code"), P(("dp", "code"))),
        check_vma=False,
    )
```

```python
import functools

import jax
import jax.numpy as jnp
from jax import lax
from jax.experimental import pallas as pl
from jax.experimental.pallas import tpu as pltpu
from jax.sharding import PartitionSpec as P

MESH = pl.DeviceIdType.MESH
DECAY = 0.8
TILE = 16
USED = 14
DEAD_SLOT = 12
CORES = 2
BIG = 3.0e38


def onehot(mask):
    return jnp.where(mask, 1.0, 0.0).astype(jnp.bfloat16)


def column(row):
    return jnp.broadcast_to(row, (128, 128)).T


def body(
    nx, ny, nz, lat_in, ids_in, dead_in, ridx_in, ema_s_in, ema_c_in, nxt_in, book, cnt_out, dist,
    lat, ids, dead, ridx, ema_s, ema_c, nxt, turned,
    pack, zbuf, relay, gsrc, gbuf, qbuf, ext, parts, rs_send, rs_recv, code, norm, acc, low_send, low_recv, cnts, in_s,
    z_s, z_r, relay_s, relay_r, g_s, g_r, q1_s, q1_r, q2_s, q2_r, q3_s, q3_r, f_s, f_r, x_s, x_r, b_s, b_r, c_s, c_r,
    right_s, right_r, left_s, left_r, m_s, m_r,
):
    rows = lat.shape[0]
    k_dev = book.shape[0]
    sub = k_dev // nx
    queries = nxt.shape[0]
    nyc = ny * CORES
    planes = nx * nyc
    group = nz // 4
    block = nyc * USED
    shift_k = k_dev.bit_length() - 1
    shift_z = nz.bit_length() - 1

    x = lax.axis_index("dp")
    me = lax.axis_index("code")
    c = lax.rem(me, CORES)
    z = lax.rem(lax.div(me, CORES), nz)
    y = lax.div(me, CORES * nz)
    me_yc = y * CORES + c
    me_p = x * nyc + me_yc

    def at(ax, ay, az, ac):
        return (ax, (ay * nz + az) * CORES + ac)

    def in_plane(p):
        yc = lax.rem(p, nyc)
        return at(lax.div(p, nyc), lax.div(yc, CORES), z, lax.rem(yc, CORES))

    def sent(ref, sem):
        pltpu.make_async_copy(ref, ref, sem).wait()

    def along_z(d):
        return at(x, y, lax.rem(z + d + nz, nz), c)

    mine = pl.ds(pl.multiple_of(x * sub, sub), sub)
    sources = (lat_in, ids_in, dead_in, ridx_in, nxt_in, ema_c_in, ema_s_in.at[mine])
    loads = [
        pltpu.make_async_copy(src, dst, in_s.at[i])
        for i, (src, dst) in enumerate(zip(sources, (lat, ids, dead, ridx, nxt, ema_c, ema_s)))
    ]
    for load in loads:
        load.start()

    barrier = pltpu.get_barrier_semaphore()

    @pl.loop(1, planes)
    def _(d):
        pl.semaphore_signal(barrier, inc=1, device_id=in_plane(lax.rem(me_p + d, planes)), device_id_type=MESH)

    @pl.loop(1, nz)
    def _(d):
        pl.semaphore_signal(barrier, inc=1, device_id=along_z(d), device_id_type=MESH)

    for load in loads[:4]:
        load.wait()
    lanes = rows + 128
    own = ids[...]

    def place(labels):
        owner = labels >> shift_k
        oc, oz, oy = owner & 1, (owner >> 1) & (nz - 1), owner >> (1 + shift_z)
        return oz * nyc + oy * CORES + oc

    owner = place(own)
    match = lax.broadcasted_iota(jnp.int32, (nyc * nz, rows), 0) == owner
    before = lax.broadcasted_iota(jnp.int32, (rows, rows), 0) < lax.broadcasted_iota(jnp.int32, (rows, rows), 1)
    earlier = jnp.dot(onehot(match), onehot(before), preferred_element_type=jnp.float32)
    rank = jnp.sum(jnp.where(match, earlier, 0.0), axis=0, keepdims=True).astype(jnp.int32)

    ext[...] = jnp.full(ext.shape, -1, jnp.int32)
    ext[0:1, 0 : dead.shape[1]] = dead[...]
    ext[1:2, 0 : dead.shape[1]] = ridx[...]
    gone = ext[0:1, :]
    gone_owner = jnp.where(gone >= 0, place(gone), -1024)
    pick = column(ext[1:2, :].astype(jnp.float32)).astype(jnp.int32)
    lane = lax.broadcasted_iota(jnp.int32, (128, 128), 1)
    picks = jnp.concatenate([onehot(pick == lane + 128 * i) for i in range(rows // 128)], axis=1)
    restarts = jnp.dot(picks, lat[...], preferred_element_type=jnp.float32).astype(jnp.bfloat16)

    all_owner = jnp.concatenate([owner, gone_owner], axis=1)
    slot = jnp.concatenate([rank, jnp.full((1, 128), DEAD_SLOT, jnp.int32)], axis=1)
    tag = jnp.concatenate([own & (k_dev - 1), (gone & (k_dev - 1)) + k_dev], axis=1)
    tag = jnp.left_shift(128 + (tag & 127), tag >> 7).astype(jnp.float32)
    local = all_owner & (nyc - 1)
    goal = all_owner >> (nyc.bit_length() - 1)
    key = local * (USED - 1) + slot
    tag_key = local + nyc * (USED - 1)
    spot = jnp.where((lax.broadcasted_iota(jnp.int32, (128, lanes), 0) & (TILE - 1)) == slot, 1.0, 0.0)
    spot = jnp.concatenate([spot[:, i * 128 : (i + 1) * 128].T for i in range(lanes // 128)], axis=0)
    data = jnp.concatenate([jnp.concatenate([lat[...], restarts], axis=0), spot.astype(jnp.bfloat16)], axis=1)
    line = lax.broadcasted_iota(jnp.int32, (block, lanes), 0)
    lane_tile = lax.broadcasted_iota(jnp.int32, (1, 128), 1) >> 4

    half = nz // 2
    way = 1 - 2 * c

    def offset(k):
        return jnp.where(lax.rem(k, 2) == 1, half - lax.div(k + 1, 2), nz - half + lax.div(k, 2))

    def packed(k):
        to = goal == lax.rem(z + offset(k), nz)
        put = jnp.where(line == jnp.where(to, key, -1), 1.0, jnp.where(line == jnp.where(to, tag_key, -1), tag, 0.0))
        moved = jnp.dot(put.astype(jnp.bfloat16), data, preferred_element_type=jnp.float32)
        here = lax.rem(me_yc * group + lax.rem(k, group), 8)
        tags = jnp.where(lane_tile == here, moved[:, 128:], 0.0)
        is_tag = lax.broadcasted_iota(jnp.int32, (block, 128), 0) >= nyc * (USED - 1)
        return jnp.where(is_tag, tags, moved[:, :128]).astype(jnp.bfloat16)

    def z_copy(k):
        return pltpu.make_async_remote_copy(
            src_ref=pack.at[k], dst_ref=zbuf.at[k], send_sem=z_s, recv_sem=z_r.at[lax.div(k, group)],
            device_id=along_z(offset(k)), device_id_type=MESH,
        )

    def relay_in():
        return pltpu.make_async_remote_copy(
            src_ref=pack.at[0], dst_ref=relay, send_sem=z_s, recv_sem=relay_r,
            device_id=along_z(way), device_id_type=MESH,
        )

    def relay_out():
        return pltpu.make_async_remote_copy(
            src_ref=relay, dst_ref=zbuf.at[0], send_sem=relay_s, recv_sem=z_r.at[0],
            device_id=along_z(way * (half - 1)), device_id_type=MESH,
        )

    def neighbour(axis, d):
        if axis == "x":
            return at(lax.rem(x + d + nx, nx), y, z, c)
        return at(x, lax.rem(y + d + ny, ny), z, c)

    def send(src, dst, sems, device):
        return pltpu.make_async_remote_copy(
            src_ref=src, dst_ref=dst, send_sem=sems[0], recv_sem=sems[1], device_id=device, device_id_type=MESH
        )

    one, two, three = (q1_s, q1_r), (q2_s, q2_r), (q3_s, q3_r)
    cores = ((0, "y", "x"), (1, "x", "y"))

    def queries_one():
        for core, axis, _ in cores:

            @pl.when(c == core)
            def _(core=core, axis=axis):
                for d in range(1, ny):
                    send(turned, qbuf.at[x, y, core], one, neighbour(axis, d)).start()

    def queries_two():
        sent(qbuf.at[0, 0 : ny - 1, 0], q1_r)
        for core, _, axis in cores:

            @pl.when(c == core)
            def _(core=core, axis=axis):
                line_of = qbuf.at[x, :, core] if axis == "x" else qbuf.at[:, y, core]
                send(line_of, line_of, two, neighbour(axis, 1)).start()
                send(line_of, line_of, two, neighbour(axis, -1)).start()

    def queries_three():
        sent(qbuf.at[0:2, :, 0], q2_r)
        for core, _, axis in cores:

            @pl.when(c == core)
            def _(core=core, axis=axis):
                lower, upper = pl.ds(0, ny // 2), pl.ds(ny // 2, ny // 2)
                if axis == "x":
                    before, after = lax.rem(x + nx - 1, nx), lax.rem(x + 1, nx)
                    on, back = qbuf.at[before, lower, core], qbuf.at[after, upper, core]
                else:
                    before, after = lax.rem(y + ny - 1, ny), lax.rem(y + 1, ny)
                    on, back = qbuf.at[lower, before, core], qbuf.at[upper, after, core]
                send(on, on, three, neighbour(axis, 1)).start()
                send(back, back, three, neighbour(axis, -1)).start()

    def queries_across():
        mine_too = qbuf.at[:, :, c]
        return send(mine_too, mine_too, (f_s, f_r), at(x, y, z, 1 - c))

    loads[4].wait()
    wide = nxt[...].astype(jnp.float32)
    query_norm = jnp.sum((wide * wide).T, axis=0, keepdims=True)
    turned[...] = wide.T.astype(jnp.bfloat16)
    qbuf[x, y, c] = turned[...]
    pack[0] = packed(jnp.int32(0))
    pl.semaphore_wait(barrier, planes - 1 + nz - 1)
    relay_in().start()
    queries_one()

    @pl.loop(0, half - 1)
    def _(o):
        for i in range(2):
            k = 1 + o * 2 + i
            pack[k] = packed(k)
            z_copy(k).start()

        @pl.when(o == (half - 1) // 2)
        def _():
            relay_in().wait_recv()
            relay_out().start()

    zbuf[nz - 1] = packed(jnp.int32(nz - 1))
    queries_two()

    acc[...] = jnp.full(acc.shape, BIG, jnp.float32)

    def g_copy(g, j):
        return pltpu.make_async_remote_copy(
            src_ref=gsrc.at[pl.ds(g * group, group), j],
            dst_ref=gbuf.at[me_yc, pl.ds(g * group, group)],
            send_sem=g_s, recv_sem=g_r.at[g],
            device_id=at(x, lax.div(j, CORES), z, lax.rem(j, CORES)), device_id_type=MESH,
        )

    row = lax.broadcasted_iota(jnp.int32, (nyc * TILE, block), 0)
    tile, spare = row >> 4, (row & (TILE - 1)) - DEAD_SLOT
    origin = jnp.where(spare <= 0, tile * (USED - 1) + DEAD_SLOT + spare, jnp.where(spare == 1, tile + nyc * (USED - 1), -1))
    spread = onehot(lax.broadcasted_iota(jnp.int32, (nyc * TILE, block), 1) == origin)

    total = nyc * group * TILE
    in_tile = lax.broadcasted_iota(jnp.int32, (8, 128), 1) & (TILE - 1)
    read = onehot(in_tile > DEAD_SLOT)
    name = (lax.broadcasted_iota(jnp.int32, (sub, total), 0) + 128).astype(jnp.float32)

    def arrived(g):
        sent(gbuf.at[0 : nyc - 1, pl.ds(g * group, group)], g_r.at[g])
        got = gbuf[:, pl.ds(g * group, group)].reshape(total, 128)
        tags = [
            jnp.dot(read, got[i * 128 : (i + 1) * 128], preferred_element_type=jnp.float32)[0:1]
            for i in range(total // 128)
        ]
        return jnp.concatenate(tags, axis=1), jnp.concatenate([got, jnp.ones((total, 128), jnp.bfloat16)], axis=1)

    def tally(tags, got, scale):
        here = tags * scale
        hits = jnp.concatenate([onehot(name == here), onehot(name == here * 0.5**nx)], axis=0)
        return jnp.dot(hits, got, preferred_element_type=jnp.float32)

    for g in range(4):
        here = pl.ds(g * group, min(group, nz - 1 - g * group))
        sent(zbuf.at[here], z_r.at[g])
        for k in range(g * group, (g + 1) * group):
            tiles = jnp.dot(spread, zbuf[k], preferred_element_type=jnp.float32)
            gsrc[k] = tiles.astype(jnp.bfloat16).reshape(nyc, TILE, 128)

        @pl.loop(1, nyc)
        def _(d):
            g_copy(g, lax.rem(me_yc + d, nyc)).start()

        gbuf[me_yc, pl.ds(g * group, group)] = gsrc[pl.ds(g * group, group), me_yc]
        if g > 0:
            tags, got = arrived(g - 1)
            for i in range(nx):
                part = tally(tags, got, 0.5**i)
                parts[i] = part if g == 1 else parts[i] + part
        if g == 0:
            queries_three()
        if g == 1:
            sent(qbuf.at[0, :, 0], q3_r)
            queries_across().start()

    def x_copy(to, frm):
        return pltpu.make_async_remote_copy(
            src_ref=rs_send.at[to], dst_ref=rs_recv.at[frm], send_sem=x_s, recv_sem=x_r,
            device_id=at(to, y, z, c), device_id_type=MESH,
        )

    tags, got = arrived(3)
    for d in range(1, nx + 1):
        to = lax.rem(x + d, nx)
        scale = jnp.float32(1.0)
        for i in range(1, nx):
            scale = jnp.where(to == i, 0.5**i, scale)
        both = parts[to] + tally(tags, got, scale)
        sums, count = both[:, :128], both[:, 128:]
        is_dead = count[sub:] > 0.5
        ref = rs_send if d < nx else rs_recv
        ref[to, 0:sub, :] = jnp.where(is_dead, sums[sub:], sums[:sub])
        ref[to, sub : sub + 8, :] = jnp.where(is_dead, -1.0, count[:sub]).T[0:8]
        if d < nx:
            x_copy(to, x).start()

    sent(rs_recv.at[0 : nx - 1], x_r)

    count = jnp.zeros((1, 128), jnp.float32)
    dead_row = jnp.zeros((1, 128), jnp.float32)
    sums = jnp.zeros((sub, 128), jnp.float32)
    restart = jnp.zeros((sub, 128), jnp.float32)
    for i in range(nx):
        part = rs_recv[i, sub : sub + 1, :]
        count += jnp.maximum(part, 0.0)
        dead_row = jnp.maximum(dead_row, -part)
        piece = rs_recv[i, 0:sub, :]
        sums += piece
        restart += jnp.where(column(part) < 0.0, piece, 0.0)
    for load in loads[5:]:
        load.wait()
    fresh_row = DECAY * ema_c[pl.ds(x, 1), :] + (1.0 - DECAY) * count
    fresh_row = jnp.where(dead_row > 0.5, 1.0, fresh_row)
    fresh = DECAY * ema_s[...] + (1.0 - DECAY) * sums
    fresh = jnp.where(column(dead_row) > 0.5, restart, fresh)
    rows_out = fresh / column(fresh_row)
    code[0] = (-2.0 * rows_out.astype(jnp.bfloat16).astype(jnp.float32)).astype(jnp.bfloat16)

    rounds = nz // 4

    def right(r, j):
        return pltpu.make_async_remote_copy(
            src_ref=code.at[jnp.maximum(4 * r - 2, 0)], dst_ref=code.at[4 * r + j],
            send_sem=right_s, recv_sem=right_r.at[r], device_id=along_z(j), device_id_type=MESH,
        )

    def left(r, j):
        return pltpu.make_async_remote_copy(
            src_ref=code.at[4 * r], dst_ref=code.at[4 * r + 2 + j],
            send_sem=left_s, recv_sem=left_r.at[r], device_id=along_z(-j), device_id_type=MESH,
        )

    right(jnp.int32(0), 2).start()
    if rounds > 1:
        left(jnp.int32(0), 2).start()
    right(jnp.int32(0), 1).start()
    left(jnp.int32(0), 1).start()

    book[mine, :] = rows_out
    cnts[x] = jnp.broadcast_to(fresh_row, (8, 128))

    def b_copy(to, frm):
        span = pl.ds(pl.multiple_of(frm * sub, sub), sub)
        return pltpu.make_async_remote_copy(
            src_ref=book.at[span], dst_ref=book.at[span], send_sem=b_s, recv_sem=b_r,
            device_id=at(to, y, z, c), device_id_type=MESH,
        )

    def c_copy(to, frm):
        return pltpu.make_async_remote_copy(
            src_ref=cnts.at[frm], dst_ref=cnts.at[frm], send_sem=c_s, recv_sem=c_r,
            device_id=at(to, y, z, c), device_id_type=MESH,
        )

    for d in range(1, nx):
        to = lax.rem(x + d, nx)
        b_copy(to, x).start()
        c_copy(to, x).start()

    sent(qbuf.at[:, :, 0], f_r)

    def m_copy(to, frm):
        return pltpu.make_async_remote_copy(
            src_ref=low_send.at[to], dst_ref=low_recv.at[frm], send_sem=m_s, recv_sem=m_r,
            device_id=in_plane(to), device_id_type=MESH,
        )

    halves = queries // 128

    def lowest(p):
        small = jnp.min(acc[p], axis=0, keepdims=True)
        parts_of = [jnp.broadcast_to(small[:, h * 128 : (h + 1) * 128], (8 // halves, 128)) for h in range(halves)]
        return jnp.concatenate(parts_of, axis=0)

    chips = nx * ny
    me_chip = x * ny + y
    unroll = 4
    spread_out = chips // unroll

    def norms(first, count):
        table = code[pl.ds(first, count)].reshape(count * sub, 128).astype(jnp.float32)
        both = 0.25 * jnp.sum(table * table, axis=1, keepdims=True)
        norm[0 : count * sub] = jnp.broadcast_to(both, (count * sub, 128))

    def compare(first, count, o):
        deep = count * sub
        for i in range(unroll):
            chip = lax.rem(me_chip + 1 + o * unroll + i, chips)
            px, py = lax.div(chip, ny), lax.rem(chip, ny)
            score = jnp.dot(
                code[pl.ds(first, count)].reshape(deep, 128),
                jnp.concatenate([qbuf[px, py, j] for j in range(CORES)], axis=1),
                preferred_element_type=jnp.float32,
            )
            lows = [
                jnp.min((norm[0:deep] + score[:, h * 128 : (h + 1) * 128]).reshape(deep // 8, 8, 128), axis=0)
                for h in range(CORES * halves)
            ]
            for j in range(CORES):
                low = jnp.concatenate(lows[j * halves : (j + 1) * halves], axis=1)
                acc[chip * CORES + j] = jnp.minimum(acc[chip * CORES + j], low)

    norms(0, 1)

    @pl.loop(0, spread_out)
    def _(o):
        compare(0, 1, o)

    @pl.loop(0, rounds - 1)
    def _(t):
        sent(code.at[0:2], right_r.at[t])
        right(t + 1, 2).start()
        sent(code.at[0:2], left_r.at[t])

        @pl.when(t < rounds - 2)
        def _():
            left(t + 1, 2).start()

        right(t + 1, 1).start()
        left(t + 1, 1).start()
        norms(4 * t + 1, 4)

        @pl.loop(0, spread_out)
        def _(o):
            compare(4 * t + 1, 4, o)

    last = 4 * (rounds - 1) + 1
    sent(code.at[0:2], right_r.at[rounds - 1])
    sent(code.at[0], left_r.at[rounds - 1])
    norms(last, 3)

    @pl.loop(0, spread_out)
    def _(o):
        compare(last, 3, o)

        @pl.loop(o * unroll * CORES, jnp.minimum((o + 1) * unroll * CORES, planes - 1))
        def _(i):
            chip = lax.rem(me_chip + 1 + lax.div(i, CORES), chips)
            to = chip * CORES + lax.rem(i + c + 1, CORES)
            low_send[to] = lowest(to)
            m_copy(to, me_p).start()

    low_recv[me_p] = lowest(me_p)

    sent(low_recv.at[0 : planes - 1], m_r)

    best = jnp.min(low_recv[...], axis=0)
    for h in range(halves):
        first = h * (8 // halves)
        dist[h : h + 1, :] = (best[first : first + 1] + query_norm[:, h * 128 : (h + 1) * 128]) / 128

    sent(book.at[0 : (nx - 1) * sub], b_r)
    sent(cnts.at[0 : nx - 1], c_r)
    for i in range(nx):
        cnt_out[i : i + 1, :] = cnts[i, 0:1, :]

    sent(pack.at[0 : nz - 1], z_s)
    sent(relay, relay_s)
    sent(qbuf.at[0, 0 : ny - 1, 0], q1_s)
    sent(qbuf.at[0:2, :, 0], q2_s)
    sent(qbuf.at[0, :, 0], q3_s)
    sent(qbuf.at[:, :, 0], f_s)
    sent(gsrc.at[:, 0 : nyc - 1], g_s)
    sent(rs_send.at[0 : nx - 1], x_s)
    sent(book.at[0 : (nx - 1) * sub], b_s)
    sent(cnts.at[0 : nx - 1], c_s)
    sent(code.at[0 : 2 * rounds], right_s)
    sent(code.at[0 : 2 * rounds - 1], left_s)
    sent(low_send.at[0 : planes - 1], m_s)


def per_device(nx, ny, nz, latents, code_ids, ema_sums, ema_counts, dead_codes, restart_index, next_latents):
    k_dev = ema_sums.shape[0]
    sub = k_dev // nx
    nyc = ny * CORES
    planes = nx * nyc
    queries = next_latents.shape[0]
    hbm = pl.BlockSpec(memory_space=pl.ANY)
    vmem = pl.BlockSpec(memory_space=pltpu.VMEM)
    dma = pltpu.SemaphoreType.DMA
    bf16, f32 = jnp.bfloat16, jnp.float32
    book, counts, dist = pl.pallas_call(
        functools.partial(body, nx, ny, nz),
        out_shape=(
            jax.ShapeDtypeStruct((k_dev, 128), f32),
            jax.ShapeDtypeStruct((nx, sub), f32),
            jax.ShapeDtypeStruct((queries // 128, 128), f32),
        ),
        in_specs=[hbm] * 7,
        out_specs=(vmem,) * 3,
        scratch_shapes=[
            pltpu.VMEM(latents.shape, bf16),
            pltpu.VMEM((1, code_ids.shape[0]), jnp.int32),
            pltpu.VMEM((1, dead_codes.shape[0]), jnp.int32),
            pltpu.VMEM((1, dead_codes.shape[0]), jnp.int32),
            pltpu.VMEM((sub, 128), f32),
            pltpu.VMEM((nx, sub), f32),
            pltpu.VMEM((queries, 128), bf16),
            pltpu.VMEM((128, queries), bf16),
            pltpu.VMEM((nz, nyc * USED, 128), bf16),
            pltpu.VMEM((nz, nyc * USED, 128), bf16),
            pltpu.VMEM((nyc * USED, 128), bf16),
            pltpu.VMEM((nz, nyc, TILE, 128), bf16),
            pltpu.VMEM((nyc, nz, TILE, 128), bf16),
            pltpu.VMEM((nx, ny, CORES, 128, queries), bf16),
            pltpu.VMEM((8, 128), jnp.int32),
            pltpu.VMEM((nx, 2 * sub, 256), f32),
            pltpu.VMEM((nx, sub + 8, 128), f32),
            pltpu.VMEM((nx, sub + 8, 128), f32),
            pltpu.VMEM((nz, sub, 128), bf16),
            pltpu.VMEM((4 * sub, 128), f32),
            pltpu.VMEM((planes, 8, queries), f32),
            pltpu.VMEM((planes, 8, 128), f32),
            pltpu.VMEM((planes, 8, 128), f32),
            pltpu.VMEM((nx, 8, 128), f32),
            dma((7,)),
            dma, dma((4,)), dma, dma,
            dma, dma((4,)),
            dma, dma, dma, dma, dma, dma, dma, dma,
            dma, dma, dma, dma, dma, dma,
            dma, dma((nz // 4,)), dma, dma((nz // 4,)),
            dma, dma,
        ],
        compiler_params=pltpu.CompilerParams(
            collective_id=0, has_side_effects=True, vmem_limit_bytes=56 * 1024 * 1024
        ),
    )(
        latents, code_ids.reshape(1, -1), dead_codes.reshape(1, -1), restart_index.reshape(1, -1),
        ema_sums, ema_counts.reshape(nx, sub), next_latents,
    )
    return book, counts.reshape(-1), dist.reshape(-1)


def solution(mesh, ny=4):
    nx = mesh.shape["dp"]
    nz = mesh.shape["code"] // (CORES * ny)
    in_specs = (
        P(("dp", "code"), None),
        P(("dp", "code")),
        P("code", None),
        P("code"),
        P(("dp", "code")),
        P(("dp", "code")),
        P(("dp", "code"), None),
    )
    reorder = functools.partial(per_device, nx, ny, nz)
    return jax.shard_map(
        lambda a, b, s, n, d, r, q: reorder(a, b, s, n, d, r, q),
        mesh=mesh,
        in_specs=in_specs,
        out_specs=(P("code", None), P("code"), P(("dp", "code"))),
        check_vma=False,
    )
```

```python
import functools

import jax
import jax.numpy as jnp
from jax import lax
from jax.experimental import pallas as pl
from jax.experimental.pallas import tpu as pltpu
from jax.sharding import PartitionSpec as P

MESH = pl.DeviceIdType.MESH
DECAY = 0.8
TILE = 16
USED = 14
DEAD_SLOT = 12
CORES = 2
BIG = 3.0e38


def onehot(mask):
    return jnp.where(mask, 1.0, 0.0).astype(jnp.bfloat16)


def column(row):
    return jnp.broadcast_to(row, (128, 128)).T


def body(
    nx, ny, nz, lat_in, ids_in, dead_in, ridx_in, ema_s_in, ema_c_in, nxt_in, book_hbm, cnt_hbm, dist,
    book, cnt_out, lat, ids, dead, ridx, ema_s, ema_c, nxt, turned,
    pack, zbuf, relay, gsrc, gbuf, qbuf, ext, parts, rs_send, rs_recv, code, norm, acc, low_send, low_recv, cnts, in_s,
    z_s, z_r, relay_s, relay_r, g_s, g_r, q1_s, q1_r, q2_s, q2_r, q3_s, q3_r, f_s, f_r, x_s, x_r, b_s, b_r, c_s, c_r,
    right_s, right_r, left_s, left_r, m_s, m_r,
):
    rows = lat.shape[0]
    k_dev = book.shape[0]
    sub = k_dev // nx
    queries = nxt.shape[0]
    nyc = ny * CORES
    planes = nx * nyc
    group = nz // 4
    block = nyc * USED
    shift_k = k_dev.bit_length() - 1
    shift_z = nz.bit_length() - 1

    x = lax.axis_index("dp")
    me = lax.axis_index("code")
    c = lax.rem(me, CORES)
    z = lax.rem(lax.div(me, CORES), nz)
    y = lax.div(me, CORES * nz)
    me_yc = y * CORES + c
    me_p = x * nyc + me_yc

    def at(ax, ay, az, ac):
        return (ax, (ay * nz + az) * CORES + ac)

    def in_plane(p):
        yc = lax.rem(p, nyc)
        return at(lax.div(p, nyc), lax.div(yc, CORES), z, lax.rem(yc, CORES))

    def sent(ref, sem):
        pltpu.make_async_copy(ref, ref, sem).wait()

    def along_z(d):
        return at(x, y, lax.rem(z + d + nz, nz), c)

    mine = pl.ds(pl.multiple_of(x * sub, sub), sub)
    sources = (lat_in, ids_in, dead_in, ridx_in, nxt_in, ema_c_in, ema_s_in.at[mine])
    loads = [
        pltpu.make_async_copy(src, dst, in_s.at[i])
        for i, (src, dst) in enumerate(zip(sources, (lat, ids, dead, ridx, nxt, ema_c, ema_s)))
    ]
    for load in loads:
        load.start()

    barrier = pltpu.get_barrier_semaphore()

    @pl.loop(1, planes)
    def _(d):
        pl.semaphore_signal(barrier, inc=1, device_id=in_plane(lax.rem(me_p + d, planes)), device_id_type=MESH)

    @pl.loop(1, nz)
    def _(d):
        pl.semaphore_signal(barrier, inc=1, device_id=along_z(d), device_id_type=MESH)

    for load in loads[:4]:
        load.wait()
    lanes = rows + 128
    own = ids[...]

    def place(labels):
        owner = labels >> shift_k
        oc, oz, oy = owner & 1, (owner >> 1) & (nz - 1), owner >> (1 + shift_z)
        return oz * nyc + oy * CORES + oc

    owner = place(own)
    match = lax.broadcasted_iota(jnp.int32, (nyc * nz, rows), 0) == owner
    before = lax.broadcasted_iota(jnp.int32, (rows, rows), 0) < lax.broadcasted_iota(jnp.int32, (rows, rows), 1)
    earlier = jnp.dot(onehot(match), onehot(before), preferred_element_type=jnp.float32)
    rank = jnp.sum(jnp.where(match, earlier, 0.0), axis=0, keepdims=True).astype(jnp.int32)

    ext[...] = jnp.full(ext.shape, -1, jnp.int32)
    ext[0:1, 0 : dead.shape[1]] = dead[...]
    ext[1:2, 0 : dead.shape[1]] = ridx[...]
    gone = ext[0:1, :]
    gone_owner = jnp.where(gone >= 0, place(gone), -1024)
    pick = column(ext[1:2, :].astype(jnp.float32)).astype(jnp.int32)
    lane = lax.broadcasted_iota(jnp.int32, (128, 128), 1)
    picks = jnp.concatenate([onehot(pick == lane + 128 * i) for i in range(rows // 128)], axis=1)
    restarts = jnp.dot(picks, lat[...], preferred_element_type=jnp.float32).astype(jnp.bfloat16)

    all_owner = jnp.concatenate([owner, gone_owner], axis=1)
    slot = jnp.concatenate([rank, jnp.full((1, 128), DEAD_SLOT, jnp.int32)], axis=1)
    tag = jnp.concatenate([own & (k_dev - 1), (gone & (k_dev - 1)) + k_dev], axis=1)
    tag = jnp.left_shift(128 + (tag & 127), tag >> 7).astype(jnp.float32)
    local = all_owner & (nyc - 1)
    goal = all_owner >> (nyc.bit_length() - 1)
    key = local * (USED - 1) + slot
    tag_key = local + nyc * (USED - 1)
    spot = jnp.where((lax.broadcasted_iota(jnp.int32, (128, lanes), 0) & (TILE - 1)) == slot, 1.0, 0.0)
    spot = jnp.concatenate([spot[:, i * 128 : (i + 1) * 128].T for i in range(lanes // 128)], axis=0)
    data = jnp.concatenate([jnp.concatenate([lat[...], restarts], axis=0), spot.astype(jnp.bfloat16)], axis=1)
    line = lax.broadcasted_iota(jnp.int32, (block, lanes), 0)
    lane_tile = lax.broadcasted_iota(jnp.int32, (1, 128), 1) >> 4

    half = nz // 2
    way = 1 - 2 * c

    def offset(k):
        return jnp.where(lax.rem(k, 2) == 1, half - lax.div(k + 1, 2), nz - half + lax.div(k, 2))

    def packed(k):
        to = goal == lax.rem(z + offset(k), nz)
        put = jnp.where(line == jnp.where(to, key, -1), 1.0, jnp.where(line == jnp.where(to, tag_key, -1), tag, 0.0))
        moved = jnp.dot(put.astype(jnp.bfloat16), data, preferred_element_type=jnp.float32)
        here = lax.rem(me_yc * group + lax.rem(k, group), 8)
        tags = jnp.where(lane_tile == here, moved[:, 128:], 0.0)
        is_tag = lax.broadcasted_iota(jnp.int32, (block, 128), 0) >= nyc * (USED - 1)
        return jnp.where(is_tag, tags, moved[:, :128]).astype(jnp.bfloat16)

    def z_copy(k):
        return pltpu.make_async_remote_copy(
            src_ref=pack.at[k], dst_ref=zbuf.at[k], send_sem=z_s, recv_sem=z_r.at[lax.div(k, group)],
            device_id=along_z(offset(k)), device_id_type=MESH,
        )

    def relay_in():
        return pltpu.make_async_remote_copy(
            src_ref=pack.at[0], dst_ref=relay, send_sem=z_s, recv_sem=relay_r,
            device_id=along_z(way), device_id_type=MESH,
        )

    def relay_out():
        return pltpu.make_async_remote_copy(
            src_ref=relay, dst_ref=zbuf.at[0], send_sem=relay_s, recv_sem=z_r.at[0],
            device_id=along_z(way * (half - 1)), device_id_type=MESH,
        )

    def neighbour(axis, d):
        if axis == "x":
            return at(lax.rem(x + d + nx, nx), y, z, c)
        return at(x, lax.rem(y + d + ny, ny), z, c)

    def send(src, dst, sems, device):
        return pltpu.make_async_remote_copy(
            src_ref=src, dst_ref=dst, send_sem=sems[0], recv_sem=sems[1], device_id=device, device_id_type=MESH
        )

    one, two, three = (q1_s, q1_r), (q2_s, q2_r), (q3_s, q3_r)
    cores = ((0, "y", "x"), (1, "x", "y"))

    def queries_one():
        for core, axis, _ in cores:

            @pl.when(c == core)
            def _(core=core, axis=axis):
                for d in range(1, ny):
                    send(turned, qbuf.at[x, y, core], one, neighbour(axis, d)).start()

    def queries_two():
        sent(qbuf.at[0, 0 : ny - 1, 0], q1_r)
        for core, _, axis in cores:

            @pl.when(c == core)
            def _(core=core, axis=axis):
                line_of = qbuf.at[x, :, core] if axis == "x" else qbuf.at[:, y, core]
                send(line_of, line_of, two, neighbour(axis, 1)).start()
                send(line_of, line_of, two, neighbour(axis, -1)).start()

    def queries_three():
        sent(qbuf.at[0:2, :, 0], q2_r)
        for core, _, axis in cores:

            @pl.when(c == core)
            def _(core=core, axis=axis):
                lower, upper = pl.ds(0, ny // 2), pl.ds(ny // 2, ny // 2)
                if axis == "x":
                    before, after = lax.rem(x + nx - 1, nx), lax.rem(x + 1, nx)
                    on, back = qbuf.at[before, lower, core], qbuf.at[after, upper, core]
                else:
                    before, after = lax.rem(y + ny - 1, ny), lax.rem(y + 1, ny)
                    on, back = qbuf.at[lower, before, core], qbuf.at[upper, after, core]
                send(on, on, three, neighbour(axis, 1)).start()
                send(back, back, three, neighbour(axis, -1)).start()

    def queries_across():
        mine_too = qbuf.at[:, :, c]
        return send(mine_too, mine_too, (f_s, f_r), at(x, y, z, 1 - c))

    loads[4].wait()
    wide = nxt[...].astype(jnp.float32)
    query_norm = jnp.sum((wide * wide).T, axis=0, keepdims=True)
    turned[...] = wide.T.astype(jnp.bfloat16)
    qbuf[x, y, c] = turned[...]
    pack[0] = packed(jnp.int32(0))
    pl.semaphore_wait(barrier, planes - 1 + nz - 1)
    relay_in().start()
    queries_one()

    @pl.loop(0, half - 1)
    def _(o):
        for i in range(2):
            k = 1 + o * 2 + i
            pack[k] = packed(k)
            z_copy(k).start()

        @pl.when(o == (half - 1) // 2)
        def _():
            relay_in().wait_recv()
            relay_out().start()

    zbuf[nz - 1] = packed(jnp.int32(nz - 1))
    queries_two()

    acc[...] = jnp.full(acc.shape, BIG, jnp.float32)

    def g_copy(g, j):
        return pltpu.make_async_remote_copy(
            src_ref=gsrc.at[pl.ds(g * group, group), j],
            dst_ref=gbuf.at[me_yc, pl.ds(g * group, group)],
            send_sem=g_s, recv_sem=g_r.at[g],
            device_id=at(x, lax.div(j, CORES), z, lax.rem(j, CORES)), device_id_type=MESH,
        )

    row = lax.broadcasted_iota(jnp.int32, (nyc * TILE, block), 0)
    tile, spare = row >> 4, (row & (TILE - 1)) - DEAD_SLOT
    origin = jnp.where(spare <= 0, tile * (USED - 1) + DEAD_SLOT + spare, jnp.where(spare == 1, tile + nyc * (USED - 1), -1))
    spread = onehot(lax.broadcasted_iota(jnp.int32, (nyc * TILE, block), 1) == origin)

    total = nyc * group * TILE
    in_tile = lax.broadcasted_iota(jnp.int32, (8, 128), 1) & (TILE - 1)
    read = onehot(in_tile > DEAD_SLOT)
    name = (lax.broadcasted_iota(jnp.int32, (sub, total), 0) + 128).astype(jnp.float32)

    def arrived(g):
        sent(gbuf.at[0 : nyc - 1, pl.ds(g * group, group)], g_r.at[g])
        got = gbuf[:, pl.ds(g * group, group)].reshape(total, 128)
        tags = [
            jnp.dot(read, got[i * 128 : (i + 1) * 128], preferred_element_type=jnp.float32)[0:1]
            for i in range(total // 128)
        ]
        return jnp.concatenate(tags, axis=1), jnp.concatenate([got, jnp.ones((total, 128), jnp.bfloat16)], axis=1)

    def tally(tags, got, scale):
        here = tags * scale
        hits = jnp.concatenate([onehot(name == here), onehot(name == here * 0.5**nx)], axis=0)
        return jnp.dot(hits, got, preferred_element_type=jnp.float32)

    for g in range(4):
        here = pl.ds(g * group, min(group, nz - 1 - g * group))
        sent(zbuf.at[here], z_r.at[g])
        for k in range(g * group, (g + 1) * group):
            tiles = jnp.dot(spread, zbuf[k], preferred_element_type=jnp.float32)
            gsrc[k] = tiles.astype(jnp.bfloat16).reshape(nyc, TILE, 128)

        @pl.loop(1, nyc)
        def _(d):
            g_copy(g, lax.rem(me_yc + d, nyc)).start()

        gbuf[me_yc, pl.ds(g * group, group)] = gsrc[pl.ds(g * group, group), me_yc]
        if g > 0:
            tags, got = arrived(g - 1)
            for i in range(nx):
                part = tally(tags, got, 0.5**i)
                parts[i] = part if g == 1 else parts[i] + part
        if g == 0:
            queries_three()
        if g == 1:
            sent(qbuf.at[0, :, 0], q3_r)
            queries_across().start()

    def x_copy(to, frm):
        return pltpu.make_async_remote_copy(
            src_ref=rs_send.at[to], dst_ref=rs_recv.at[frm], send_sem=x_s, recv_sem=x_r,
            device_id=at(to, y, z, c), device_id_type=MESH,
        )

    tags, got = arrived(3)
    for d in (nx // 2, *(i for i in range(1, nx) if i != nx // 2), nx):
        to = lax.rem(x + d, nx)
        scale = jnp.float32(1.0)
        for i in range(1, nx):
            scale = jnp.where(to == i, 0.5**i, scale)
        both = parts[to] + tally(tags, got, scale)
        sums, count = both[:, :128], both[:, 128:]
        is_dead = count[sub:] > 0.5
        ref = rs_send if d < nx else rs_recv
        ref[to, 0:sub, :] = jnp.where(is_dead, sums[sub:], sums[:sub])
        ref[to, sub : sub + 8, :] = jnp.where(is_dead, -1.0, count[:sub]).T[0:8]
        if d < nx:
            x_copy(to, x).start()

    sent(rs_recv.at[0 : nx - 1], x_r)

    count = jnp.zeros((1, 128), jnp.float32)
    dead_row = jnp.zeros((1, 128), jnp.float32)
    sums = jnp.zeros((sub, 128), jnp.float32)
    restart = jnp.zeros((sub, 128), jnp.float32)
    for i in range(nx):
        part = rs_recv[i, sub : sub + 1, :]
        count += jnp.maximum(part, 0.0)
        dead_row = jnp.maximum(dead_row, -part)
        piece = rs_recv[i, 0:sub, :]
        sums += piece
        restart += jnp.where(column(part) < 0.0, piece, 0.0)
    for load in loads[5:]:
        load.wait()
    fresh_row = DECAY * ema_c[pl.ds(x, 1), :] + (1.0 - DECAY) * count
    fresh_row = jnp.where(dead_row > 0.5, 1.0, fresh_row)
    fresh = DECAY * ema_s[...] + (1.0 - DECAY) * sums
    fresh = jnp.where(column(dead_row) > 0.5, restart, fresh)
    rows_out = fresh / column(fresh_row)
    code[0] = (-2.0 * rows_out.astype(jnp.bfloat16).astype(jnp.float32)).astype(jnp.bfloat16)

    rounds = nz // 4

    def right(r, j):
        return pltpu.make_async_remote_copy(
            src_ref=code.at[jnp.maximum(4 * r - 2, 0)], dst_ref=code.at[4 * r + j],
            send_sem=right_s, recv_sem=right_r.at[r, j - 1], device_id=along_z(j), device_id_type=MESH,
        )

    def left(r, j):
        return pltpu.make_async_remote_copy(
            src_ref=code.at[4 * r], dst_ref=code.at[4 * r + 2 + j],
            send_sem=left_s, recv_sem=left_r.at[r, j - 1], device_id=along_z(-j), device_id_type=MESH,
        )

    right(jnp.int32(0), 2).start()
    if rounds > 1:
        left(jnp.int32(0), 2).start()
    right(jnp.int32(0), 1).start()
    left(jnp.int32(0), 1).start()

    book[mine, :] = rows_out
    cnts[x] = jnp.broadcast_to(fresh_row, (8, 128))

    def b_copy(to, frm):
        span = pl.ds(pl.multiple_of(frm * sub, sub), sub)
        return pltpu.make_async_remote_copy(
            src_ref=book.at[span], dst_ref=book.at[span], send_sem=b_s, recv_sem=b_r,
            device_id=at(to, y, z, c), device_id_type=MESH,
        )

    def c_copy(to, frm):
        return pltpu.make_async_remote_copy(
            src_ref=cnts.at[frm], dst_ref=cnts.at[frm], send_sem=c_s, recv_sem=c_r,
            device_id=at(to, y, z, c), device_id_type=MESH,
        )

    for d in range(1, nx):
        to = lax.rem(x + d, nx)
        b_copy(to, x).start()
        c_copy(to, x).start()

    sent(qbuf.at[:, :, 0], f_r)

    def m_copy(to, frm):
        return pltpu.make_async_remote_copy(
            src_ref=low_send.at[to], dst_ref=low_recv.at[frm], send_sem=m_s, recv_sem=m_r,
            device_id=in_plane(to), device_id_type=MESH,
        )

    halves = queries // 128

    def lowest(p):
        small = jnp.min(acc[p], axis=0, keepdims=True)
        parts_of = [jnp.broadcast_to(small[:, h * 128 : (h + 1) * 128], (8 // halves, 128)) for h in range(halves)]
        return jnp.concatenate(parts_of, axis=0)

    chips = nx * ny
    me_chip = x * ny + y
    unroll = 4
    spread_out = chips // unroll

    def norms(first, count):
        table = code[pl.ds(first, count)].reshape(count * sub, 128).astype(jnp.float32)
        both = 0.25 * jnp.sum(table * table, axis=1, keepdims=True)
        norm[0 : count * sub] = jnp.broadcast_to(both, (count * sub, 128))

    def compare(first, count, o):
        deep = count * sub
        for i in range(unroll):
            chip = lax.rem(me_chip + 1 + o * unroll + i, chips)
            px, py = lax.div(chip, ny), lax.rem(chip, ny)
            score = jnp.dot(
                code[pl.ds(first, count)].reshape(deep, 128),
                jnp.concatenate([qbuf[px, py, j] for j in range(CORES)], axis=1),
                preferred_element_type=jnp.float32,
            )
            lows = [
                jnp.min((norm[0:deep] + score[:, h * 128 : (h + 1) * 128]).reshape(deep // 8, 8, 128), axis=0)
                for h in range(CORES * halves)
            ]
            for j in range(CORES):
                low = jnp.concatenate(lows[j * halves : (j + 1) * halves], axis=1)
                acc[chip * CORES + j] = jnp.minimum(acc[chip * CORES + j], low)

    norms(0, 1)

    @pl.loop(0, spread_out)
    def _(o):
        compare(0, 1, o)

    @pl.loop(0, rounds - 1)
    def _(t):
        sent(code.at[0], right_r.at[t, 1])
        right(t + 1, 2).start()
        sent(code.at[0], left_r.at[t, 1])

        @pl.when(t < rounds - 2)
        def _():
            left(t + 1, 2).start()

        right(t + 1, 1).start()
        left(t + 1, 1).start()
        sent(code.at[0], right_r.at[t, 0])
        sent(code.at[0], left_r.at[t, 0])
        norms(4 * t + 1, 4)

        @pl.loop(0, spread_out)
        def _(o):
            compare(4 * t + 1, 4, o)

    last = 4 * (rounds - 1) + 1
    sent(book.at[0 : (nx - 1) * sub], b_r)
    sent(cnts.at[0 : nx - 1], c_r)
    for i in range(nx):
        cnt_out[i : i + 1, :] = cnts[i, 0:1, :]
    results = [
        pltpu.make_async_copy(book, book_hbm, in_s.at[0]),
        pltpu.make_async_copy(cnt_out, cnt_hbm, in_s.at[1]),
    ]
    for result in results:
        result.start()
    sent(code.at[0], right_r.at[rounds - 1, 0])
    sent(code.at[0], left_r.at[rounds - 1, 0])
    sent(code.at[0], right_r.at[rounds - 1, 1])
    norms(last, 3)

    @pl.loop(0, spread_out)
    def _(o):
        compare(last, 3, o)

        @pl.loop(o * unroll * CORES, jnp.minimum((o + 1) * unroll * CORES, planes - 1))
        def _(i):
            chip = lax.rem(me_chip + 1 + lax.div(i, CORES), chips)
            to = chip * CORES + lax.rem(i + c + 1, CORES)
            low_send[to] = lowest(to)
            m_copy(to, me_p).start()

    low_recv[me_p] = lowest(me_p)

    sent(low_recv.at[0 : planes - 1], m_r)

    best = jnp.min(low_recv[...], axis=0)
    for h in range(halves):
        first = h * (8 // halves)
        dist[h : h + 1, :] = (best[first : first + 1] + query_norm[:, h * 128 : (h + 1) * 128]) / 128

    for result in results:
        result.wait()

    sent(pack.at[0 : nz - 1], z_s)
    sent(relay, relay_s)
    sent(qbuf.at[0, 0 : ny - 1, 0], q1_s)
    sent(qbuf.at[0:2, :, 0], q2_s)
    sent(qbuf.at[0, :, 0], q3_s)
    sent(qbuf.at[:, :, 0], f_s)
    sent(gsrc.at[:, 0 : nyc - 1], g_s)
    sent(rs_send.at[0 : nx - 1], x_s)
    sent(book.at[0 : (nx - 1) * sub], b_s)
    sent(cnts.at[0 : nx - 1], c_s)
    sent(code.at[0 : 2 * rounds], right_s)
    sent(code.at[0 : 2 * rounds - 1], left_s)
    sent(low_send.at[0 : planes - 1], m_s)


def per_device(nx, ny, nz, latents, code_ids, ema_sums, ema_counts, dead_codes, restart_index, next_latents):
    k_dev = ema_sums.shape[0]
    sub = k_dev // nx
    nyc = ny * CORES
    planes = nx * nyc
    queries = next_latents.shape[0]
    hbm = pl.BlockSpec(memory_space=pl.ANY)
    vmem = pl.BlockSpec(memory_space=pltpu.VMEM)
    dma = pltpu.SemaphoreType.DMA
    bf16, f32 = jnp.bfloat16, jnp.float32
    book, counts, dist = pl.pallas_call(
        functools.partial(body, nx, ny, nz),
        out_shape=(
            jax.ShapeDtypeStruct((k_dev, 128), f32),
            jax.ShapeDtypeStruct((nx, sub), f32),
            jax.ShapeDtypeStruct((queries // 128, 128), f32),
        ),
        in_specs=[hbm] * 7,
        out_specs=(hbm, hbm, vmem),
        scratch_shapes=[
            pltpu.VMEM((k_dev, 128), f32),
            pltpu.VMEM((nx, sub), f32),
            pltpu.VMEM(latents.shape, bf16),
            pltpu.VMEM((1, code_ids.shape[0]), jnp.int32),
            pltpu.VMEM((1, dead_codes.shape[0]), jnp.int32),
            pltpu.VMEM((1, dead_codes.shape[0]), jnp.int32),
            pltpu.VMEM((sub, 128), f32),
            pltpu.VMEM((nx, sub), f32),
            pltpu.VMEM((queries, 128), bf16),
            pltpu.VMEM((128, queries), bf16),
            pltpu.VMEM((nz, nyc * USED, 128), bf16),
            pltpu.VMEM((nz, nyc * USED, 128), bf16),
            pltpu.VMEM((nyc * USED, 128), bf16),
            pltpu.VMEM((nz, nyc, TILE, 128), bf16),
            pltpu.VMEM((nyc, nz, TILE, 128), bf16),
            pltpu.VMEM((nx, ny, CORES, 128, queries), bf16),
            pltpu.VMEM((8, 128), jnp.int32),
            pltpu.VMEM((nx, 2 * sub, 256), f32),
            pltpu.VMEM((nx, sub + 8, 128), f32),
            pltpu.VMEM((nx, sub + 8, 128), f32),
            pltpu.VMEM((nz, sub, 128), bf16),
            pltpu.VMEM((4 * sub, 128), f32),
            pltpu.VMEM((planes, 8, queries), f32),
            pltpu.VMEM((planes, 8, 128), f32),
            pltpu.VMEM((planes, 8, 128), f32),
            pltpu.VMEM((nx, 8, 128), f32),
            dma((7,)),
            dma, dma((4,)), dma, dma,
            dma, dma((4,)),
            dma, dma, dma, dma, dma, dma, dma, dma,
            dma, dma, dma, dma, dma, dma,
            dma, dma((nz // 4, 2)), dma, dma((nz // 4, 2)),
            dma, dma,
        ],
        compiler_params=pltpu.CompilerParams(
            collective_id=0, has_side_effects=True, vmem_limit_bytes=56 * 1024 * 1024
        ),
    )(
        latents, code_ids.reshape(1, -1), dead_codes.reshape(1, -1), restart_index.reshape(1, -1),
        ema_sums, ema_counts.reshape(nx, sub), next_latents,
    )
    return book, counts.reshape(-1), dist.reshape(-1)


def solution(mesh, ny=4):
    nx = mesh.shape["dp"]
    nz = mesh.shape["code"] // (CORES * ny)
    in_specs = (
        P(("dp", "code"), None),
        P(("dp", "code")),
        P("code", None),
        P("code"),
        P(("dp", "code")),
        P(("dp", "code")),
        P(("dp", "code"), None),
    )
    reorder = functools.partial(per_device, nx, ny, nz)
    return jax.shard_map(
        lambda a, b, s, n, d, r, q: reorder(a, b, s, n, d, r, q),
        mesh=mesh,
        in_specs=in_specs,
        out_specs=(P("code", None), P("code"), P(("dp", "code"))),
        check_vma=False,
    )
```

```python
import functools

import jax
import jax.numpy as jnp
from jax import lax
from jax.experimental import pallas as pl
from jax.experimental.pallas import tpu as pltpu
from jax.sharding import PartitionSpec as P

MESH = pl.DeviceIdType.MESH
DECAY = 0.8
TILE = 16
USED = 14
DEAD_SLOT = 12
CORES = 2
BIG = 3.0e38


def onehot(mask):
    return jnp.where(mask, 1.0, 0.0).astype(jnp.bfloat16)


def column(row):
    return jnp.broadcast_to(row, (128, 128)).T


def body(
    nx, ny, nz, lat_in, ids_in, dead_in, ridx_in, ema_s_in, ema_c_in, nxt_in, book_hbm, cnt_hbm, dist,
    book, cnt_out, lat, ids, dead, ridx, ema_s, ema_c, nxt, turned,
    pack, zbuf, relay, gsrc, gbuf, qbuf, ext, parts, rs_send, rs_recv, code, norm, acc, low_send, low_recv, cnts, in_s,
    z_s, z_r, relay_s, relay_r, g_s, g_r, q1_s, q1_r, q2_s, q2_r, q3_s, q3_r, f_s, f_r, x_s, x_r, b_s, b_r, c_s, c_r,
    right_s, right_r, left_s, left_r, m_s, m_r,
):
    rows = lat.shape[0]
    k_dev = book.shape[0]
    sub = k_dev // nx
    queries = nxt.shape[0]
    nyc = ny * CORES
    planes = nx * nyc
    group = nz // 4
    block = nyc * USED
    shift_k = k_dev.bit_length() - 1
    shift_z = nz.bit_length() - 1

    x = lax.axis_index("dp")
    me = lax.axis_index("code")
    c = lax.rem(me, CORES)
    z = lax.rem(lax.div(me, CORES), nz)
    y = lax.div(me, CORES * nz)
    me_yc = y * CORES + c
    me_p = x * nyc + me_yc

    def at(ax, ay, az, ac):
        return (ax, (ay * nz + az) * CORES + ac)

    def in_plane(p):
        yc = lax.rem(p, nyc)
        return at(lax.div(p, nyc), lax.div(yc, CORES), z, lax.rem(yc, CORES))

    def sent(ref, sem):
        pltpu.make_async_copy(ref, ref, sem).wait()

    def along_z(d):
        return at(x, y, lax.rem(z + d + nz, nz), c)

    mine = pl.ds(pl.multiple_of(x * sub, sub), sub)
    sources = (lat_in, ids_in, dead_in, ridx_in, nxt_in, ema_c_in, ema_s_in.at[mine])
    loads = [
        pltpu.make_async_copy(src, dst, in_s.at[i])
        for i, (src, dst) in enumerate(zip(sources, (lat, ids, dead, ridx, nxt, ema_c, ema_s)))
    ]
    for load in loads:
        load.start()

    barrier = pltpu.get_barrier_semaphore()

    @pl.loop(1, planes)
    def _(d):
        pl.semaphore_signal(barrier, inc=1, device_id=in_plane(lax.rem(me_p + d, planes)), device_id_type=MESH)

    @pl.loop(1, nz)
    def _(d):
        pl.semaphore_signal(barrier, inc=1, device_id=along_z(d), device_id_type=MESH)

    for load in loads[:4]:
        load.wait()
    lanes = rows + 128
    own = ids[...]

    def place(labels):
        owner = labels >> shift_k
        oc, oz, oy = owner & 1, (owner >> 1) & (nz - 1), owner >> (1 + shift_z)
        return oz * nyc + oy * CORES + oc

    owner = place(own)
    match = lax.broadcasted_iota(jnp.int32, (nyc * nz, rows), 0) == owner
    before = lax.broadcasted_iota(jnp.int32, (rows, rows), 0) < lax.broadcasted_iota(jnp.int32, (rows, rows), 1)
    earlier = jnp.dot(onehot(match), onehot(before), preferred_element_type=jnp.float32)
    rank = jnp.sum(jnp.where(match, earlier, 0.0), axis=0, keepdims=True).astype(jnp.int32)

    ext[...] = jnp.full(ext.shape, -1, jnp.int32)
    ext[0:1, 0 : dead.shape[1]] = dead[...]
    ext[1:2, 0 : dead.shape[1]] = ridx[...]
    gone = ext[0:1, :]
    gone_owner = jnp.where(gone >= 0, place(gone), -1024)
    pick = column(ext[1:2, :].astype(jnp.float32)).astype(jnp.int32)
    lane = lax.broadcasted_iota(jnp.int32, (128, 128), 1)
    picks = jnp.concatenate([onehot(pick == lane + 128 * i) for i in range(rows // 128)], axis=1)
    restarts = jnp.dot(picks, lat[...], preferred_element_type=jnp.float32).astype(jnp.bfloat16)

    all_owner = jnp.concatenate([owner, gone_owner], axis=1)
    slot = jnp.concatenate([rank, jnp.full((1, 128), DEAD_SLOT, jnp.int32)], axis=1)
    tag = jnp.concatenate([own & (k_dev - 1), (gone & (k_dev - 1)) + k_dev], axis=1)
    tag = jnp.left_shift(128 + (tag & 127), tag >> 7).astype(jnp.float32)
    local = all_owner & (nyc - 1)
    goal = all_owner >> (nyc.bit_length() - 1)
    key = local * (USED - 1) + slot
    tag_key = local + nyc * (USED - 1)
    spot = jnp.where((lax.broadcasted_iota(jnp.int32, (128, lanes), 0) & (TILE - 1)) == slot, 1.0, 0.0)
    spot = jnp.concatenate([spot[:, i * 128 : (i + 1) * 128].T for i in range(lanes // 128)], axis=0)
    data = jnp.concatenate([jnp.concatenate([lat[...], restarts], axis=0), spot.astype(jnp.bfloat16)], axis=1)
    line = lax.broadcasted_iota(jnp.int32, (block, lanes), 0)
    lane_tile = lax.broadcasted_iota(jnp.int32, (1, 128), 1) >> 4

    half = nz // 2
    way = 1 - 2 * c

    def offset(k):
        return jnp.where(lax.rem(k, 2) == 1, half - lax.div(k + 1, 2), nz - half + lax.div(k, 2))

    def packed(k):
        to = goal == lax.rem(z + offset(k), nz)
        put = jnp.where(line == jnp.where(to, key, -1), 1.0, jnp.where(line == jnp.where(to, tag_key, -1), tag, 0.0))
        moved = jnp.dot(put.astype(jnp.bfloat16), data, preferred_element_type=jnp.float32)
        here = lax.rem(me_yc * group + lax.rem(k, group), 8)
        tags = jnp.where(lane_tile == here, moved[:, 128:], 0.0)
        is_tag = lax.broadcasted_iota(jnp.int32, (block, 128), 0) >= nyc * (USED - 1)
        return jnp.where(is_tag, tags, moved[:, :128]).astype(jnp.bfloat16)

    def z_copy(k):
        return pltpu.make_async_remote_copy(
            src_ref=pack.at[k], dst_ref=zbuf.at[k], send_sem=z_s, recv_sem=z_r.at[lax.div(k, group)],
            device_id=along_z(offset(k)), device_id_type=MESH,
        )

    def relay_in():
        return pltpu.make_async_remote_copy(
            src_ref=pack.at[0], dst_ref=relay, send_sem=z_s, recv_sem=relay_r,
            device_id=along_z(way), device_id_type=MESH,
        )

    def relay_out():
        return pltpu.make_async_remote_copy(
            src_ref=relay, dst_ref=zbuf.at[0], send_sem=relay_s, recv_sem=z_r.at[0],
            device_id=along_z(way * (half - 1)), device_id_type=MESH,
        )

    def neighbour(axis, d):
        if axis == "x":
            return at(lax.rem(x + d + nx, nx), y, z, c)
        return at(x, lax.rem(y + d + ny, ny), z, c)

    def send(src, dst, sems, device):
        return pltpu.make_async_remote_copy(
            src_ref=src, dst_ref=dst, send_sem=sems[0], recv_sem=sems[1], device_id=device, device_id_type=MESH
        )

    one, two, three = (q1_s, q1_r), (q2_s, q2_r), (q3_s, q3_r)
    cores = ((0, "y", "x"), (1, "x", "y"))

    def queries_one():
        for core, axis, _ in cores:

            @pl.when(c == core)
            def _(core=core, axis=axis):
                for d in range(1, ny):
                    send(turned, qbuf.at[x, y, core], one, neighbour(axis, d)).start()

    def queries_two():
        sent(qbuf.at[0, 0 : ny - 1, 0], q1_r)
        for core, _, axis in cores:

            @pl.when(c == core)
            def _(core=core, axis=axis):
                line_of = qbuf.at[x, :, core] if axis == "x" else qbuf.at[:, y, core]
                send(line_of, line_of, two, neighbour(axis, 1)).start()
                send(line_of, line_of, two, neighbour(axis, -1)).start()

    def queries_three():
        sent(qbuf.at[0:2, :, 0], q2_r)
        for core, _, axis in cores:

            @pl.when(c == core)
            def _(core=core, axis=axis):
                lower, upper = pl.ds(0, ny // 2), pl.ds(ny // 2, ny // 2)
                if axis == "x":
                    before, after = lax.rem(x + nx - 1, nx), lax.rem(x + 1, nx)
                    on, back = qbuf.at[before, lower, core], qbuf.at[after, upper, core]
                else:
                    before, after = lax.rem(y + ny - 1, ny), lax.rem(y + 1, ny)
                    on, back = qbuf.at[lower, before, core], qbuf.at[upper, after, core]
                send(on, on, three, neighbour(axis, 1)).start()
                send(back, back, three, neighbour(axis, -1)).start()

    def queries_across():
        mine_too = qbuf.at[:, :, c]
        return send(mine_too, mine_too, (f_s, f_r), at(x, y, z, 1 - c))

    loads[4].wait()
    wide = nxt[...].astype(jnp.float32)
    query_norm = jnp.sum((wide * wide).T, axis=0, keepdims=True)
    turned[...] = wide.T.astype(jnp.bfloat16)
    qbuf[x, y, c] = turned[...]
    pack[0] = packed(jnp.int32(0))
    pl.semaphore_wait(barrier, planes - 1 + nz - 1)
    relay_in().start()
    queries_one()

    @pl.loop(0, half - 1)
    def _(o):
        for i in range(2):
            k = 1 + o * 2 + i
            pack[k] = packed(k)
            z_copy(k).start()

        @pl.when(o == (half - 1) // 2)
        def _():
            relay_in().wait_recv()
            relay_out().start()

    zbuf[nz - 1] = packed(jnp.int32(nz - 1))
    queries_two()

    acc[...] = jnp.full(acc.shape, BIG, jnp.float32)

    def g_copy(g, j):
        return pltpu.make_async_remote_copy(
            src_ref=gsrc.at[pl.ds(g * group, group), j],
            dst_ref=gbuf.at[me_yc, pl.ds(g * group, group)],
            send_sem=g_s, recv_sem=g_r.at[g],
            device_id=at(x, lax.div(j, CORES), z, lax.rem(j, CORES)), device_id_type=MESH,
        )

    row = lax.broadcasted_iota(jnp.int32, (nyc * TILE, block), 0)
    tile, spare = row >> 4, (row & (TILE - 1)) - DEAD_SLOT
    origin = jnp.where(spare <= 0, tile * (USED - 1) + DEAD_SLOT + spare, jnp.where(spare == 1, tile + nyc * (USED - 1), -1))
    spread = onehot(lax.broadcasted_iota(jnp.int32, (nyc * TILE, block), 1) == origin)

    total = nyc * group * TILE
    in_tile = lax.broadcasted_iota(jnp.int32, (8, 128), 1) & (TILE - 1)
    read = onehot(in_tile > DEAD_SLOT)
    name = (lax.broadcasted_iota(jnp.int32, (sub, total), 0) + 128).astype(jnp.float32)

    def arrived(g):
        sent(gbuf.at[0 : nyc - 1, pl.ds(g * group, group)], g_r.at[g])
        got = gbuf[:, pl.ds(g * group, group)].reshape(total, 128)
        tags = [
            jnp.dot(read, got[i * 128 : (i + 1) * 128], preferred_element_type=jnp.float32)[0:1]
            for i in range(total // 128)
        ]
        return jnp.concatenate(tags, axis=1), jnp.concatenate([got, jnp.ones((total, 128), jnp.bfloat16)], axis=1)

    def tally(tags, got, scale):
        here = tags * scale
        hits = jnp.concatenate([onehot(name == here), onehot(name == here * 0.5**nx)], axis=0)
        return jnp.dot(hits, got, preferred_element_type=jnp.float32)

    for g in range(4):
        here = pl.ds(g * group, min(group, nz - 1 - g * group))
        sent(zbuf.at[here], z_r.at[g])
        for k in range(g * group, (g + 1) * group):
            tiles = jnp.dot(spread, zbuf[k], preferred_element_type=jnp.float32)
            gsrc[k] = tiles.astype(jnp.bfloat16).reshape(nyc, TILE, 128)

        @pl.loop(1, nyc)
        def _(d):
            away = lax.rem(d + nyc // 2 - 2, nyc - 1) + 1
            g_copy(g, lax.rem(me_yc + away, nyc)).start()

        gbuf[me_yc, pl.ds(g * group, group)] = gsrc[pl.ds(g * group, group), me_yc]
        if g > 0:
            tags, got = arrived(g - 1)
            for i in range(nx):
                part = tally(tags, got, 0.5**i)
                parts[i] = part if g == 1 else parts[i] + part
        if g == 0:
            queries_three()
        if g == 1:
            sent(qbuf.at[0, :, 0], q3_r)
            queries_across().start()

    def x_copy(to, frm):
        return pltpu.make_async_remote_copy(
            src_ref=rs_send.at[to], dst_ref=rs_recv.at[frm], send_sem=x_s, recv_sem=x_r,
            device_id=at(to, y, z, c), device_id_type=MESH,
        )

    tags, got = arrived(3)
    for d in (nx // 2, *(i for i in range(1, nx) if i != nx // 2), nx):
        to = lax.rem(x + d, nx)
        scale = jnp.float32(1.0)
        for i in range(1, nx):
            scale = jnp.where(to == i, 0.5**i, scale)
        both = parts[to] + tally(tags, got, scale)
        sums, count = both[:, :128], both[:, 128:]
        is_dead = count[sub:] > 0.5
        ref = rs_send if d < nx else rs_recv
        ref[to, 0:sub, :] = jnp.where(is_dead, sums[sub:], sums[:sub])
        ref[to, sub : sub + 8, :] = jnp.where(is_dead, -1.0, count[:sub]).T[0:8]
        if d < nx:
            x_copy(to, x).start()

    sent(rs_recv.at[0 : nx - 1], x_r)

    count = jnp.zeros((1, 128), jnp.float32)
    dead_row = jnp.zeros((1, 128), jnp.float32)
    sums = jnp.zeros((sub, 128), jnp.float32)
    restart = jnp.zeros((sub, 128), jnp.float32)
    for i in range(nx):
        part = rs_recv[i, sub : sub + 1, :]
        count += jnp.maximum(part, 0.0)
        dead_row = jnp.maximum(dead_row, -part)
        piece = rs_recv[i, 0:sub, :]
        sums += piece
        restart += jnp.where(column(part) < 0.0, piece, 0.0)
    for load in loads[5:]:
        load.wait()
    fresh_row = DECAY * ema_c[pl.ds(x, 1), :] + (1.0 - DECAY) * count
    fresh_row = jnp.where(dead_row > 0.5, 1.0, fresh_row)
    fresh = DECAY * ema_s[...] + (1.0 - DECAY) * sums
    fresh = jnp.where(column(dead_row) > 0.5, restart, fresh)
    rows_out = fresh / column(fresh_row)
    code[0] = (-2.0 * rows_out.astype(jnp.bfloat16).astype(jnp.float32)).astype(jnp.bfloat16)

    rounds = nz // 4

    def right(r, j):
        return pltpu.make_async_remote_copy(
            src_ref=code.at[jnp.maximum(4 * r - 2, 0)], dst_ref=code.at[4 * r + j],
            send_sem=right_s, recv_sem=right_r.at[r, j - 1], device_id=along_z(j), device_id_type=MESH,
        )

    def left(r, j):
        return pltpu.make_async_remote_copy(
            src_ref=code.at[4 * r], dst_ref=code.at[4 * r + 2 + j],
            send_sem=left_s, recv_sem=left_r.at[r, j - 1], device_id=along_z(-j), device_id_type=MESH,
        )

    right(jnp.int32(0), 2).start()
    if rounds > 1:
        left(jnp.int32(0), 2).start()
    right(jnp.int32(0), 1).start()
    left(jnp.int32(0), 1).start()

    book[mine, :] = rows_out
    cnts[x] = jnp.broadcast_to(fresh_row, (8, 128))

    def b_copy(to, frm):
        span = pl.ds(pl.multiple_of(frm * sub, sub), sub)
        return pltpu.make_async_remote_copy(
            src_ref=book.at[span], dst_ref=book.at[span], send_sem=b_s, recv_sem=b_r,
            device_id=at(to, y, z, c), device_id_type=MESH,
        )

    def c_copy(to, frm):
        return pltpu.make_async_remote_copy(
            src_ref=cnts.at[frm], dst_ref=cnts.at[frm], send_sem=c_s, recv_sem=c_r,
            device_id=at(to, y, z, c), device_id_type=MESH,
        )

    for d in range(1, nx):
        to = lax.rem(x + d, nx)
        b_copy(to, x).start()
        c_copy(to, x).start()

    sent(qbuf.at[:, :, 0], f_r)

    def m_copy(to, frm):
        return pltpu.make_async_remote_copy(
            src_ref=low_send.at[to], dst_ref=low_recv.at[frm], send_sem=m_s, recv_sem=m_r,
            device_id=in_plane(to), device_id_type=MESH,
        )

    halves = queries // 128

    def lowest(p):
        small = jnp.min(acc[p], axis=0, keepdims=True)
        parts_of = [jnp.broadcast_to(small[:, h * 128 : (h + 1) * 128], (8 // halves, 128)) for h in range(halves)]
        return jnp.concatenate(parts_of, axis=0)

    chips = nx * ny
    me_chip = x * ny + y
    unroll = 4
    spread_out = chips // unroll

    def norms(first, count):
        table = code[pl.ds(first, count)].reshape(count * sub, 128).astype(jnp.float32)
        both = 0.25 * jnp.sum(table * table, axis=1, keepdims=True)
        norm[0 : count * sub] = jnp.broadcast_to(both, (count * sub, 128))

    def compare(first, count, o, unroll):
        deep = count * sub
        for i in range(unroll):
            chip = lax.rem(me_chip + 1 + o * unroll + i, chips)
            px, py = lax.div(chip, ny), lax.rem(chip, ny)
            score = jnp.dot(
                code[pl.ds(first, count)].reshape(deep, 128),
                jnp.concatenate([qbuf[px, py, j] for j in range(CORES)], axis=1),
                preferred_element_type=jnp.float32,
            )
            lows = [
                jnp.min((norm[0:deep] + score[:, h * 128 : (h + 1) * 128]).reshape(deep // 8, 8, 128), axis=0)
                for h in range(CORES * halves)
            ]
            for j in range(CORES):
                low = jnp.concatenate(lows[j * halves : (j + 1) * halves], axis=1)
                acc[chip * CORES + j] = jnp.minimum(acc[chip * CORES + j], low)

    norms(0, 1)

    @pl.loop(0, spread_out)
    def _(o):
        compare(0, 1, o, unroll)

    @pl.loop(0, rounds - 1)
    def _(t):
        sent(code.at[0], right_r.at[t, 1])
        right(t + 1, 2).start()
        sent(code.at[0], left_r.at[t, 1])

        @pl.when(t < rounds - 2)
        def _():
            left(t + 1, 2).start()

        right(t + 1, 1).start()
        left(t + 1, 1).start()
        sent(code.at[0], right_r.at[t, 0])
        sent(code.at[0], left_r.at[t, 0])
        norms(4 * t + 1, 4)

        @pl.loop(0, spread_out)
        def _(o):
            compare(4 * t + 1, 4, o, unroll)

    last = 4 * (rounds - 1) + 1
    sent(book.at[0 : (nx - 1) * sub], b_r)
    sent(cnts.at[0 : nx - 1], c_r)
    for i in range(nx):
        cnt_out[i : i + 1, :] = cnts[i, 0:1, :]
    results = [
        pltpu.make_async_copy(book, book_hbm, in_s.at[0]),
        pltpu.make_async_copy(cnt_out, cnt_hbm, in_s.at[1]),
    ]
    for result in results:
        result.start()
    sent(code.at[0], right_r.at[rounds - 1, 0])
    sent(code.at[0], left_r.at[rounds - 1, 0])
    sent(code.at[0], right_r.at[rounds - 1, 1])
    norms(last, 3)

    few = 2

    @pl.loop(0, chips // few)
    def _(o):
        compare(last, 3, o, few)

        @pl.loop(o * few * CORES, jnp.minimum((o + 1) * few * CORES, planes - 1))
        def _(i):
            chip = lax.rem(me_chip + 1 + lax.div(i, CORES), chips)
            to = chip * CORES + lax.rem(i + c + 1, CORES)
            low_send[to] = lowest(to)
            m_copy(to, me_p).start()

    low_recv[me_p] = lowest(me_p)

    sent(low_recv.at[0 : planes - 1], m_r)

    best = jnp.min(low_recv[...], axis=0)
    for h in range(halves):
        first = h * (8 // halves)
        dist[h : h + 1, :] = (best[first : first + 1] + query_norm[:, h * 128 : (h + 1) * 128]) / 128

    for result in results:
        result.wait()

    sent(pack.at[0 : nz - 1], z_s)
    sent(relay, relay_s)
    sent(qbuf.at[0, 0 : ny - 1, 0], q1_s)
    sent(qbuf.at[0:2, :, 0], q2_s)
    sent(qbuf.at[0, :, 0], q3_s)
    sent(qbuf.at[:, :, 0], f_s)
    sent(gsrc.at[:, 0 : nyc - 1], g_s)
    sent(rs_send.at[0 : nx - 1], x_s)
    sent(book.at[0 : (nx - 1) * sub], b_s)
    sent(cnts.at[0 : nx - 1], c_s)
    sent(code.at[0 : 2 * rounds], right_s)
    sent(code.at[0 : 2 * rounds - 1], left_s)
    sent(low_send.at[0 : planes - 1], m_s)


def per_device(nx, ny, nz, latents, code_ids, ema_sums, ema_counts, dead_codes, restart_index, next_latents):
    k_dev = ema_sums.shape[0]
    sub = k_dev // nx
    nyc = ny * CORES
    planes = nx * nyc
    queries = next_latents.shape[0]
    hbm = pl.BlockSpec(memory_space=pl.ANY)
    vmem = pl.BlockSpec(memory_space=pltpu.VMEM)
    dma = pltpu.SemaphoreType.DMA
    bf16, f32 = jnp.bfloat16, jnp.float32
    book, counts, dist = pl.pallas_call(
        functools.partial(body, nx, ny, nz),
        out_shape=(
            jax.ShapeDtypeStruct((k_dev, 128), f32),
            jax.ShapeDtypeStruct((nx, sub), f32),
            jax.ShapeDtypeStruct((queries // 128, 128), f32),
        ),
        in_specs=[hbm] * 7,
        out_specs=(hbm, hbm, vmem),
        scratch_shapes=[
            pltpu.VMEM((k_dev, 128), f32),
            pltpu.VMEM((nx, sub), f32),
            pltpu.VMEM(latents.shape, bf16),
            pltpu.VMEM((1, code_ids.shape[0]), jnp.int32),
            pltpu.VMEM((1, dead_codes.shape[0]), jnp.int32),
            pltpu.VMEM((1, dead_codes.shape[0]), jnp.int32),
            pltpu.VMEM((sub, 128), f32),
            pltpu.VMEM((nx, sub), f32),
            pltpu.VMEM((queries, 128), bf16),
            pltpu.VMEM((128, queries), bf16),
            pltpu.VMEM((nz, nyc * USED, 128), bf16),
            pltpu.VMEM((nz, nyc * USED, 128), bf16),
            pltpu.VMEM((nyc * USED, 128), bf16),
            pltpu.VMEM((nz, nyc, TILE, 128), bf16),
            pltpu.VMEM((nyc, nz, TILE, 128), bf16),
            pltpu.VMEM((nx, ny, CORES, 128, queries), bf16),
            pltpu.VMEM((8, 128), jnp.int32),
            pltpu.VMEM((nx, 2 * sub, 256), f32),
            pltpu.VMEM((nx, sub + 8, 128), f32),
            pltpu.VMEM((nx, sub + 8, 128), f32),
            pltpu.VMEM((nz, sub, 128), bf16),
            pltpu.VMEM((4 * sub, 128), f32),
            pltpu.VMEM((planes, 8, queries), f32),
            pltpu.VMEM((planes, 8, 128), f32),
            pltpu.VMEM((planes, 8, 128), f32),
            pltpu.VMEM((nx, 8, 128), f32),
            dma((7,)),
            dma, dma((4,)), dma, dma,
            dma, dma((4,)),
            dma, dma, dma, dma, dma, dma, dma, dma,
            dma, dma, dma, dma, dma, dma,
            dma, dma((nz // 4, 2)), dma, dma((nz // 4, 2)),
            dma, dma,
        ],
        compiler_params=pltpu.CompilerParams(
            collective_id=0, has_side_effects=True, vmem_limit_bytes=56 * 1024 * 1024
        ),
    )(
        latents, code_ids.reshape(1, -1), dead_codes.reshape(1, -1), restart_index.reshape(1, -1),
        ema_sums, ema_counts.reshape(nx, sub), next_latents,
    )
    return book, counts.reshape(-1), dist.reshape(-1)


def solution(mesh, ny=4):
    nx = mesh.shape["dp"]
    nz = mesh.shape["code"] // (CORES * ny)
    in_specs = (
        P(("dp", "code"), None),
        P(("dp", "code")),
        P("code", None),
        P("code"),
        P(("dp", "code")),
        P(("dp", "code")),
        P(("dp", "code"), None),
    )
    reorder = functools.partial(per_device, nx, ny, nz)
    return jax.shard_map(
        lambda a, b, s, n, d, r, q: reorder(a, b, s, n, d, r, q),
        mesh=mesh,
        in_specs=in_specs,
        out_specs=(P("code", None), P("code"), P(("dp", "code"))),
        check_vma=False,
    )
```
